128 devices in a mesh: sub: 32 (over y, z, core), grp: 4 (over x).
Axes of the slice: x: 4, y: 4, z: 4, core: 2. Of those that a mesh axis runs over, the one named last changes fastest.
Arguments:
- load: float32 [4096, 32, 128], P(('sub', 'grp')), may hold values from -6 to 6
- schur: bfloat16 [128, 2048, 2048], P(('sub', 'grp')), as said below
- coarse_basis: float32 [128, 2048, 32], P(('sub', 'grp')), may hold values from -0.375 to 0.375
- coarse_index: int32 [128, 32], P(('sub', 'grp')), may hold values from 0 to 1023
- coarse_inverse: float32 [1024, 1024], replicated, as said below
- send_order: int32 [8192], P(('sub', 'grp')), may hold values from 0 to 63, as said below
- recv_owner: int32 [8192], P(('sub', 'grp')), may hold values from 0 to 31, as said below
Outputs:
- solution: float32 [4096, 32, 128], P(('sub', 'grp'))
- residual: float32 [4096, 32, 128], P(('sub', 'grp'))
The draws below stay inside these ranges and needn't reach their ends.
Inputs may be any that keep to these rules, and one draw needn't show every extreme that they name: `send_order`: each subdomain's 64 entries are a permutation of 0 to 63. `recv_owner`: within each device's 64 entries every value from 0 to 31 appears exactly twice. Each subdomain's schur is symmetric positive definite. `coarse_inverse`: symmetric positive definite.
All inputs are finite; a program needn't handle non-finite values.
Results may differ from the reference program's by a relative error of at most 0.007.
The reference program's roundings to bfloat16 on the way count: a program that leaves them out, or rounds other values in their place, can miss the bound.
Values may be sent and summed in bfloat16 or wider, within the bound.
No kernel may reach another device: no remote copies, remote signals or barrier semaphores. Data moves between devices by JAX's collectives and lax.ppermute only.
A program may use at most 64 MiB of HBM per device.

```python
import math
import jax
import jax.numpy as jnp
from jax import lax

NI = 2048
R = 128
NCC = 32
SLOTS = 2
ITERS = 2
SUBDOMAINS = 128
LB = 64
BW = 32
OB = 32
NC = 1024
N_SUB = 32
N_GRP = 4
DEVICES = 128


def symmetric_dominant(key, count, order, spread_scale, low, high):
    first, second = jax.random.split(key)
    raw = jax.random.uniform(first, (count, order, order), jnp.float32, -1.7320508, 1.7320508)
    offdiag = (raw + jnp.swapaxes(raw, 1, 2)) * (spread_scale / math.sqrt(2.0 * order))
    diagonal = jax.random.uniform(second, (count, order), jnp.float32, low, high)
    return offdiag + diagonal[:, :, None] * jnp.eye(order, dtype=jnp.float32)[None, :, :]


def draw_schur(key, part):
    folded = jax.random.fold_in(key, 11)
    return symmetric_dominant(folded, SUBDOMAINS, NI, 0.6, 2.0, 4.5).astype(jnp.bfloat16)


def draw_coarse_inverse(key, part):
    folded = jax.random.fold_in(key, 23)
    return symmetric_dominant(folded, 1, NC, 0.3, 0.8, 1.6)[0]


def draw_send_order(key, part):
    keys = jax.random.split(jax.random.fold_in(key, 31), SUBDOMAINS)
    orders = jax.vmap(lambda single: jax.random.permutation(single, LB))(keys)
    return orders.reshape(-1).astype(jnp.int32)


def draw_recv_owner(key, part):
    keys = jax.random.split(jax.random.fold_in(key, 37), SUBDOMAINS)
    doubled = jnp.concatenate([jnp.arange(OB, dtype=jnp.int32), jnp.arange(OB, dtype=jnp.int32)])
    owners = jax.vmap(lambda single: jax.random.permutation(single, doubled))(keys)
    return owners.reshape(-1).astype(jnp.int32)


def touch_ends(values, own_key, smallest, largest):
    extent = values.shape
    spot = [jax.random.randint(jax.random.fold_in(own_key, axis), (), 0, extent[axis]) for axis in range(len(extent))]
    values = values.at[tuple(spot)].set(smallest)
    longest = extent.index(max(extent))
    spot[longest] = (spot[longest] + 1) % extent[longest]
    return values.at[tuple(spot)].set(largest)


def levels(own_key, extent, cuts, low, top_value):
    def one(axis_at, parts):
        heights = jax.random.uniform(jax.random.fold_in(jax.random.fold_in(own_key, 6), axis_at), (parts,), jnp.float32, low / len(cuts), top_value / len(cuts))
        return jnp.repeat(jnp.exp(heights), extent[axis_at] // parts).reshape((-1,) + (1,) * (len(extent) - axis_at - 1))

    level = one(*cuts[0])
    for cut in cuts[1:]:
        level = level * one(*cut)
    return level


def scatter_about(rng, shape, deviation, reach, pieces=(), held_as=jnp.bfloat16):
    entries = deviation * jax.random.normal(rng, shape, jnp.float32)
    if pieces:
        entries = entries * levels(rng, shape, pieces, -0.22, 0.18)
    return jnp.clip(entries, -reach, reach).astype(held_as)


def setup_inputs(seed: int = 0) -> dict:
    streams_of = jax.random.split(jax.random.key(seed), 8)
    return {
        "load": scatter_about(streams_of[0], (SUBDOMAINS * OB, BW, R), 1.0, 6.0, ((0, 128),), jnp.float32),
        "schur": draw_schur(jax.random.fold_in(streams_of[7], 71), 0),
        "coarse_basis": scatter_about(streams_of[2], (SUBDOMAINS, NI, NCC), (0.4 / (NI * NCC) ** 0.25), 0.375, ((0, 128),), jnp.float32),
        "coarse_index": touch_ends(jax.random.randint(streams_of[3], (SUBDOMAINS, NCC), 0, NC), jax.random.fold_in(streams_of[3], 1), 0, NC - 1).astype(jnp.int32),
        "coarse_inverse": draw_coarse_inverse(jax.random.fold_in(streams_of[7], 71), 0),
        "send_order": draw_send_order(jax.random.fold_in(streams_of[7], 71), 0),
        "recv_owner": draw_recv_owner(jax.random.fold_in(streams_of[7], 71), 0),
    }


relaxation = 0.2


def swap_pieces(blocks_all):
    shaped = blocks_all.reshape(N_SUB, N_GRP, N_SUB, SLOTS, BW, R)
    shaped = jnp.transpose(shaped, (2, 1, 0, 3, 4, 5))
    return shaped.reshape(DEVICES, LB, BW, R)


def reference(load, schur, coarse_basis, coarse_index, coarse_inverse, send_order, recv_owner):
    order_table = send_order.reshape(DEVICES, LB)
    owner_list = recv_owner.reshape(DEVICES, LB)
    inverse_order = jax.vmap(lambda order: jnp.zeros((LB,), jnp.int32).at[order].set(jnp.arange(LB, dtype=jnp.int32)))(order_table)
    owner_table = (owner_list[:, None, :] == jnp.arange(OB, dtype=jnp.int32)[None, :, None]).astype(jnp.float32)
    highest = lax.Precision.HIGHEST

    def spread(owned):
        flat = owned.reshape(DEVICES, OB, BW * R)
        expanded = jnp.einsum('dol,dok->dlk', owner_table, flat, precision=highest).reshape(DEVICES, LB, BW, R)
        returned = swap_pieces(expanded)
        local = jax.vmap(lambda blocks, index: jnp.take(blocks, index, axis=0))(returned, inverse_order)
        return local.reshape(DEVICES, NI, R)

    def collect(local):
        blocks = local.reshape(DEVICES, LB, BW, R)
        outgoing = jax.vmap(lambda rows, index: jnp.take(rows, index, axis=0))(blocks, order_table)
        arrived = swap_pieces(outgoing).reshape(DEVICES, LB, BW * R)
        owned = jnp.einsum('dol,dlk->dok', owner_table, arrived, precision=highest)
        return owned.reshape(DEVICES * OB, BW, R)

    def schur_apply(local):
        operand = local.astype(jnp.bfloat16)
        return lax.map(lambda operands: jnp.dot(operands[0], operands[1], preferred_element_type=jnp.float32), (schur, operand))

    def precondition(target):
        scaled = 0.5 * spread(target)
        neumann = scaled
        for sweep_index in range(2):
            neumann = scaled + neumann - relaxation * schur_apply(neumann)
        coarse_part = jnp.einsum('dnc,dnr->dcr', coarse_basis, scaled, precision=highest)
        coarse_sum = jnp.zeros((NC, R), jnp.float32).at[coarse_index.reshape(-1)].add(coarse_part.reshape(-1, R))
        coarse_sol = jnp.dot(coarse_inverse, coarse_sum, precision=highest)
        picked = coarse_sol[coarse_index]
        combined = neumann + jnp.einsum('dnc,dcr->dnr', coarse_basis, picked, precision=highest)
        return collect(0.5 * combined)

    solution = jnp.zeros_like(load)
    residual = load
    precond = precondition(residual)
    direction = precond
    rz_now = jnp.sum(residual * precond, axis=(0, 1))
    for iteration in range(ITERS):
        image = collect(schur_apply(spread(direction)))
        alpha = rz_now / jnp.sum(direction * image, axis=(0, 1))
        solution = solution + alpha * direction
        residual = residual - alpha * image
        if iteration + 1 < ITERS:
            precond = precondition(residual)
            rz_next = jnp.sum(residual * precond, axis=(0, 1))
            direction = precond + (rz_next / rz_now) * direction
            rz_now = rz_next
    return (solution, residual)
```

```python
import functools

import jax
import jax.numpy as jnp
from jax import lax
from jax.experimental import pallas as pl
from jax.experimental.pallas import tpu as pltpu
from jax.sharding import PartitionSpec as P

F32, BF16, I32 = jnp.float32, jnp.bfloat16, jnp.int32
HIGHEST = lax.Precision.HIGHEST
RELAX = 0.2
BW = 32
LANES = 128
CHUNK = 256
MIB = 1 << 20

VMEM = pl.BlockSpec(memory_space=pltpu.VMEM)
SMEM = pl.BlockSpec(memory_space=pltpu.SMEM)
ANY = pl.BlockSpec(memory_space=pl.ANY)

SPREAD_DTYPE = BF16
COLLECT_DTYPE = BF16


def call(body, name, specs, outs, args, scratch=(), flops=0, moved=2 * MIB, vmem=24):
    return pl.pallas_call(
        body,
        name=name,
        out_shape=outs,
        in_specs=specs,
        out_specs=jax.tree.map(lambda _: VMEM, outs),
        scratch_shapes=list(scratch),
        compiler_params=pltpu.CompilerParams(vmem_limit_bytes=vmem * MIB),
        cost_estimate=pl.CostEstimate(flops=flops, bytes_accessed=moved, transcendentals=0),
    )(*args)


def shape(dims, dtype=F32):
    return jax.ShapeDtypeStruct(dims, dtype)


def rows_of(index):
    return pl.ds(pl.multiple_of(index * BW, BW), BW)


def piece(ref, k):
    return ref.at[k // 2, (k % 2) * BW : (k % 2 + 1) * BW, :]


def split3(value):
    high = value.astype(BF16)
    rest = value - high.astype(F32)
    middle = rest.astype(BF16)
    low = (rest - middle.astype(F32)).astype(BF16)
    return high, middle, low


def tile_of(values, dtype):
    height = 8 if dtype == F32 else 16
    if dtype != F32:
        values = [part.astype(F32) for value in values for part in split3(value)]
    row = lax.broadcasted_iota(I32, (height, LANES), 0)
    tile = jnp.zeros((height, LANES), F32)
    for i, value in enumerate(values):
        tile = jnp.where(row == i, value, tile)
    return tile.astype(dtype)


def tile_height(dtype):
    return 8 if dtype == F32 else 16


def sum_tiles(ref):
    total = jnp.sum(ref[:, 2 * BW :, :].astype(F32), axis=0)
    if ref.dtype == F32:
        return total
    row = lax.broadcasted_iota(I32, (8, LANES), 0)
    value = total[0:1] + total[1:2] + total[2:3]
    return jnp.where(row == 0, value, 0.0)


def pack_owner_body(owner, owned, out):
    for k in range(owner.shape[0]):
        piece(out, k)[...] = owned[owner[k]].astype(out.dtype)


def coarse_contribution(basis_t, scaled):
    return jnp.dot(basis_t, scaled, precision=HIGHEST, preferred_element_type=F32)


def unpack_first_body(order, received, basis_t, basis_rows, index_tile, local, out):
    for j in range(order.shape[0]):
        local[rows_of(order[j]), :] = piece(received, j)[...]
    part = coarse_contribution(basis_t[...], 0.5 * local[...])
    tile = index_tile[...]
    for d in range(out.shape[0]):
        out[d, 0:32, :] = part
        out[d, 32:40, :] = basis_rows[order[2 * d]]
        out[d, 40:48, :] = basis_rows[order[2 * d + 1]]
        out[d, 48:56, :] = tile


def unpack_second_body(
    order, received, first, image, sums0, sums1, sums2, sums3, coarse_rz, basis_t, local, out, scalars
):
    total = sums0[...] + sums1[...] + sums2[...] + sums3[...]
    rz = total[1:2] + coarse_rz[0:1, :]
    alpha = rz / total[0:1]
    row = lax.broadcasted_iota(I32, (8, LANES), 0)
    scalars[...] = jnp.where(row == 0, alpha, jnp.where(row == 1, rz, 0.0))
    for j in range(order.shape[0]):
        rows = rows_of(order[j])
        local[rows, :] = first[rows, :] - alpha * (image[rows, :] + piece(received, j)[...].astype(F32))
    part = coarse_contribution(basis_t[...], 0.5 * local[...])
    for d in range(out.shape[0]):
        out[d] = part


def start_matrix(matrix, held, sems):
    copies = []
    for i in range(held.shape[0] // CHUNK):
        rows = pl.ds(i * CHUNK, CHUNK)
        copies.append(pltpu.make_async_copy(matrix.at[0, rows, :], held.at[rows, :], sems.at[i]))
        copies[-1].start()
    return copies


def neumann_body(order, local, matrix, out, sums, held, operand, work, sems):
    copies = start_matrix(matrix, held, sems)
    operand[...] = (0.5 * local[...]).astype(BF16)
    for i, copy in enumerate(copies):
        rows = pl.ds(i * CHUNK, CHUNK)
        copy.wait()
        product = jnp.dot(held[rows, :], operand[...], preferred_element_type=F32)
        scaled = 0.5 * local[rows, :]
        work[rows, :] = scaled + scaled - RELAX * product
    operand[...] = work[...].astype(BF16)
    rz = jnp.zeros((1, LANES), F32)
    for i in range(len(copies)):
        rows = pl.ds(i * CHUNK, CHUNK)
        product = jnp.dot(held[rows, :], operand[...], preferred_element_type=F32)
        value = 0.5 * (0.5 * local[rows, :] + work[rows, :] - RELAX * product)
        work[rows, :] = value
        rz = rz + jnp.sum(local[rows, :] * value, axis=0, keepdims=True)
    sums[...] = tile_of([rz], F32)
    for j in range(order.shape[0]):
        piece(out, j)[...] = work[rows_of(order[j]), :].astype(out.dtype)
    if out.shape[1] > 2 * BW:
        tile = tile_of([rz], out.dtype)
        for d in range(out.shape[0]):
            out[d, 2 * BW :, :] = tile


def apply_body(order, received, matrix, earlier, out, image, held, operand, sems):
    copies = start_matrix(matrix, held, sems)
    for j in range(order.shape[0]):
        operand[rows_of(order[j]), :] = piece(received, j)[...]
    dot = jnp.zeros((1, LANES), F32)
    for i, copy in enumerate(copies):
        rows = pl.ds(i * CHUNK, CHUNK)
        copy.wait()
        product = jnp.dot(held[rows, :], operand[...], preferred_element_type=F32)
        image[rows, :] = product
        dot = dot + jnp.sum(product * operand[rows, :].astype(F32), axis=0, keepdims=True)
    values = [dot, earlier[0:1, :]] if out.dtype == F32 else [dot]
    tile = tile_of(values, out.dtype)
    for j in range(order.shape[0]):
        piece(out, j)[...] = image[rows_of(order[j]), :].astype(out.dtype)
    for d in range(out.shape[0]):
        out[d, 2 * BW :, :] = tile


def coarse_sum_body(place, index_row, received, out0, out1, out2, out3):
    parts = received[:, 0:32, :].astype(F32).reshape(-1, LANES)
    split = jnp.concatenate(split3(parts), axis=1)
    group = place[0]
    for t, out in enumerate((out0, out1, out2, out3)):
        base = lax.rem(group + t, 4) * out.shape[0]
        row = lax.broadcasted_iota(I32, (out.shape[0], parts.shape[0]), 0) + base
        table = jnp.where(row == index_row[...], 1.0, 0.0).astype(BF16)
        sums = jnp.dot(table, split, preferred_element_type=F32)
        out[...] = sums[:, 0:LANES] + sums[:, LANES : 2 * LANES] + sums[:, 2 * LANES :]


def coarse_solve_body(
    place, owner, index_column, mine, from1, from2, from3, inverse, basis, out, coarse_rz, held, picked
):
    quarter = mine.shape[0]
    group = place[0]
    for t, part in enumerate((mine, from1, from2, from3)):
        base = pl.multiple_of(lax.rem(group + 4 - t, 4) * quarter, quarter)
        held[pl.ds(base, quarter), :] = part[...]
    solved = jnp.dot(inverse[...], held[...], precision=HIGHEST, preferred_element_type=F32)
    rz = jnp.sum(held[...] * solved, axis=0, keepdims=True)
    coarse_rz[...] = jnp.broadcast_to(rz, (8, LANES))
    split = jnp.concatenate(split3(solved), axis=1)
    count = held.shape[0]
    for i in range(count // CHUNK):
        rows = pl.ds(i * CHUNK, CHUNK)
        column = lax.broadcasted_iota(I32, (CHUNK, count), 1)
        table = jnp.where(column == index_column[rows, :], 1.0, 0.0).astype(BF16)
        sums = jnp.dot(table, split, preferred_element_type=F32)
        picked[rows, :] = 0.5 * (sums[:, 0:LANES] + sums[:, LANES : 2 * LANES] + sums[:, 2 * LANES :])
    out[...] = jnp.zeros(out.shape, F32)
    for s in range(basis.shape[0]):
        term = jnp.dot(
            basis[s], picked[s * 32 : (s + 1) * 32, :], precision=HIGHEST, preferred_element_type=F32
        )
        out[owner[2 * s]] += term[0:BW]
        out[owner[2 * s + 1]] += term[BW:]


def direction_body(owner, coarse_term, received, direction, out):
    direction[...] = coarse_term[...]
    for k in range(owner.shape[0]):
        direction[owner[k]] += piece(received, k)[...].astype(F32)
    for k in range(owner.shape[0]):
        piece(out, k)[...] = direction[owner[k]].astype(out.dtype)


def image_body(owner, partner, received, image, sums, out):
    image[...] = jnp.zeros(image.shape, F32)
    for k in range(owner.shape[0]):
        image[owner[k]] += piece(received, k)[...]
    for k in range(owner.shape[0]):
        source = partner[k]
        start = pl.multiple_of(lax.rem(source, 2) * BW, BW)
        piece(out, k)[...] = received[lax.div(source, 2), pl.ds(start, BW), :].astype(out.dtype)
    sums[...] = sum_tiles(received)


def collect_body(owner, start, received, value, sums):
    value[...] = start[...]
    for k in range(owner.shape[0]):
        value[owner[k]] += piece(received, k)[...].astype(F32)
    sums[...] = sum_tiles(received)


def next_direction_body(
    owner, precond, before, sums0, sums1, sums2, sums3, coarse_rz, scalars, direction, out, later
):
    total = sums0[...] + sums1[...] + sums2[...] + sums3[...]
    rz = total[0:1] + coarse_rz[0:1, :]
    ratio = rz / scalars[1:2, :]
    later[...] = jnp.broadcast_to(rz, (8, LANES))
    direction[...] = precond[...] + ratio[None] * before[...]
    for k in range(owner.shape[0]):
        piece(out, k)[...] = direction[owner[k]].astype(out.dtype)


def finish_body(
    owner, load, first, second, image, received, sums0, sums1, sums2, sums3, scalars, later, solution, residual
):
    total = sums0[...] + sums1[...] + sums2[...] + sums3[...]
    alpha0 = scalars[0:1, :][None]
    alpha1 = (later[0:1, :] / total[0:1])[None]
    solution[...] = alpha0 * first[...] + alpha1 * second[...]
    residual[...] = load[...] - alpha0 * image[...]
    for k in range(owner.shape[0]):
        residual[owner[k]] -= alpha1[0] * piece(received, k)[...].astype(F32)


def final_sums_body(received, sums):
    sums[...] = sum_tiles(received)


def shards(n_sub, n_grp, load, schur, coarse_basis, coarse_index, coarse_inverse, send_order, recv_owner):
    owned = shape(load.shape)
    blocks = send_order.shape[0]
    dofs = schur.shape[1]
    coarse = coarse_inverse.shape[0]
    quarter = coarse // n_grp
    local_shape = shape((dofs, LANES))
    tile = shape((8, LANES))
    place = lax.axis_index("grp").astype(I32).reshape(1)
    matrix_scratch = [pltpu.VMEM((dofs, dofs), BF16), pltpu.VMEM((dofs, LANES), BF16)]
    semaphores = pltpu.SemaphoreType.DMA((dofs // CHUNK,))
    product_flops = 2 * dofs * dofs * LANES

    def hop(payload):
        return lax.all_to_all(payload, "sub", split_axis=0, concat_axis=0, tiled=True)

    def shifted(value, step):
        return lax.ppermute(value, "grp", [(i, (i + step) % n_grp) for i in range(n_grp)])

    def over_groups(value):
        return [value] + [shifted(value, step) for step in range(1, n_grp)]

    def payload(height, dtype=F32):
        return shape((n_sub, height, LANES), dtype)

    def neumann(local, dtype, tiled):
        height = 2 * BW + (tile_height(dtype) if tiled else 0)
        return call(
            neumann_body,
            "neumann",
            [SMEM, VMEM, ANY],
            [payload(height, dtype), tile],
            [send_order, local, schur],
            matrix_scratch + [pltpu.VMEM((dofs, LANES), F32), semaphores],
            flops=2 * product_flops,
            moved=12 * MIB,
        )

    def apply(received, earlier, dtype):
        return call(
            apply_body,
            "apply",
            [SMEM, VMEM, ANY, VMEM],
            [payload(2 * BW + tile_height(dtype), dtype), local_shape],
            [send_order, received, schur, earlier],
            matrix_scratch + [semaphores],
            flops=product_flops,
            moved=12 * MIB,
        )

    def coarse_term(received, index_row, index_column, basis):
        parts = call(
            coarse_sum_body,
            "coarse_sum",
            [SMEM, VMEM, VMEM],
            [shape((quarter, LANES))] * 4,
            [place, index_row, received],
            flops=2 * coarse * coarse * LANES * 3,
        )
        mine = parts[0]
        for step in range(1, n_grp):
            mine = mine + shifted(parts[step], step)
        return call(
            coarse_solve_body,
            "coarse_solve",
            [SMEM, SMEM] + [VMEM] * 7,
            [owned, tile],
            [place, recv_owner, index_column, *over_groups(mine), coarse_inverse, basis],
            [pltpu.VMEM((coarse, LANES), F32), pltpu.VMEM((coarse, LANES), F32)],
            flops=2 * coarse * coarse * LANES * 12,
            moved=8 * MIB,
            vmem=32,
        )

    basis_t = jnp.swapaxes(coarse_basis[0], 0, 1)
    basis_rows = (
        coarse_basis[0].reshape(blocks, 4, 8, 32).transpose(0, 2, 1, 3).reshape(blocks, 8, LANES)
    )
    lane = lax.broadcasted_iota(I32, (8, LANES), 1)
    index_tile = jnp.where(
        lane // 32 == lax.rem(lax.axis_index("sub"), 4), jnp.tile(coarse_index.astype(F32), (8, 4)), 0.0
    )
    position = jnp.arange(blocks, dtype=I32)
    partner = jnp.sum(
        jnp.where(
            (recv_owner[:, None] == recv_owner[None, :]) & (position[:, None] != position[None, :]),
            position[None, :],
            0,
        ),
        axis=1,
    ).astype(I32)

    sent = call(pack_owner_body, "pack_load", [SMEM, VMEM], payload(2 * BW), [recv_owner, load])
    local0, parts0 = call(
        unpack_first_body,
        "unpack_first",
        [SMEM, VMEM, VMEM, VMEM, VMEM],
        [local_shape, payload(56)],
        [send_order, hop(sent), basis_t, basis_rows, index_tile],
    )
    shared0 = hop(parts0)
    sent, rz_part = neumann(local0, F32, False)
    gathered = hop(sent)
    basis = (
        shared0[:, 32:48, :].reshape(n_sub, 2, 8, 4, 32).transpose(0, 1, 3, 2, 4).reshape(n_sub, 2 * BW, 32)
    )
    index_all = shared0[:, 48, :].reshape(n_sub // 4, 4, LANES).sum(1).reshape(-1).astype(I32)
    index_row, index_column = index_all.reshape(1, -1), index_all.reshape(-1, 1)
    term0, coarse_rz0 = coarse_term(shared0, index_row, index_column, basis)
    direction0, sent = call(
        direction_body,
        "direction",
        [SMEM, VMEM, VMEM],
        [owned, payload(2 * BW, BF16)],
        [recv_owner, term0, gathered],
    )

    sent, image_local = apply(hop(sent), rz_part, F32)
    image0, sums, sent = call(
        image_body,
        "image",
        [SMEM, SMEM, VMEM],
        [owned, tile, payload(2 * BW, SPREAD_DTYPE)],
        [recv_owner, partner, hop(sent)],
    )
    sums = over_groups(sums)
    local1, parts1, scalars = call(
        unpack_second_body,
        "unpack_second",
        [SMEM] + [VMEM] * 9,
        [local_shape, payload(32), tile],
        [send_order, hop(sent), local0, image_local, *sums, coarse_rz0, basis_t],
    )

    shared1 = hop(parts1)
    sent, _ = neumann(local1, COLLECT_DTYPE, True)
    gathered = hop(sent)
    term1, coarse_rz1 = coarse_term(shared1, index_row, index_column, basis)
    precond1, sums = call(
        collect_body,
        "collect",
        [SMEM, VMEM, VMEM],
        [owned, tile],
        [recv_owner, term1, gathered],
    )
    direction1, sent, later = call(
        next_direction_body,
        "next_direction",
        [SMEM] + [VMEM] * 8,
        [owned, payload(2 * BW, BF16), tile],
        [recv_owner, precond1, direction0, *over_groups(sums), coarse_rz1, scalars],
    )

    sent, _ = apply(hop(sent), rz_part, COLLECT_DTYPE)
    gathered = hop(sent)
    sums = call(final_sums_body, "final_sums", [VMEM], tile, [gathered])
    return tuple(
        call(
            finish_body,
            "finish",
            [SMEM] + [VMEM] * 11,
            [owned, owned],
            [recv_owner, load, direction0, direction1, image0, gathered, *over_groups(sums), scalars, later],
        )
    )


def solution(mesh):
    both = ("sub", "grp")
    in_specs = (
        P(both, None, None),
        P(both, None, None),
        P(both, None, None),
        P(both, None),
        P(),
        P(both),
        P(both),
    )
    out_specs = (P(both, None, None), P(both, None, None))
    body = functools.partial(shards, mesh.shape["sub"], mesh.shape["grp"])
    return jax.shard_map(body, mesh=mesh, in_specs=in_specs, out_specs=out_specs, check_vma=False)
```

```python
import functools

import jax
import jax.numpy as jnp
from jax import lax
from jax.experimental import pallas as pl
from jax.experimental.pallas import tpu as pltpu
from jax.sharding import PartitionSpec as P

F32, BF16, I32 = jnp.float32, jnp.bfloat16, jnp.int32
HIGHEST = lax.Precision.HIGHEST
RELAX = 0.2
BW = 32
LANES = 128
CHUNK = 256
MIB = 1 << 20

SPREAD_DTYPE = BF16
COLLECT_DTYPE = BF16

SPECS = {
    "v": pl.BlockSpec(memory_space=pltpu.VMEM),
    "s": pl.BlockSpec(memory_space=pltpu.SMEM),
    "h": pl.BlockSpec(memory_space=pltpu.HBM),
}


def call(body, name, ins, outs, scratch=(), flops=0, moved=2 * MIB, vmem=24, copies=24):
    arrays = [pltpu.with_memory_space_constraint(a, pltpu.HBM) if kind == "h" else a for kind, a in ins]
    shapes = [pltpu.HBM(like.shape, like.dtype) if kind == "h" else like for kind, like in outs]
    return pl.pallas_call(
        body,
        name=name,
        out_shape=shapes,
        in_specs=[SPECS[kind] for kind, _ in ins],
        out_specs=[SPECS[kind] for kind, _ in outs],
        scratch_shapes=[pltpu.VMEM(like.shape, like.dtype) for like in scratch]
        + [pltpu.SemaphoreType.DMA((copies,))],
        compiler_params=pltpu.CompilerParams(vmem_limit_bytes=vmem * MIB),
        cost_estimate=pl.CostEstimate(flops=flops, bytes_accessed=moved, transcendentals=0),
    )(*arrays)


def shape(dims, dtype=F32):
    return jax.ShapeDtypeStruct(dims, dtype)


def begin(source, target, sem):
    copy = pltpu.make_async_copy(source, target, sem)
    copy.start()
    return copy


def finish_all(copies):
    for copy in copies:
        copy.wait()


def rows_of(index):
    return pl.ds(pl.multiple_of(index * BW, BW), BW)


def piece(ref, k):
    return ref.at[k // 2, (k % 2) * BW : (k % 2 + 1) * BW, :]


def split2(value):
    high = value.astype(BF16)
    return high, (value - high.astype(F32)).astype(BF16)


def split3(value):
    high = value.astype(BF16)
    rest = value - high.astype(F32)
    middle = rest.astype(BF16)
    low = (rest - middle.astype(F32)).astype(BF16)
    return high, middle, low


def tile_of(values, dtype):
    height = tile_height(dtype)
    if dtype != F32:
        values = [part.astype(F32) for value in values for part in split3(value)]
    row = lax.broadcasted_iota(I32, (height, LANES), 0)
    tile = jnp.zeros((height, LANES), F32)
    for i, value in enumerate(values):
        tile = jnp.where(row == i, value, tile)
    return tile.astype(dtype)


def tile_height(dtype):
    return 8 if dtype == F32 else 16


def sum_tiles(ref):
    total = jnp.sum(ref[:, 2 * BW :, :].astype(F32), axis=0)
    if ref.dtype == F32:
        return total
    row = lax.broadcasted_iota(I32, (8, LANES), 0)
    value = total[0:1] + total[1:2] + total[2:3]
    return jnp.where(row == 0, value, 0.0)


def fill_and_send(fill, held, out, sems, first=0):
    copies = []
    step = out.shape[0] // 4
    for part in range(4):
        for d in range(part * step, (part + 1) * step):
            fill(d)
        chosen = pl.ds(part * step, step)
        copies.append(begin(held.at[chosen], out.at[chosen], sems.at[first + part]))
    return copies


def pack(order, local, tile, held, out, sems, first=0):
    def fill(d):
        for k in (2 * d, 2 * d + 1):
            piece(held, k)[...] = local[rows_of(order[k]), :].astype(out.dtype)
        if tile is not None:
            held[d, 2 * BW :, :] = tile

    return fill_and_send(fill, held, out, sems, first)


def pack_load_body(owner, owned, out, sems):
    finish_all(
        [begin(owned.at[owner[k]], piece(out, k), sems.at[k]) for k in range(owner.shape[0])]
    )


def coarse_contribution(basis_t, scaled):
    return jnp.dot(basis_t, scaled, precision=HIGHEST, preferred_element_type=F32)


def unpack_first_body(order, received, basis_t, basis_rows, index_tile, local_out, out, local, held, sems):
    for j in range(order.shape[0]):
        local[rows_of(order[j]), :] = piece(received, j)[...]
    copies = [begin(local, local_out, sems.at[0])]
    part = coarse_contribution(basis_t[...], 0.5 * local[...])
    tile = index_tile[...]

    def fill(d):
        held[d, 0:32, :] = part
        held[d, 32:40, :] = basis_rows[order[2 * d]]
        held[d, 40:48, :] = basis_rows[order[2 * d + 1]]
        held[d, 48:56, :] = tile

    finish_all(copies + fill_and_send(fill, held, out, sems, 1))


def unpack_second_body(
    order,
    received,
    first_in,
    image_in,
    sums0,
    sums1,
    sums2,
    sums3,
    rz_in,
    basis_t,
    local_out,
    out,
    scalars_out,
    first,
    image,
    local,
    held,
    rz_tile,
    scalars,
    sems,
):
    loads = [
        begin(rz_in, rz_tile, sems.at[0]),
        begin(first_in, first, sems.at[1]),
        begin(image_in, image, sems.at[2]),
    ]
    finish_all(loads)
    total = sums0[...] + sums1[...] + sums2[...] + sums3[...]
    rz = total[1:2] + rz_tile[0:1, :]
    alpha = rz / total[0:1]
    row = lax.broadcasted_iota(I32, (8, LANES), 0)
    scalars[...] = jnp.where(row == 0, alpha, jnp.where(row == 1, rz, 0.0))
    for j in range(order.shape[0]):
        rows = rows_of(order[j])
        local[rows, :] = first[rows, :] - alpha * (image[rows, :] + piece(received, j)[...].astype(F32))
    copies = [begin(local, local_out, sems.at[3]), begin(scalars, scalars_out, sems.at[4])]
    part = coarse_contribution(basis_t[...], 0.5 * local[...])

    def fill(d):
        held[d] = part

    finish_all(copies + fill_and_send(fill, held, out, sems, 5))


def stream(matrix, held, sems, first, ahead=5):
    count = held.shape[0] // CHUNK
    copies = []
    for i in range(count):
        rows = pl.ds(i * CHUNK, CHUNK)
        copies.append(pltpu.make_async_copy(matrix.at[0, rows, :], held.at[rows, :], sems.at[first + i]))
    for copy in copies[:ahead]:
        copy.start()

    def ready(i):
        copies[i].wait()
        if i + ahead < count:
            copies[i + ahead].start()

    return ready


def chunks(ref):
    return [pl.ds(i * CHUNK, CHUNK) for i in range(ref.shape[0] // CHUNK)]


def product_rows(held, rows, operand):
    return jnp.dot(held[rows, :], operand[...], preferred_element_type=F32)


def neumann_body(order, local_in, matrix, out, sums_out, held, local, operand, work, staged, sums, sems):
    load = begin(local_in, local, sems.at[16])
    ready = stream(matrix, held, sems, 0)
    load.wait()
    operand[...] = (0.5 * local[...]).astype(BF16)
    for i, rows in enumerate(chunks(held)):
        ready(i)
        scaled = 0.5 * local[rows, :]
        work[rows, :] = scaled + scaled - RELAX * product_rows(held, rows, operand)
    operand[...] = work[...].astype(BF16)
    rz = jnp.zeros((1, LANES), F32)
    for rows in chunks(held):
        value = 0.5 * (0.5 * local[rows, :] + work[rows, :] - RELAX * product_rows(held, rows, operand))
        work[rows, :] = value
        rz = rz + jnp.sum(local[rows, :] * value, axis=0, keepdims=True)
    sums[...] = tile_of([rz], F32)
    finish_all([begin(sums, sums_out, sems.at[17])] + pack(order, work, None, staged, out, sems, 18))


def first_sweep_body(local_in, matrix, base, swept, held, sums, local, operand, sems):
    load = begin(local_in, local, sems.at[16])
    ready = stream(matrix, held, sems, 0)
    load.wait()
    operand[...] = (0.5 * local[...]).astype(BF16)
    rz = jnp.zeros((1, LANES), F32)
    for i, rows in enumerate(chunks(held)):
        ready(i)
        product = product_rows(held, rows, operand)
        scaled = 0.5 * local[rows, :]
        value = scaled + scaled - RELAX * product
        rounded = value.astype(BF16)
        swept[rows, :] = rounded
        both = scaled + value
        base[rows, :] = both
        rz = rz + jnp.sum(scaled * both - RELAX * product * rounded.astype(F32), axis=0, keepdims=True)
    sums[...] = tile_of([rz], F32)


def second_sweep_body(base, swept, held, out, sems):
    for rows in chunks(held):
        out[rows, :] = 0.5 * (base[rows, :] - RELAX * product_rows(held, rows, swept))


def pack_second_body(order, local, sums0, sums1, sums2, sums3, out, token, staged, sems):
    total = sums0[...] + sums1[...] + sums2[...] + sums3[...]
    token[...] = total
    finish_all(pack(order, local, tile_of([total[0:1]], out.dtype), staged, out, sems))


def apply_body(
    order, received, matrix, earlier_in, out, image_out, held, operand, image, staged, earlier, sems
):
    load = begin(earlier_in, earlier, sems.at[16])
    ready = stream(matrix, held, sems, 0)
    for j in range(order.shape[0]):
        operand[rows_of(order[j]), :] = piece(received, j)[...]
    dot = jnp.zeros((1, LANES), F32)
    for i, rows in enumerate(chunks(held)):
        ready(i)
        product = product_rows(held, rows, operand)
        image[rows, :] = product
        dot = dot + jnp.sum(product * operand[rows, :].astype(F32), axis=0, keepdims=True)
    copy = begin(image, image_out, sems.at[17])
    load.wait()
    values = [dot, earlier[0:1, :]] if out.dtype == F32 else [dot]
    finish_all([copy] + pack(order, image, tile_of(values, out.dtype), staged, out, sems, 18))


def split_body(source, high, low, high_out, low_out, held, sems):
    parts = chunks(held)
    loads = [begin(source.at[rows, :], held.at[rows, :], sems.at[i]) for i, rows in enumerate(parts)]
    copies = []
    for i, rows in enumerate(parts):
        loads[i].wait()
        high[rows, :], low[rows, :] = split2(held[rows, :])
        copies.append(begin(high.at[rows, :], high_out.at[rows, :], sems.at[8 + i]))
        copies.append(begin(low.at[rows, :], low_out.at[rows, :], sems.at[16 + i]))
    finish_all(copies)


def dot_split(high, low, value):
    parts = split2(value)
    wide = jnp.dot(high[...], jnp.concatenate(parts, axis=1), preferred_element_type=F32)
    return wide[:, 0:LANES] + wide[:, LANES:] + jnp.dot(low[...], parts[0], preferred_element_type=F32)


def coarse_sum_body(place, index_row, received, token, out0, out1, out2, out3, sems):
    parts = received[:, 0:32, :].astype(F32).reshape(-1, LANES)
    split = jnp.concatenate(split3(parts), axis=1)
    group = place[0]
    for t, out in enumerate((out0, out1, out2, out3)):
        base = lax.rem(group + t, 4) * out.shape[0]
        row = lax.broadcasted_iota(I32, (out.shape[0], parts.shape[0]), 0) + base
        table = jnp.where(row == index_row[...], 1.0, 0.0).astype(BF16)
        sums = jnp.dot(table, split, preferred_element_type=F32)
        out[...] = sums[:, 0:LANES] + sums[:, LANES : 2 * LANES] + sums[:, 2 * LANES :]


def assemble_body(
    owner, index_rows, received, high, low, table, high_out, low_out, table_out, wide, sems
):
    wide[...] = jnp.zeros(wide.shape, F32)
    group = lax.broadcasted_iota(I32, (8, LANES), 1) // 32
    for k in range(owner.shape[0]):
        s, m = k // 2, k % 2
        packed = 0.5 * received[s, 32 + 8 * m : 40 + 8 * m, :]
        lanes = slice(s // 4 * LANES, (s // 4 + 1) * LANES)
        start = owner[k] * BW
        for i in range(4):
            turn = (32 * (s % 4 - i)) % LANES
            moved = pltpu.roll(packed, turn, 1) if turn else packed
            rows = pl.ds(pl.multiple_of(start + 8 * i, 8), 8)
            wide[rows, lanes] += jnp.where(group == s % 4, moved, 0.0)
    for rows in chunks(wide):
        high[rows, :], low[rows, :] = split2(wide[rows, :])
    copies = [begin(high, high_out, sems.at[0]), begin(low, low_out, sems.at[1])]
    count = index_rows.shape[0]
    turned = jnp.transpose(
        jnp.concatenate([index_rows[...], jnp.zeros((LANES - count, LANES), F32)], axis=0)
    )
    column = lax.broadcasted_iota(I32, (LANES, table.shape[1]), 1).astype(F32)
    for q in range(count):
        hit = column == turned[:, q : q + 1]
        table[q * LANES : (q + 1) * LANES, :] = jnp.where(hit, 1.0, 0.0).astype(BF16)
    finish_all(copies + [begin(table, table_out, sems.at[2])])


def gather_quarters(place, parts, held):
    quarter = parts[0].shape[0]
    for t, part in enumerate(parts):
        base = pl.multiple_of(lax.rem(place[0] + 4 - t, 4) * quarter, quarter)
        held[pl.ds(base, quarter), :] = part[...]


def solve(waits, held, inverse_high, inverse_low, high, low, table, term, rz_tile, out, rz_out, sems, first):
    waits[0]()
    solved = dot_split(inverse_high, inverse_low, held[...])
    rz = jnp.sum(held[...] * solved, axis=0, keepdims=True)
    rz_tile[...] = jnp.broadcast_to(rz, (8, LANES))
    copies = [begin(rz_tile, rz_out, sems.at[first])]
    waits[1]()
    sums = jnp.dot(table[...], jnp.concatenate(split2(solved), axis=1), preferred_element_type=F32)
    picked = sums[:, 0:LANES] + sums[:, LANES:]
    waits[2]()
    term[...] = dot_split(high, low, picked).reshape(term.shape)
    finish_all(copies + [begin(term, out, sems.at[first + 1])])


def first_solve_body(
    place, part0, part1, part2, part3, inverse_high, inverse_low, high, low, table, out, rz_out, *rest
):
    held, term, rz_tile, sems = rest
    gather_quarters(place, (part0, part1, part2, part3), held)
    waits = [lambda: None] * 3
    solve(waits, held, inverse_high, inverse_low, high, low, table, term, rz_tile, out, rz_out, sems, 0)


def second_solve_body(place, part0, part1, part2, part3, *rest):
    sources, (out, rz_out), (held, term, rz_tile), targets, sems = (
        rest[0:5],
        rest[5:7],
        rest[7:10],
        rest[10:15],
        rest[15],
    )
    inverse_high, inverse_low, high, low, table = targets
    loads = [begin(source, target, sems.at[i]) for i, (source, target) in enumerate(zip(sources, targets))]
    gather_quarters(place, (part0, part1, part2, part3), held)
    waits = [
        lambda: finish_all(loads[0:2]),
        lambda: finish_all(loads[4:5]),
        lambda: finish_all(loads[2:4]),
    ]
    solve(waits, held, inverse_high, inverse_low, high, low, table, term, rz_tile, out, rz_out, sems, 5)


def add_blocks(owner, received, total):
    total[...] = jnp.zeros(total.shape, F32)
    for k in range(owner.shape[0]):
        total[owner[k]] += piece(received, k)[...].astype(F32)


def direction_body(owner, term_in, received, direction_out, out, term, direction, sems):
    load = begin(term_in, term, sems.at[0])
    add_blocks(owner, received, direction)
    load.wait()
    direction[...] += term[...]
    copy = begin(direction, direction_out, sems.at[1])
    for k in range(owner.shape[0]):
        piece(out, k)[...] = direction[owner[k]].astype(out.dtype)
    copy.wait()


def image_body(owner, partner, received, image_out, sums, out, image, staged, sems):
    sums[...] = sum_tiles(received)

    def fill(d):
        for k in (2 * d, 2 * d + 1):
            source = partner[k]
            start = pl.multiple_of(lax.rem(source, 2) * BW, BW)
            piece(staged, k)[...] = received[lax.div(source, 2), pl.ds(start, BW), :].astype(out.dtype)

    copies = fill_and_send(fill, staged, out, sems)
    add_blocks(owner, received, image)
    finish_all(copies + [begin(image, image_out, sems.at[4])])


def next_direction_body(
    owner,
    term_in,
    received,
    before_in,
    rz_in,
    scalars_in,
    direction_out,
    out,
    later_out,
    term,
    before,
    rz_tile,
    scalars,
    direction,
    later,
    sems,
):
    loads = [
        begin(source, target, sems.at[i])
        for i, (source, target) in enumerate(
            ((rz_in, rz_tile), (scalars_in, scalars), (term_in, term), (before_in, before))
        )
    ]
    total = sum_tiles(received)[0:1]
    add_blocks(owner, received, direction)
    finish_all(loads)
    rz = total + rz_tile[0:1, :]
    ratio = rz / scalars[1:2, :]
    later[...] = jnp.broadcast_to(rz, (8, LANES))
    direction[...] = direction[...] + term[...] + ratio[None] * before[...]
    copies = [begin(direction, direction_out, sems.at[4]), begin(later, later_out, sems.at[5])]
    for k in range(owner.shape[0]):
        piece(out, k)[...] = direction[owner[k]].astype(out.dtype)
    finish_all(copies)


def finish_body(owner, received, sums0, sums1, sums2, sums3, *rest):
    sources, outs, targets, results, sems = rest[0:6], rest[6:8], rest[8:14], rest[14:16], rest[16]
    loads = [begin(source, target, sems.at[i]) for i, (source, target) in enumerate(zip(sources, targets))]
    load, first, second, image, scalars, later = targets
    solution, residual = results
    total = sums0[...] + sums1[...] + sums2[...] + sums3[...]
    add_blocks(owner, received, residual)
    finish_all(loads)
    alpha0 = scalars[0:1, :][None]
    alpha1 = (later[0:1, :] / total[0:1])[None]
    residual[...] = load[...] - alpha0 * image[...] - alpha1 * residual[...]
    copies = [begin(residual, outs[1], sems.at[6])]
    solution[...] = alpha0 * first[...] + alpha1 * second[...]
    finish_all(copies + [begin(solution, outs[0], sems.at[7])])


def final_sums_body(received, sums, sems):
    sums[...] = sum_tiles(received)


def shards(n_sub, n_grp, load, schur, coarse_basis, coarse_index, coarse_inverse, send_order, recv_owner):
    owned = shape(load.shape)
    blocks = send_order.shape[0]
    dofs = schur.shape[1]
    coarse = coarse_inverse.shape[0]
    quarter = coarse // n_grp
    local = shape((dofs, LANES))
    tile = shape((8, LANES))
    operand = shape((dofs, LANES), BF16)
    held = shape((dofs, dofs), BF16)
    square = shape((coarse, coarse), BF16)
    place = lax.axis_index("grp").astype(I32).reshape(1)
    product_flops = 2 * dofs * dofs * LANES

    def hop(payload):
        return lax.all_to_all(payload, "sub", split_axis=0, concat_axis=0, tiled=True)

    def shifted(value, step):
        return lax.ppermute(value, "grp", [(i, (i + step) % n_grp) for i in range(n_grp)])

    def over_groups(value):
        return [value] + [shifted(value, step) for step in range(1, n_grp)]

    def payload(height, dtype=F32):
        return shape((n_sub, height, LANES), dtype)

    def apply(received, earlier, dtype):
        like = payload(2 * BW + tile_height(dtype), dtype)
        return call(
            apply_body,
            "apply",
            [("s", send_order), ("v", received), ("h", schur), ("h", earlier)],
            [("h", like), ("h", local)],
            [held, operand, local, like, tile],
            flops=product_flops,
            moved=12 * MIB,
        )

    def coarse_parts(received, token):
        parts = call(
            coarse_sum_body,
            "coarse_sum",
            [("s", place), ("v", index_row), ("v", received), ("v", token)],
            [("v", shape((quarter, LANES)))] * 4,
            flops=2 * coarse * coarse * LANES * 3,
        )
        mine = parts[0]
        for step in range(1, n_grp):
            mine = mine + shifted(parts[step], step)
        return [("s", place)] + [("v", part) for part in over_groups(mine)]

    solve_scratch = [shape((coarse, LANES)), owned, tile]
    solve_flops = 2 * coarse * coarse * LANES * 8

    basis_t = jnp.swapaxes(coarse_basis[0], 0, 1)
    basis_rows = (
        coarse_basis[0].reshape(blocks, 4, 8, 32).transpose(0, 2, 1, 3).reshape(blocks, 8, LANES)
    )
    lane = lax.broadcasted_iota(I32, (8, LANES), 1)
    index_tile = jnp.where(
        lane // 32 == lax.rem(lax.axis_index("sub"), 4), jnp.tile(coarse_index.astype(F32), (8, 4)), 0.0
    )
    position = jnp.arange(blocks, dtype=I32)
    partner = jnp.sum(
        jnp.where(
            (recv_owner[:, None] == recv_owner[None, :]) & (position[:, None] != position[None, :]),
            position[None, :],
            0,
        ),
        axis=1,
    ).astype(I32)

    [sent] = call(
        pack_load_body,
        "pack_load",
        [("s", recv_owner), ("h", load)],
        [("h", payload(2 * BW))],
        copies=blocks,
    )
    inverse_high, inverse_low, kept_inverse_high, kept_inverse_low = call(
        split_body,
        "split_inverse",
        [("h", coarse_inverse)],
        [("v", square), ("v", square), ("h", square), ("h", square)],
        [shape((coarse, coarse))],
        moved=12 * MIB,
    )
    local0, parts0 = call(
        unpack_first_body,
        "unpack_first",
        [("s", send_order), ("v", hop(sent)), ("v", basis_t), ("v", basis_rows), ("v", index_tile)],
        [("h", local), ("h", payload(56))],
        [local, payload(56)],
    )
    shared0 = hop(parts0)
    sent, rz_part = call(
        neumann_body,
        "neumann",
        [("s", send_order), ("h", local0), ("h", schur)],
        [("h", payload(2 * BW)), ("h", tile)],
        [held, local, operand, local, payload(2 * BW), tile],
        flops=2 * product_flops,
        moved=12 * MIB,
    )
    gathered = hop(sent)
    index_rows = shared0[:, 48, :].reshape(n_sub // 4, 4, LANES).sum(1)
    index_row = index_rows.reshape(1, -1).astype(I32)
    high, low, table, kept_high, kept_low, kept_table = call(
        assemble_body,
        "assemble",
        [("s", recv_owner), ("v", index_rows), ("v", shared0)],
        [("v", square)] * 3 + [("h", square)] * 3,
        [shape((owned.shape[0] * BW, coarse))],
        moved=10 * MIB,
    )
    term0, coarse_rz0 = call(
        first_solve_body,
        "coarse_solve",
        coarse_parts(shared0, index_row) + [("v", a) for a in (inverse_high, inverse_low, high, low, table)],
        [("h", owned), ("h", tile)],
        solve_scratch,
        flops=solve_flops,
        moved=8 * MIB,
    )
    direction0, sent = call(
        direction_body,
        "direction",
        [("s", recv_owner), ("h", term0), ("v", gathered)],
        [("h", owned), ("v", payload(2 * BW, BF16))],
        [owned, owned],
    )

    sent, image_local = apply(hop(sent), rz_part, F32)
    image0, sums, sent = call(
        image_body,
        "image",
        [("s", recv_owner), ("s", partner), ("v", hop(sent))],
        [("h", owned), ("v", tile), ("h", payload(2 * BW, SPREAD_DTYPE))],
        [owned, payload(2 * BW, SPREAD_DTYPE)],
    )
    local1, parts1, scalars = call(
        unpack_second_body,
        "unpack_second",
        [("s", send_order), ("v", hop(sent)), ("h", local0), ("h", image_local)]
        + [("v", part) for part in over_groups(sums)]
        + [("h", coarse_rz0), ("v", basis_t)],
        [("h", local), ("h", payload(32)), ("h", tile)],
        [local, local, local, payload(32), tile, tile],
    )

    shared1 = hop(parts1)
    base, swept, matrix, sums = call(
        first_sweep_body,
        "first_sweep",
        [("h", local1), ("h", schur)],
        [("v", local), ("v", operand), ("v", held), ("v", tile)],
        [local, operand],
        flops=product_flops,
        moved=12 * MIB,
    )
    [swept] = call(
        second_sweep_body,
        "second_sweep",
        [("v", base), ("v", swept), ("v", matrix)],
        [("v", local)],
        flops=product_flops,
        moved=4 * MIB,
    )
    like = payload(2 * BW + tile_height(COLLECT_DTYPE), COLLECT_DTYPE)
    sent, token = call(
        pack_second_body,
        "pack_second",
        [("s", send_order), ("v", swept)] + [("v", part) for part in over_groups(sums)],
        [("h", like), ("v", tile)],
        [like],
    )
    gathered = hop(sent)
    term1, coarse_rz1 = call(
        second_solve_body,
        "coarse_solve",
        coarse_parts(shared1, token)
        + [("h", a) for a in (kept_inverse_high, kept_inverse_low, kept_high, kept_low, kept_table)],
        [("h", owned), ("h", tile)],
        solve_scratch + [square] * 5,
        flops=solve_flops,
        moved=8 * MIB,
    )
    direction1, sent, later = call(
        next_direction_body,
        "next_direction",
        [
            ("s", recv_owner),
            ("h", term1),
            ("v", gathered),
            ("h", direction0),
            ("h", coarse_rz1),
            ("h", scalars),
        ],
        [("h", owned), ("v", payload(2 * BW, BF16)), ("h", tile)],
        [owned, owned, tile, tile, owned, tile],
    )

    sent, _ = apply(hop(sent), rz_part, COLLECT_DTYPE)
    gathered = hop(sent)
    [sums] = call(final_sums_body, "final_sums", [("v", gathered)], [("v", tile)])
    return tuple(
        call(
            finish_body,
            "finish",
            [("s", recv_owner), ("v", gathered)]
            + [("v", part) for part in over_groups(sums)]
            + [("h", a) for a in (load, direction0, direction1, image0, scalars, later)],
            [("h", owned), ("h", owned)],
            [owned, owned, owned, owned, tile, tile, owned, owned],
        )
    )


def solution(mesh):
    both = ("sub", "grp")
    in_specs = (
        P(both, None, None),
        P(both, None, None),
        P(both, None, None),
        P(both, None),
        P(),
        P(both),
        P(both),
    )
    out_specs = (P(both, None, None), P(both, None, None))
    body = functools.partial(shards, mesh.shape["sub"], mesh.shape["grp"])
    return jax.shard_map(body, mesh=mesh, in_specs=in_specs, out_specs=out_specs, check_vma=False)
```

```python
import functools

import jax
import jax.numpy as jnp
from jax import lax
from jax.experimental import pallas as pl
from jax.experimental.pallas import tpu as pltpu
from jax.sharding import PartitionSpec as P

F32, BF16, I32 = jnp.float32, jnp.bfloat16, jnp.int32
HIGHEST = lax.Precision.HIGHEST
RELAX = 0.2
BW = 32
LANES = 128
CHUNK = 256
MIB = 1 << 20

SPREAD_DTYPE = BF16
COLLECT_DTYPE = BF16

SPECS = {
    "v": pl.BlockSpec(memory_space=pltpu.VMEM),
    "s": pl.BlockSpec(memory_space=pltpu.SMEM),
    "h": pl.BlockSpec(memory_space=pltpu.HBM),
}


def call(body, name, ins, outs, scratch=(), flops=0, moved=2 * MIB, vmem=24, copies=24):
    arrays = [pltpu.with_memory_space_constraint(a, pltpu.HBM) if kind == "h" else a for kind, a in ins]
    shapes = [pltpu.HBM(like.shape, like.dtype) if kind == "h" else like for kind, like in outs]
    return pl.pallas_call(
        body,
        name=name,
        out_shape=shapes,
        in_specs=[SPECS[kind] for kind, _ in ins],
        out_specs=[SPECS[kind] for kind, _ in outs],
        scratch_shapes=[pltpu.VMEM(like.shape, like.dtype) for like in scratch]
        + [pltpu.SemaphoreType.DMA((copies,))],
        compiler_params=pltpu.CompilerParams(vmem_limit_bytes=vmem * MIB),
        cost_estimate=pl.CostEstimate(flops=flops, bytes_accessed=moved, transcendentals=0),
    )(*arrays)


def shape(dims, dtype=F32):
    return jax.ShapeDtypeStruct(dims, dtype)


def begin(source, target, sem):
    copy = pltpu.make_async_copy(source, target, sem)
    copy.start()
    return copy


def finish_all(copies):
    for copy in copies:
        copy.wait()


def rows_of(index):
    return pl.ds(pl.multiple_of(index * BW, BW), BW)


def piece(ref, k):
    return ref.at[k // 2, (k % 2) * BW : (k % 2 + 1) * BW, :]


def split2(value):
    high = value.astype(BF16)
    return high, (value - high.astype(F32)).astype(BF16)


def split3(value):
    high = value.astype(BF16)
    rest = value - high.astype(F32)
    middle = rest.astype(BF16)
    low = (rest - middle.astype(F32)).astype(BF16)
    return high, middle, low


def tile_of(values, dtype):
    height = tile_height(dtype)
    if dtype != F32:
        values = [part.astype(F32) for value in values for part in split3(value)]
    row = lax.broadcasted_iota(I32, (height, LANES), 0)
    tile = jnp.zeros((height, LANES), F32)
    for i, value in enumerate(values):
        tile = jnp.where(row == i, value, tile)
    return tile.astype(dtype)


def tile_height(dtype):
    return 8 if dtype == F32 else 16


def sum_tiles(ref):
    total = jnp.sum(ref[:, 2 * BW :, :].astype(F32), axis=0)
    if ref.dtype == F32:
        return total
    row = lax.broadcasted_iota(I32, (8, LANES), 0)
    value = total[0:1] + total[1:2] + total[2:3]
    return jnp.where(row == 0, value, 0.0)


def fill_and_send(fill, held, out, sems, first=0):
    copies = []
    step = out.shape[0] // 4
    for part in range(4):
        for d in range(part * step, (part + 1) * step):
            fill(d)
        chosen = pl.ds(part * step, step)
        copies.append(begin(held.at[chosen], out.at[chosen], sems.at[first + part]))
    return copies


def send_quarters(held, out, sems, first=0):
    return fill_and_send(lambda d: None, held, out, sems, first)


def fill_tiles(held, tile):
    for d in range(held.shape[0]):
        held[d, 2 * BW :, :] = tile


def place_blocks(slot, rows, value, held):
    for i in range(CHUNK // BW):
        k = slot[rows.start // BW + i]
        start = pl.multiple_of(lax.rem(k, 2) * BW, BW)
        held[lax.div(k, 2), pl.ds(start, BW), :] = value[i * BW : (i + 1) * BW].astype(held.dtype)


def pack_load_body(owner, owned_in, out, owned, held, sems):
    begin(owned_in, owned, sems.at[0]).wait()

    def fill(d):
        for k in (2 * d, 2 * d + 1):
            piece(held, k)[...] = owned[owner[k]]

    finish_all(fill_and_send(fill, held, out, sems, 1))


def coarse_contribution(basis_t, scaled):
    return jnp.dot(basis_t, scaled, precision=HIGHEST, preferred_element_type=F32)


def unpack_first_body(order, received, basis_t, basis_rows, index_tile, local_out, out, local, held, sems):
    for j in range(order.shape[0]):
        local[rows_of(order[j]), :] = piece(received, j)[...]
    copies = [begin(local, local_out, sems.at[0])]
    part = coarse_contribution(basis_t[...], 0.5 * local[...])
    tile = index_tile[...]

    def fill(d):
        held[d, 0:32, :] = part
        held[d, 32:40, :] = basis_rows[order[2 * d]]
        held[d, 40:48, :] = basis_rows[order[2 * d + 1]]
        held[d, 48:56, :] = tile

    finish_all(copies + fill_and_send(fill, held, out, sems, 1))


def unpack_second_body(
    order,
    received,
    first_in,
    image_in,
    sums0,
    sums1,
    sums2,
    sums3,
    rz_in,
    basis_t,
    local_out,
    out,
    scalars_out,
    first,
    image,
    local,
    held,
    rz_tile,
    scalars,
    sems,
):
    loads = [
        begin(rz_in, rz_tile, sems.at[0]),
        begin(first_in, first, sems.at[1]),
        begin(image_in, image, sems.at[2]),
    ]
    finish_all(loads)
    total = sums0[...] + sums1[...] + sums2[...] + sums3[...]
    rz = total[1:2] + rz_tile[0:1, :]
    alpha = rz / total[0:1]
    row = lax.broadcasted_iota(I32, (8, LANES), 0)
    scalars[...] = jnp.where(row == 0, alpha, jnp.where(row == 1, rz, 0.0))
    for j in range(order.shape[0]):
        rows = rows_of(order[j])
        local[rows, :] = first[rows, :] - alpha * (image[rows, :] + piece(received, j)[...].astype(F32))
    copies = [begin(local, local_out, sems.at[3]), begin(scalars, scalars_out, sems.at[4])]
    part = coarse_contribution(basis_t[...], 0.5 * local[...])

    def fill(d):
        held[d] = part

    finish_all(copies + fill_and_send(fill, held, out, sems, 5))


def stream(matrix, held, sems, first, ahead=5):
    count = held.shape[0] // CHUNK
    copies = []
    for i in range(count):
        rows = pl.ds(i * CHUNK, CHUNK)
        copies.append(pltpu.make_async_copy(matrix.at[0, rows, :], held.at[rows, :], sems.at[first + i]))
    for copy in copies[:ahead]:
        copy.start()

    def ready(i):
        copies[i].wait()
        if i + ahead < count:
            copies[i + ahead].start()

    return ready


def chunks(ref):
    return [pl.ds(i * CHUNK, CHUNK) for i in range(ref.shape[0] // CHUNK)]


def product_rows(held, rows, operand):
    return jnp.dot(held[rows, :], operand[...], preferred_element_type=F32)


def neumann_body(slot, local_in, matrix, out, sums_out, held, local, operand, work, staged, sums, sems):
    load = begin(local_in, local, sems.at[16])
    ready = stream(matrix, held, sems, 0)
    load.wait()
    operand[...] = (0.5 * local[...]).astype(BF16)
    for i, rows in enumerate(chunks(held)):
        ready(i)
        scaled = 0.5 * local[rows, :]
        work[rows, :] = scaled + scaled - RELAX * product_rows(held, rows, operand)
    operand[...] = work[...].astype(BF16)
    rz = jnp.zeros((1, LANES), F32)
    for rows in chunks(held):
        value = 0.5 * (0.5 * local[rows, :] + work[rows, :] - RELAX * product_rows(held, rows, operand))
        place_blocks(slot, rows, value, staged)
        rz = rz + jnp.sum(local[rows, :] * value, axis=0, keepdims=True)
    copies = send_quarters(staged, out, sems, 18)
    sums[...] = tile_of([rz], F32)
    finish_all([begin(sums, sums_out, sems.at[17])] + copies)


def first_sweep_body(local_in, matrix, base, swept, held, sums, local, operand, sems):
    load = begin(local_in, local, sems.at[16])
    ready = stream(matrix, held, sems, 0)
    load.wait()
    operand[...] = (0.5 * local[...]).astype(BF16)
    rz = jnp.zeros((1, LANES), F32)
    for i, rows in enumerate(chunks(held)):
        ready(i)
        product = product_rows(held, rows, operand)
        scaled = 0.5 * local[rows, :]
        value = scaled + scaled - RELAX * product
        rounded = value.astype(BF16)
        swept[rows, :] = rounded
        both = scaled + value
        base[rows, :] = both
        rz = rz + jnp.sum(scaled * both - RELAX * product * rounded.astype(F32), axis=0, keepdims=True)
    sums[...] = tile_of([rz], F32)


def second_sweep_body(slot, base, swept, held, out, sems):
    for rows in chunks(held):
        value = 0.5 * (base[rows, :] - RELAX * product_rows(held, rows, swept))
        place_blocks(slot, rows, value, out)


def pack_second_body(packed, sums0, sums1, sums2, sums3, out, token, staged, sems):
    total = sums0[...] + sums1[...] + sums2[...] + sums3[...]
    token[...] = total
    tile = tile_of([total[0:1]], out.dtype)

    def fill(d):
        staged[d, 0 : 2 * BW, :] = packed[d]
        staged[d, 2 * BW :, :] = tile

    finish_all(fill_and_send(fill, staged, out, sems))


def apply_first_body(
    order, slot, received, matrix, earlier_in, kept, out, image_out, kept_out, held, operand, image, staged, earlier, sems
):
    load = begin(earlier_in, earlier, sems.at[16])
    copies = [begin(kept, kept_out, sems.at[22])]
    dot = apply_matrix(order, slot, received, matrix, held, operand, image, staged, sems)
    copies.append(begin(image, image_out, sems.at[17]))
    load.wait()
    fill_tiles(staged, tile_of([dot, earlier[0:1, :]], out.dtype))
    finish_all(copies + send_quarters(staged, out, sems, 18))


def apply_second_body(order, slot, received, matrix, out, held, operand, staged, sems):
    dot = apply_matrix(order, slot, received, matrix, held, operand, None, staged, sems)
    fill_tiles(staged, tile_of([dot], out.dtype))
    finish_all(send_quarters(staged, out, sems, 18))


def apply_matrix(order, slot, received, matrix, held, operand, image, staged, sems):
    ready = stream(matrix, held, sems, 0)
    for j in range(order.shape[0]):
        operand[rows_of(order[j]), :] = piece(received, j)[...]
    dot = jnp.zeros((1, LANES), F32)
    for i, rows in enumerate(chunks(held)):
        ready(i)
        product = product_rows(held, rows, operand)
        if image is not None:
            image[rows, :] = product
        place_blocks(slot, rows, product, staged)
        dot = dot + jnp.sum(product * operand[rows, :].astype(F32), axis=0, keepdims=True)
    return dot


def dot_split(high, low, value):
    parts = split2(value)
    wide = jnp.dot(high[...], jnp.concatenate(parts, axis=1), preferred_element_type=F32)
    return wide[:, 0:LANES] + wide[:, LANES:] + jnp.dot(low[...], parts[0], preferred_element_type=F32)


def coarse_sum_body(place, index_row, received, token, out0, out1, out2, out3, sems):
    parts = received[:, 0:32, :].astype(F32).reshape(-1, LANES)
    split = jnp.concatenate(split3(parts), axis=1)
    group = place[0]
    for t, out in enumerate((out0, out1, out2, out3)):
        base = lax.rem(group + t, 4) * out.shape[0]
        row = lax.broadcasted_iota(I32, (out.shape[0], parts.shape[0]), 0) + base
        table = jnp.where(row == index_row[...], 1.0, 0.0).astype(BF16)
        sums = jnp.dot(table, split, preferred_element_type=F32)
        out[...] = sums[:, 0:LANES] + sums[:, LANES : 2 * LANES] + sums[:, 2 * LANES :]


def assemble_body(
    owner, index_rows, received, inverse_in, token, inverse_high, inverse_low, high, low, table, wide, inverse, sems
):
    load = begin(inverse_in, inverse, sems.at[0])
    wide[...] = jnp.zeros(wide.shape, F32)
    group = lax.broadcasted_iota(I32, (8, LANES), 1) // 32
    for k in range(owner.shape[0]):
        s, m = k // 2, k % 2
        packed = 0.5 * received[s, 32 + 8 * m : 40 + 8 * m, :]
        lanes = slice(s // 4 * LANES, (s // 4 + 1) * LANES)
        start = owner[k] * BW
        for i in range(4):
            turn = (32 * (s % 4 - i)) % LANES
            moved = pltpu.roll(packed, turn, 1) if turn else packed
            rows = pl.ds(pl.multiple_of(start + 8 * i, 8), 8)
            wide[rows, lanes] += jnp.where(group == s % 4, moved, 0.0)
    for rows in chunks(wide):
        high[rows, :], low[rows, :] = split2(wide[rows, :])
    count = index_rows.shape[0]
    turned = jnp.transpose(
        jnp.concatenate([index_rows[...], jnp.zeros((LANES - count, LANES), F32)], axis=0)
    )
    column = lax.broadcasted_iota(I32, (LANES, table.shape[1]), 1).astype(F32)
    for q in range(count):
        hit = column == turned[:, q : q + 1]
        table[q * LANES : (q + 1) * LANES, :] = jnp.where(hit, 1.0, 0.0).astype(BF16)
    load.wait()
    for rows in chunks(inverse):
        inverse_high[rows, :], inverse_low[rows, :] = split2(inverse[rows, :])


def gather_quarters(place, parts, held):
    quarter = parts[0].shape[0]
    for t, part in enumerate(parts):
        base = pl.multiple_of(lax.rem(place[0] + 4 - t, 4) * quarter, quarter)
        held[pl.ds(base, quarter), :] = part[...]


def solve_body(
    place,
    part0,
    part1,
    part2,
    part3,
    inverse_high,
    inverse_low,
    high,
    low,
    table,
    out,
    rz_out,
    held,
    term,
    rz_tile,
    sems,
):
    gather_quarters(place, (part0, part1, part2, part3), held)
    solved = dot_split(inverse_high, inverse_low, held[...])
    rz = jnp.sum(held[...] * solved, axis=0, keepdims=True)
    rz_tile[...] = jnp.broadcast_to(rz, (8, LANES))
    copies = [begin(rz_tile, rz_out, sems.at[0])]
    sums = jnp.dot(table[...], jnp.concatenate(split2(solved), axis=1), preferred_element_type=F32)
    picked = sums[:, 0:LANES] + sums[:, LANES:]
    term[...] = dot_split(high, low, picked).reshape(term.shape)
    finish_all(copies + [begin(term, out, sems.at[1])])


def add_blocks(owner, received, total):
    total[...] = jnp.zeros(total.shape, F32)
    for k in range(owner.shape[0]):
        total[owner[k]] += piece(received, k)[...].astype(F32)


def direction_body(owner, term_in, received, direction, out, term, sems):
    load = begin(term_in, term, sems.at[0])
    add_blocks(owner, received, direction)
    load.wait()
    direction[...] += term[...]
    for k in range(owner.shape[0]):
        piece(out, k)[...] = direction[owner[k]].astype(out.dtype)


def image_body(owner, partner, received, image_out, sums, out, image, staged, sems):
    sums[...] = sum_tiles(received)

    def fill(d):
        for k in (2 * d, 2 * d + 1):
            source = partner[k]
            start = pl.multiple_of(lax.rem(source, 2) * BW, BW)
            piece(staged, k)[...] = received[lax.div(source, 2), pl.ds(start, BW), :].astype(out.dtype)

    copies = fill_and_send(fill, staged, out, sems)
    add_blocks(owner, received, image)
    finish_all(copies + [begin(image, image_out, sems.at[4])])


def next_direction_body(
    owner,
    term_in,
    received,
    before_in,
    rz_in,
    scalars_in,
    direction,
    out,
    later,
    term,
    before,
    rz_tile,
    scalars,
    sems,
):
    loads = [
        begin(source, target, sems.at[i])
        for i, (source, target) in enumerate(
            ((rz_in, rz_tile), (scalars_in, scalars), (term_in, term), (before_in, before))
        )
    ]
    total = sum_tiles(received)[0:1]
    add_blocks(owner, received, direction)
    finish_all(loads)
    rz = total + rz_tile[0:1, :]
    ratio = rz / scalars[1:2, :]
    later[...] = jnp.broadcast_to(rz, (8, LANES))
    direction[...] = direction[...] + term[...] + ratio[None] * before[...]
    for k in range(owner.shape[0]):
        piece(out, k)[...] = direction[owner[k]].astype(out.dtype)


def before_last_body(owner, received, *rest):
    sources, (image1, part, base), targets, sems = rest[0:4], rest[4:7], rest[7:11], rest[11]
    loads = [begin(source, target, sems.at[i]) for i, (source, target) in enumerate(zip(sources, targets))]
    scalars, load, image, first = targets
    add_blocks(owner, received, image1)
    finish_all(loads)
    alpha = scalars[0:1, :][None]
    base[...] = load[...] - alpha * image[...]
    part[...] = alpha * first[...]


def finish_body(image1, part, base, second, later, sums0, sums1, sums2, sums3, *rest):
    solution_out, residual_out, solution, residual, sems = rest
    total = sums0[...] + sums1[...] + sums2[...] + sums3[...]
    alpha = (later[0:1, :] / total[0:1])[None]
    residual[...] = base[...] - alpha * image1[...]
    copies = [begin(residual, residual_out, sems.at[0])]
    solution[...] = part[...] + alpha * second[...]
    finish_all(copies + [begin(solution, solution_out, sems.at[1])])


def final_sums_body(received, sums, sems):
    sums[...] = sum_tiles(received)


def shards(n_sub, n_grp, load, schur, coarse_basis, coarse_index, coarse_inverse, send_order, recv_owner):
    owned = shape(load.shape)
    blocks = send_order.shape[0]
    dofs = schur.shape[1]
    coarse = coarse_inverse.shape[0]
    quarter = coarse // n_grp
    local = shape((dofs, LANES))
    tile = shape((8, LANES))
    operand = shape((dofs, LANES), BF16)
    held = shape((dofs, dofs), BF16)
    square = shape((coarse, coarse), BF16)
    place = lax.axis_index("grp").astype(I32).reshape(1)
    product_flops = 2 * dofs * dofs * LANES

    def hop(payload):
        return lax.all_to_all(payload, "sub", split_axis=0, concat_axis=0, tiled=True)

    def shifted(value, step):
        return lax.ppermute(value, "grp", [(i, (i + step) % n_grp) for i in range(n_grp)])

    def over_groups(value):
        return [value] + [shifted(value, step) for step in range(1, n_grp)]

    def payload(height, dtype=F32):
        return shape((n_sub, height, LANES), dtype)

    def coarse_parts(received, token):
        return call(
            coarse_sum_body,
            "coarse_sum",
            [("s", place), ("v", index_row), ("v", received), ("v", token)],
            [("v", shape((quarter, LANES)))] * 4,
            flops=2 * coarse * coarse * LANES * 3,
        )

    def coarse_term(parts):
        mine = parts[0]
        for step in range(1, n_grp):
            mine = mine + shifted(parts[step], step)
        gathered = over_groups(mine)
        factors = call(
            assemble_body,
            "assemble",
            [("s", recv_owner), ("v", index_rows), ("v", shared0), ("h", coarse_inverse), ("v", mine)],
            [("v", square)] * 5,
            [shape((owned.shape[0] * BW, coarse)), shape((coarse, coarse))],
            moved=10 * MIB,
        )
        return call(
            solve_body,
            "coarse_solve",
            [("s", place)] + [("v", part) for part in gathered] + [("v", factor) for factor in factors],
            [("h", owned), ("h", tile)],
            [shape((coarse, LANES)), owned, tile],
            flops=2 * coarse * coarse * LANES * 8,
            moved=8 * MIB,
        )

    basis_t = jnp.swapaxes(coarse_basis[0], 0, 1)
    basis_rows = (
        coarse_basis[0].reshape(blocks, 4, 8, 32).transpose(0, 2, 1, 3).reshape(blocks, 8, LANES)
    )
    lane = lax.broadcasted_iota(I32, (8, LANES), 1)
    index_tile = jnp.where(
        lane // 32 == lax.rem(lax.axis_index("sub"), 4), jnp.tile(coarse_index.astype(F32), (8, 4)), 0.0
    )
    position = jnp.arange(blocks, dtype=I32)
    slot = jnp.sum(
        jnp.where(send_order[:, None] == position[None, :], position[:, None], 0), axis=0
    ).astype(I32)
    partner = jnp.sum(
        jnp.where(
            (recv_owner[:, None] == recv_owner[None, :]) & (position[:, None] != position[None, :]),
            position[None, :],
            0,
        ),
        axis=1,
    ).astype(I32)

    [sent] = call(
        pack_load_body,
        "pack_load",
        [("s", recv_owner), ("h", load)],
        [("h", payload(2 * BW))],
        [owned, payload(2 * BW)],
    )
    local0, parts0 = call(
        unpack_first_body,
        "unpack_first",
        [("s", send_order), ("v", hop(sent)), ("v", basis_t), ("v", basis_rows), ("v", index_tile)],
        [("h", local), ("h", payload(56))],
        [local, payload(56)],
    )
    shared0 = hop(parts0)
    sent, rz_part = call(
        neumann_body,
        "neumann",
        [("s", slot), ("h", local0), ("h", schur)],
        [("h", payload(2 * BW)), ("h", tile)],
        [held, local, operand, local, payload(2 * BW), tile],
        flops=2 * product_flops,
        moved=12 * MIB,
    )
    index_rows = shared0[:, 48, :].reshape(n_sub // 4, 4, LANES).sum(1)
    index_row = index_rows.reshape(1, -1).astype(I32)
    parts = coarse_parts(shared0, index_row)
    parts, sent = lax.optimization_barrier((parts, sent))
    gathered = hop(sent)
    term0, coarse_rz0 = coarse_term(parts)
    direction0, sent = call(
        direction_body,
        "direction",
        [("s", recv_owner), ("h", term0), ("v", gathered)],
        [("v", owned), ("v", payload(2 * BW, BF16))],
        [owned],
    )

    like = payload(2 * BW + tile_height(F32))
    sent, image_local, direction0 = call(
        apply_first_body,
        "apply_first",
        [
            ("s", send_order),
            ("s", slot),
            ("v", hop(sent)),
            ("h", schur),
            ("h", rz_part),
            ("v", direction0),
        ],
        [("h", like), ("h", local), ("h", owned)],
        [held, operand, local, like, tile],
        flops=product_flops,
        moved=12 * MIB,
    )
    image0, sums, sent = call(
        image_body,
        "image",
        [("s", recv_owner), ("s", partner), ("v", hop(sent))],
        [("h", owned), ("v", tile), ("h", payload(2 * BW, SPREAD_DTYPE))],
        [owned, payload(2 * BW, SPREAD_DTYPE)],
    )
    local1, parts1, scalars = call(
        unpack_second_body,
        "unpack_second",
        [("s", send_order), ("v", hop(sent)), ("h", local0), ("h", image_local)]
        + [("v", part) for part in over_groups(sums)]
        + [("h", coarse_rz0), ("v", basis_t)],
        [("h", local), ("h", payload(32)), ("h", tile)],
        [local, local, local, payload(32), tile, tile],
    )

    shared1 = hop(parts1)
    base, swept, matrix, sums = call(
        first_sweep_body,
        "first_sweep",
        [("h", local1), ("h", schur)],
        [("v", local), ("v", operand), ("v", held), ("v", tile)],
        [local, operand],
        flops=product_flops,
        moved=12 * MIB,
    )
    [packed] = call(
        second_sweep_body,
        "second_sweep",
        [("s", slot), ("v", base), ("v", swept), ("v", matrix)],
        [("v", payload(2 * BW, COLLECT_DTYPE))],
        flops=product_flops,
        moved=4 * MIB,
    )
    like = payload(2 * BW + tile_height(COLLECT_DTYPE), COLLECT_DTYPE)
    sent, token = call(
        pack_second_body,
        "pack_second",
        [("v", packed)] + [("v", part) for part in over_groups(sums)],
        [("h", like), ("v", tile)],
        [like],
    )
    gathered = hop(sent)
    term1, coarse_rz1 = coarse_term(coarse_parts(shared1, token))
    direction1, sent, later = call(
        next_direction_body,
        "next_direction",
        [
            ("s", recv_owner),
            ("h", term1),
            ("v", gathered),
            ("h", direction0),
            ("h", coarse_rz1),
            ("h", scalars),
        ],
        [("v", owned), ("v", payload(2 * BW, BF16)), ("v", tile)],
        [owned, owned, tile, tile],
    )

    [sent] = call(
        apply_second_body,
        "apply_second",
        [("s", send_order), ("s", slot), ("v", hop(sent)), ("h", schur)],
        [("h", like)],
        [held, operand, like],
        flops=product_flops,
        moved=12 * MIB,
    )
    gathered = hop(sent)
    [sums] = call(final_sums_body, "final_sums", [("v", gathered)], [("v", tile)])
    image1, part, base = call(
        before_last_body,
        "before_last",
        [("s", recv_owner), ("v", gathered)] + [("h", a) for a in (scalars, load, image0, direction0)],
        [("v", owned)] * 3,
        [tile, owned, owned, owned],
    )
    return tuple(
        call(
            finish_body,
            "finish",
            [("v", a) for a in (image1, part, base, direction1, later, *over_groups(sums))],
            [("h", owned), ("h", owned)],
            [owned, owned],
        )
    )


def solution(mesh):
    both = ("sub", "grp")
    in_specs = (
        P(both, None, None),
        P(both, None, None),
        P(both, None, None),
        P(both, None),
        P(),
        P(both),
        P(both),
    )
    out_specs = (P(both, None, None), P(both, None, None))
    body = functools.partial(shards, mesh.shape["sub"], mesh.shape["grp"])
    return jax.shard_map(body, mesh=mesh, in_specs=in_specs, out_specs=out_specs, check_vma=False)
```

```python
import functools

import jax
import jax.numpy as jnp
from jax import lax
from jax.experimental import pallas as pl
from jax.experimental.pallas import tpu as pltpu
from jax.sharding import PartitionSpec as P

F32, BF16, I32 = jnp.float32, jnp.bfloat16, jnp.int32
HIGHEST = lax.Precision.HIGHEST
RELAX = 0.2
BW = 32
LANES = 128
CHUNK = 256
MIB = 1 << 20

SPREAD_DTYPE = BF16
COLLECT_DTYPE = BF16

SPECS = {
    "v": pl.BlockSpec(memory_space=pltpu.VMEM),
    "m": pl.BlockSpec(memory_space=pltpu.VMEM),
    "s": pl.BlockSpec(memory_space=pltpu.SMEM),
    "h": pl.BlockSpec(memory_space=pltpu.HBM),
}


def call(body, name, ins, outs, scratch=(), flops=0, moved=2 * MIB, vmem=24, copies=24):
    pinned = {"h": pltpu.HBM, "m": pltpu.VMEM}
    arrays = [
        pltpu.with_memory_space_constraint(a, pinned[kind]) if kind in pinned else a for kind, a in ins
    ]
    shapes = [pinned[kind](like.shape, like.dtype) if kind in pinned else like for kind, like in outs]
    return pl.pallas_call(
        body,
        name=name,
        out_shape=shapes,
        in_specs=[SPECS[kind] for kind, _ in ins],
        out_specs=[SPECS[kind] for kind, _ in outs],
        scratch_shapes=[pltpu.VMEM(like.shape, like.dtype) for like in scratch]
        + [pltpu.SemaphoreType.DMA((copies,))],
        compiler_params=pltpu.CompilerParams(vmem_limit_bytes=vmem * MIB),
        cost_estimate=pl.CostEstimate(flops=flops, bytes_accessed=moved, transcendentals=0),
    )(*arrays)


def shape(dims, dtype=F32):
    return jax.ShapeDtypeStruct(dims, dtype)


def begin(source, target, sem):
    copy = pltpu.make_async_copy(source, target, sem)
    copy.start()
    return copy


def finish_all(copies):
    for copy in copies:
        copy.wait()


def rows_of(index):
    return pl.ds(pl.multiple_of(index * BW, BW), BW)


def piece(ref, k):
    return ref.at[k // 2, (k % 2) * BW : (k % 2 + 1) * BW, :]


def split2(value):
    high = value.astype(BF16)
    return high, (value - high.astype(F32)).astype(BF16)


def split3(value):
    high = value.astype(BF16)
    rest = value - high.astype(F32)
    middle = rest.astype(BF16)
    low = (rest - middle.astype(F32)).astype(BF16)
    return high, middle, low


def tile_of(values, dtype):
    height = tile_height(dtype)
    if dtype != F32:
        values = [part.astype(F32) for value in values for part in split3(value)]
    row = lax.broadcasted_iota(I32, (height, LANES), 0)
    tile = jnp.zeros((height, LANES), F32)
    for i, value in enumerate(values):
        tile = jnp.where(row == i, value, tile)
    return tile.astype(dtype)


def tile_height(dtype):
    return 8 if dtype == F32 else 16


def sum_tiles(ref):
    total = jnp.sum(ref[:, 2 * BW :, :].astype(F32), axis=0)
    if ref.dtype == F32:
        return total
    row = lax.broadcasted_iota(I32, (8, LANES), 0)
    value = total[0:1] + total[1:2] + total[2:3]
    return jnp.where(row == 0, value, 0.0)


def fill_and_send(fill, held, out, sems, first=0):
    copies = []
    step = out.shape[0] // 4
    for part in range(4):
        for d in range(part * step, (part + 1) * step):
            fill(d)
        chosen = pl.ds(part * step, step)
        copies.append(begin(held.at[chosen], out.at[chosen], sems.at[first + part]))
    return copies


def send_quarters(held, out, sems, first=0):
    return fill_and_send(lambda d: None, held, out, sems, first)


def fill_tiles(held, tile):
    for d in range(held.shape[0]):
        held[d, 2 * BW :, :] = tile


def place_blocks(slot, rows, value, held):
    for i in range(CHUNK // BW):
        k = slot[rows.start // BW + i]
        start = pl.multiple_of(lax.rem(k, 2) * BW, BW)
        held[lax.div(k, 2), pl.ds(start, BW), :] = value[i * BW : (i + 1) * BW].astype(held.dtype)


def pack_load_body(owner, owned_in, out, owned, held, sems):
    begin(owned_in, owned, sems.at[0]).wait()

    def fill(d):
        for k in (2 * d, 2 * d + 1):
            piece(held, k)[...] = owned[owner[k]]

    finish_all(fill_and_send(fill, held, out, sems, 1))


def coarse_contribution(basis_t, scaled):
    return jnp.dot(basis_t, scaled, precision=HIGHEST, preferred_element_type=F32)


def unpack_first_body(order, received, basis_t, basis_rows, index_tile, local_out, out, local, held, sems):
    for j in range(order.shape[0]):
        local[rows_of(order[j]), :] = piece(received, j)[...]
    copies = [begin(local, local_out, sems.at[0])]
    part = coarse_contribution(basis_t[...], 0.5 * local[...])
    tile = index_tile[...]

    def fill(d):
        held[d, 0:32, :] = part
        held[d, 32:40, :] = basis_rows[order[2 * d]]
        held[d, 40:48, :] = basis_rows[order[2 * d + 1]]
        held[d, 48:56, :] = tile

    finish_all(copies + fill_and_send(fill, held, out, sems, 1))


def unpack_second_body(
    order, received, first_in, image_in, scalars_in, basis_t, local_out, out, first, image, local, held, scalars, sems
):
    loads = [
        begin(scalars_in, scalars, sems.at[0]),
        begin(first_in, first, sems.at[1]),
        begin(image_in, image, sems.at[2]),
    ]
    finish_all(loads)
    alpha = scalars[0:1, :]
    for j in range(order.shape[0]):
        rows = rows_of(order[j])
        local[rows, :] = first[rows, :] - alpha * (image[rows, :] + piece(received, j)[...].astype(F32))
    copies = [begin(local, local_out, sems.at[3])]
    part = coarse_contribution(basis_t[...], 0.5 * local[...])

    def fill(d):
        held[d] = part

    finish_all(copies + fill_and_send(fill, held, out, sems, 5))


def stream(matrix, held, sems, first, ahead=5, start=0):
    count = held.shape[0] // CHUNK
    copies = []
    for i in range(count):
        rows = pl.ds(i * CHUNK, CHUNK)
        source = matrix.at[0, pl.ds(start + i * CHUNK, CHUNK), :]
        copies.append(pltpu.make_async_copy(source, held.at[rows, :], sems.at[first + i]))
    for copy in copies[:ahead]:
        copy.start()

    def ready(i):
        copies[i].wait()
        if i + ahead < count:
            copies[i + ahead].start()

    return ready


def chunks(ref):
    return [pl.ds(i * CHUNK, CHUNK) for i in range(ref.shape[0] // CHUNK)]


def product_rows(held, rows, operand):
    return jnp.dot(held[rows, :], operand[...], preferred_element_type=F32)


def neumann_body(slot, local_in, matrix, out, sums_out, held, local, operand, work, staged, sums, sems):
    load = begin(local_in, local, sems.at[16])
    ready = stream(matrix, held, sems, 0)
    load.wait()
    operand[...] = (0.5 * local[...]).astype(BF16)
    for i, rows in enumerate(chunks(held)):
        ready(i)
        scaled = 0.5 * local[rows, :]
        work[rows, :] = scaled + scaled - RELAX * product_rows(held, rows, operand)
    operand[...] = work[...].astype(BF16)
    rz = jnp.zeros((1, LANES), F32)
    for rows in chunks(held):
        value = 0.5 * (0.5 * local[rows, :] + work[rows, :] - RELAX * product_rows(held, rows, operand))
        place_blocks(slot, rows, value, staged)
        rz = rz + jnp.sum(local[rows, :] * value, axis=0, keepdims=True)
    copies = send_quarters(staged, out, sems, 18)
    sums[...] = tile_of([rz], F32)
    finish_all([begin(sums, sums_out, sems.at[17])] + copies)


def first_sweep_body(local_in, matrix, base, swept, held, sums, local, operand, sems):
    load = begin(local_in, local, sems.at[16])
    ready = stream(matrix, held, sems, 0)
    load.wait()
    operand[...] = (0.5 * local[...]).astype(BF16)
    rz = jnp.zeros((1, LANES), F32)
    for i, rows in enumerate(chunks(held)):
        ready(i)
        product = product_rows(held, rows, operand)
        scaled = 0.5 * local[rows, :]
        value = scaled + scaled - RELAX * product
        rounded = value.astype(BF16)
        swept[rows, :] = rounded
        both = scaled + value
        base[rows, :] = both
        rz = rz + jnp.sum(scaled * both - RELAX * product * rounded.astype(F32), axis=0, keepdims=True)
    sums[...] = tile_of([rz], F32)


def second_sweep_body(slot, base, swept, held, out, sems):
    for rows in chunks(held):
        value = 0.5 * (base[rows, :] - RELAX * product_rows(held, rows, swept))
        place_blocks(slot, rows, value, out)


def pack_second_body(packed, sums0, sums1, sums2, sums3, out, token, staged, sems):
    total = sums0[...] + sums1[...] + sums2[...] + sums3[...]
    token[...] = total
    tile = tile_of([total[0:1]], out.dtype)

    def fill(d):
        staged[d, 0 : 2 * BW, :] = packed[d]
        staged[d, 2 * BW :, :] = tile

    finish_all(fill_and_send(fill, staged, out, sems))


def apply_first_body(
    order, slot, received, half, matrix, earlier_in, kept, out, image_out, kept_out, held, operand, image, staged, earlier, sems
):
    load = begin(earlier_in, earlier, sems.at[16])
    copies = [begin(kept, kept_out, sems.at[22])]
    dot = apply_matrix(order, slot, received, half, matrix, held, operand, image, staged, sems)
    copies.append(begin(image, image_out, sems.at[17]))
    load.wait()
    fill_tiles(staged, tile_of([dot, earlier[0:1, :]], out.dtype))
    finish_all(copies + send_quarters(staged, out, sems, 18))


def apply_second_body(order, slot, received, half, matrix, out, held, operand, staged, sems):
    dot = apply_matrix(order, slot, received, half, matrix, held, operand, None, staged, sems)
    fill_tiles(staged, tile_of([dot], out.dtype))
    finish_all(send_quarters(staged, out, sems, 18))


def stage_half(matrix, half, sem):
    return begin(matrix.at[0, pl.ds(0, half.shape[0]), :], half, sem)


def apply_matrix(order, slot, received, half, matrix, held, operand, image, staged, sems):
    ready = stream(matrix, held, sems, 0, start=half.shape[0])
    for j in range(order.shape[0]):
        operand[rows_of(order[j]), :] = piece(received, j)[...]
    dot = jnp.zeros((1, LANES), F32)
    count = half.shape[0] // CHUNK
    for i, rows in enumerate(chunks(operand)):
        if i < count:
            product = product_rows(half, rows, operand)
        else:
            ready(i - count)
            product = product_rows(held, pl.ds((i - count) * CHUNK, CHUNK), operand)
        if image is not None:
            image[rows, :] = product
        place_blocks(slot, rows, product, staged)
        dot = dot + jnp.sum(product * operand[rows, :].astype(F32), axis=0, keepdims=True)
    return dot


def dot_split(high, low, value):
    parts = split2(value)
    wide = jnp.dot(high[...], jnp.concatenate(parts, axis=1), preferred_element_type=F32)
    return wide[:, 0:LANES] + wide[:, LANES:] + jnp.dot(low[...], parts[0], preferred_element_type=F32)


def coarse_sum_body(place, index_row, received, token, out0, out1, out2, out3, sems):
    parts = received[:, 0:32, :].astype(F32).reshape(-1, LANES)
    split = jnp.concatenate(split3(parts), axis=1)
    group = place[0]
    for t, out in enumerate((out0, out1, out2, out3)):
        base = lax.rem(group + t, 4) * out.shape[0]
        row = lax.broadcasted_iota(I32, (out.shape[0], parts.shape[0]), 0) + base
        table = jnp.where(row == index_row[...], 1.0, 0.0).astype(BF16)
        sums = jnp.dot(table, split, preferred_element_type=F32)
        out[...] = sums[:, 0:LANES] + sums[:, LANES : 2 * LANES] + sums[:, 2 * LANES :]


def assemble_body(
    owner, index_rows, received, inverse_in, token, inverse_high, inverse_low, high, low, table, wide, inverse, sems
):
    load = begin(inverse_in, inverse, sems.at[0])
    wide[...] = jnp.zeros(wide.shape, F32)
    group = lax.broadcasted_iota(I32, (8, LANES), 1) // 32
    for k in range(owner.shape[0]):
        s, m = k // 2, k % 2
        packed = 0.5 * received[s, 32 + 8 * m : 40 + 8 * m, :]
        lanes = slice(s // 4 * LANES, (s // 4 + 1) * LANES)
        start = owner[k] * BW
        for i in range(4):
            turn = (32 * (s % 4 - i)) % LANES
            moved = pltpu.roll(packed, turn, 1) if turn else packed
            rows = pl.ds(pl.multiple_of(start + 8 * i, 8), 8)
            wide[rows, lanes] += jnp.where(group == s % 4, moved, 0.0)
    for rows in chunks(wide):
        high[rows, :], low[rows, :] = split2(wide[rows, :])
    count = index_rows.shape[0]
    turned = jnp.transpose(
        jnp.concatenate([index_rows[...], jnp.zeros((LANES - count, LANES), F32)], axis=0)
    )
    column = lax.broadcasted_iota(I32, (LANES, table.shape[1]), 1).astype(F32)
    for q in range(count):
        hit = column == turned[:, q : q + 1]
        table[q * LANES : (q + 1) * LANES, :] = jnp.where(hit, 1.0, 0.0).astype(BF16)
    load.wait()
    for rows in chunks(inverse):
        inverse_high[rows, :], inverse_low[rows, :] = split2(inverse[rows, :])


def gather_quarters(place, parts, held):
    quarter = parts[0].shape[0]
    for t, part in enumerate(parts):
        base = pl.multiple_of(lax.rem(place[0] + 4 - t, 4) * quarter, quarter)
        held[pl.ds(base, quarter), :] = part[...]


def solve_body(
    place,
    part0,
    part1,
    part2,
    part3,
    inverse_high,
    inverse_low,
    high,
    low,
    table,
    out,
    rz_out,
    held,
    term,
    rz_tile,
    sems,
):
    gather_quarters(place, (part0, part1, part2, part3), held)
    solved = dot_split(inverse_high, inverse_low, held[...])
    rz = jnp.sum(held[...] * solved, axis=0, keepdims=True)
    rz_tile[...] = jnp.broadcast_to(rz, (8, LANES))
    copies = [begin(rz_tile, rz_out, sems.at[0])]
    sums = jnp.dot(table[...], jnp.concatenate(split2(solved), axis=1), preferred_element_type=F32)
    picked = sums[:, 0:LANES] + sums[:, LANES:]
    term[...] = dot_split(high, low, picked).reshape(term.shape)
    finish_all(copies + [begin(term, out, sems.at[1])])


def add_blocks(owner, received, total):
    total[...] = jnp.zeros(total.shape, F32)
    for k in range(owner.shape[0]):
        total[owner[k]] += piece(received, k)[...].astype(F32)


def direction_body(owner, term_in, received, matrix, direction, out, half, term, sems):
    load = begin(term_in, term, sems.at[0])
    staged = stage_half(matrix, half, sems.at[1])
    add_blocks(owner, received, direction)
    load.wait()
    direction[...] += term[...]
    for k in range(owner.shape[0]):
        piece(out, k)[...] = direction[owner[k]].astype(out.dtype)
    staged.wait()


def image_body(owner, partner, received, image_out, sums, out, image, staged, sems):
    sums[...] = sum_tiles(received)

    def fill(d):
        for k in (2 * d, 2 * d + 1):
            source = partner[k]
            start = pl.multiple_of(lax.rem(source, 2) * BW, BW)
            piece(staged, k)[...] = received[lax.div(source, 2), pl.ds(start, BW), :].astype(out.dtype)

    copies = fill_and_send(fill, staged, out, sems)
    add_blocks(owner, received, image)
    finish_all(copies + [begin(image, image_out, sems.at[4])])


def next_direction_body(
    owner,
    term_in,
    received,
    before_in,
    rz_in,
    scalars_in,
    matrix,
    direction,
    out,
    later,
    half,
    term,
    before,
    rz_tile,
    scalars,
    sems,
):
    loads = [
        begin(source, target, sems.at[i])
        for i, (source, target) in enumerate(
            ((rz_in, rz_tile), (scalars_in, scalars), (term_in, term), (before_in, before))
        )
    ]
    staged = stage_half(matrix, half, sems.at[4])
    total = sum_tiles(received)[0:1]
    add_blocks(owner, received, direction)
    finish_all(loads)
    rz = total + rz_tile[0:1, :]
    ratio = rz / scalars[1:2, :]
    later[...] = jnp.broadcast_to(rz, (8, LANES))
    direction[...] = direction[...] + term[...] + ratio[None] * before[...]
    for k in range(owner.shape[0]):
        piece(out, k)[...] = direction[owner[k]].astype(out.dtype)
    staged.wait()


def first_update_body(sums0, sums1, sums2, sums3, *rest):
    sources, outs, targets, scalars, sems = rest[0:4], rest[4:7], rest[7:11], rest[11], rest[12]
    loads = [begin(source, target, sems.at[i]) for i, (source, target) in enumerate(zip(sources, targets))]
    rz_tile, load, image, first = targets
    total = sums0[...] + sums1[...] + sums2[...] + sums3[...]
    finish_all(loads[0:1])
    rz = total[1:2] + rz_tile[0:1, :]
    alpha = rz / total[0:1]
    row = lax.broadcasted_iota(I32, (8, LANES), 0)
    scalars[...] = jnp.where(row == 0, alpha, jnp.where(row == 1, rz, 0.0))
    copies = [begin(scalars, outs[0], sems.at[4])]
    finish_all(loads[1:])
    load[...] = load[...] - alpha[None] * image[...]
    first[...] = alpha[None] * first[...]
    finish_all(copies + [begin(load, outs[1], sems.at[5]), begin(first, outs[2], sems.at[6])])


def before_last_body(owner, received, base_in, part_in, image1, base, part, sems):
    loads = [begin(base_in, base, sems.at[0]), begin(part_in, part, sems.at[1])]
    add_blocks(owner, received, image1)
    finish_all(loads)


def finish_body(image1, part, base, second, later, sums0, sums1, sums2, sums3, *rest):
    solution_out, residual_out, solution, residual, sems = rest
    total = sums0[...] + sums1[...] + sums2[...] + sums3[...]
    alpha = (later[0:1, :] / total[0:1])[None]
    residual[...] = base[...] - alpha * image1[...]
    copies = [begin(residual, residual_out, sems.at[0])]
    solution[...] = part[...] + alpha * second[...]
    finish_all(copies + [begin(solution, solution_out, sems.at[1])])


def final_sums_body(received, sums, sems):
    sums[...] = sum_tiles(received)


def shards(n_sub, n_grp, load, schur, coarse_basis, coarse_index, coarse_inverse, send_order, recv_owner):
    owned = shape(load.shape)
    blocks = send_order.shape[0]
    dofs = schur.shape[1]
    coarse = coarse_inverse.shape[0]
    quarter = coarse // n_grp
    local = shape((dofs, LANES))
    tile = shape((8, LANES))
    operand = shape((dofs, LANES), BF16)
    held = shape((dofs, dofs), BF16)
    half_held = shape((dofs // 2, dofs), BF16)
    square = shape((coarse, coarse), BF16)
    place = lax.axis_index("grp").astype(I32).reshape(1)
    product_flops = 2 * dofs * dofs * LANES

    def hop(payload):
        return lax.all_to_all(payload, "sub", split_axis=0, concat_axis=0, tiled=True)

    def shifted(value, step):
        return lax.ppermute(value, "grp", [(i, (i + step) % n_grp) for i in range(n_grp)])

    def over_groups(value):
        return [value] + [shifted(value, step) for step in range(1, n_grp)]

    def payload(height, dtype=F32):
        return shape((n_sub, height, LANES), dtype)

    def coarse_parts(received, token):
        return call(
            coarse_sum_body,
            "coarse_sum",
            [("s", place), ("v", index_row), ("v", received), ("v", token)],
            [("v", shape((quarter, LANES)))] * 4,
            flops=2 * coarse * coarse * LANES * 3,
        )

    def coarse_term(parts, early):
        mine = parts[0]
        for step in range(1, n_grp):
            mine = mine + shifted(parts[step], step)
        factors = call(
            assemble_body,
            "assemble",
            [("s", recv_owner), ("v", index_rows), ("v", shared0), ("h", coarse_inverse), ("v", parts[0] if early else mine)],
            [("v", square)] * 5,
            [shape((owned.shape[0] * BW, coarse)), shape((coarse, coarse))],
            moved=10 * MIB,
        )
        if early:
            mine, factors = lax.optimization_barrier((mine, factors))
        gathered = over_groups(mine)
        return call(
            solve_body,
            "coarse_solve",
            [("s", place)] + [("v", part) for part in gathered] + [("v", factor) for factor in factors],
            [("h", owned), ("h", tile)],
            [shape((coarse, LANES)), owned, tile],
            flops=2 * coarse * coarse * LANES * 8,
            moved=8 * MIB,
        )

    basis_t = jnp.swapaxes(coarse_basis[0], 0, 1)
    basis_rows = (
        coarse_basis[0].reshape(blocks, 4, 8, 32).transpose(0, 2, 1, 3).reshape(blocks, 8, LANES)
    )
    lane = lax.broadcasted_iota(I32, (8, LANES), 1)
    index_tile = jnp.where(
        lane // 32 == lax.rem(lax.axis_index("sub"), 4), jnp.tile(coarse_index.astype(F32), (8, 4)), 0.0
    )
    position = jnp.arange(blocks, dtype=I32)
    slot = jnp.sum(
        jnp.where(send_order[:, None] == position[None, :], position[:, None], 0), axis=0
    ).astype(I32)
    partner = jnp.sum(
        jnp.where(
            (recv_owner[:, None] == recv_owner[None, :]) & (position[:, None] != position[None, :]),
            position[None, :],
            0,
        ),
        axis=1,
    ).astype(I32)

    [sent] = call(
        pack_load_body,
        "pack_load",
        [("s", recv_owner), ("h", load)],
        [("h", payload(2 * BW))],
        [owned, payload(2 * BW)],
    )
    local0, parts0 = call(
        unpack_first_body,
        "unpack_first",
        [("s", send_order), ("v", hop(sent)), ("v", basis_t), ("v", basis_rows), ("v", index_tile)],
        [("h", local), ("h", payload(56))],
        [local, payload(56)],
    )
    shared0 = hop(parts0)
    sent, rz_part = call(
        neumann_body,
        "neumann",
        [("s", slot), ("h", local0), ("h", schur)],
        [("h", payload(2 * BW)), ("h", tile)],
        [held, local, operand, local, payload(2 * BW), tile],
        flops=2 * product_flops,
        moved=12 * MIB,
    )
    index_rows = shared0[:, 48, :].reshape(n_sub // 4, 4, LANES).sum(1)
    index_row = index_rows.reshape(1, -1).astype(I32)
    parts = coarse_parts(shared0, index_row)
    parts, sent = lax.optimization_barrier((parts, sent))
    gathered = hop(sent)
    term0, coarse_rz0 = coarse_term(parts, True)
    direction0, sent, half = call(
        direction_body,
        "direction",
        [("s", recv_owner), ("h", term0), ("v", gathered), ("h", schur)],
        [("v", owned), ("v", payload(2 * BW, BF16)), ("m", half_held)],
        [owned],
    )

    like = payload(2 * BW + tile_height(F32))
    sent, image_local, direction0 = call(
        apply_first_body,
        "apply_first",
        [
            ("s", send_order),
            ("s", slot),
            ("v", hop(sent)),
            ("m", half),
            ("h", schur),
            ("h", rz_part),
            ("v", direction0),
        ],
        [("h", like), ("h", local), ("h", owned)],
        [half_held, operand, local, like, tile],
        flops=product_flops,
        moved=12 * MIB,
    )
    image0, sums, sent = call(
        image_body,
        "image",
        [("s", recv_owner), ("s", partner), ("v", hop(sent))],
        [("h", owned), ("v", tile), ("h", payload(2 * BW, SPREAD_DTYPE))],
        [owned, payload(2 * BW, SPREAD_DTYPE)],
    )
    gathered = hop(sent)
    scalars, base0, part0 = call(
        first_update_body,
        "first_update",
        [("v", part) for part in over_groups(sums)]
        + [("h", a) for a in (coarse_rz0, load, image0, direction0)],
        [("h", tile), ("h", owned), ("h", owned)],
        [tile, owned, owned, owned, tile],
    )
    local1, parts1 = call(
        unpack_second_body,
        "unpack_second",
        [("s", send_order), ("v", gathered), ("h", local0), ("h", image_local), ("h", scalars), ("v", basis_t)],
        [("h", local), ("h", payload(32))],
        [local, local, local, payload(32), tile],
    )

    shared1 = hop(parts1)
    base, swept, matrix, sums = call(
        first_sweep_body,
        "first_sweep",
        [("h", local1), ("h", schur)],
        [("v", local), ("v", operand), ("v", held), ("v", tile)],
        [local, operand],
        flops=product_flops,
        moved=12 * MIB,
    )
    [packed] = call(
        second_sweep_body,
        "second_sweep",
        [("s", slot), ("v", base), ("v", swept), ("v", matrix)],
        [("v", payload(2 * BW, COLLECT_DTYPE))],
        flops=product_flops,
        moved=4 * MIB,
    )
    like = payload(2 * BW + tile_height(COLLECT_DTYPE), COLLECT_DTYPE)
    sent, token = call(
        pack_second_body,
        "pack_second",
        [("v", packed)] + [("v", part) for part in over_groups(sums)],
        [("h", like), ("v", tile)],
        [like],
    )
    gathered = hop(sent)
    term1, coarse_rz1 = coarse_term(coarse_parts(shared1, token), False)
    direction1, sent, later, half = call(
        next_direction_body,
        "next_direction",
        [
            ("s", recv_owner),
            ("h", term1),
            ("v", gathered),
            ("h", direction0),
            ("h", coarse_rz1),
            ("h", scalars),
            ("h", schur),
        ],
        [("v", owned), ("v", payload(2 * BW, BF16)), ("v", tile), ("m", half_held)],
        [owned, owned, tile, tile],
    )

    [sent] = call(
        apply_second_body,
        "apply_second",
        [("s", send_order), ("s", slot), ("v", hop(sent)), ("m", half), ("h", schur)],
        [("h", like)],
        [half_held, operand, like],
        flops=product_flops,
        moved=12 * MIB,
    )
    gathered = hop(sent)
    [sums] = call(final_sums_body, "final_sums", [("v", gathered)], [("v", tile)])
    image1, base, part = call(
        before_last_body,
        "before_last",
        [("s", recv_owner), ("v", gathered), ("h", base0), ("h", part0)],
        [("v", owned)] * 3,
    )
    return tuple(
        call(
            finish_body,
            "finish",
            [("v", a) for a in (image1, part, base, direction1, later, *over_groups(sums))],
            [("h", owned), ("h", owned)],
            [owned, owned],
        )
    )


def solution(mesh):
    both = ("sub", "grp")
    in_specs = (
        P(both, None, None),
        P(both, None, None),
        P(both, None, None),
        P(both, None),
        P(),
        P(both),
        P(both),
    )
    out_specs = (P(both, None, None), P(both, None, None))
    body = functools.partial(shards, mesh.shape["sub"], mesh.shape["grp"])
    return jax.shard_map(body, mesh=mesh, in_specs=in_specs, out_specs=out_specs, check_vma=False)
```

```python
import functools

import jax
import jax.numpy as jnp
from jax import lax
from jax.experimental import pallas as pl
from jax.experimental.pallas import tpu as pltpu
from jax.sharding import PartitionSpec as P

F32, BF16, I32 = jnp.float32, jnp.bfloat16, jnp.int32
HIGHEST = lax.Precision.HIGHEST
RELAX = 0.2
BW = 32
LANES = 128
CHUNK = 256
MIB = 1 << 20

SPREAD_DTYPE = BF16
COLLECT_DTYPE = BF16

SPECS = {
    "v": pl.BlockSpec(memory_space=pltpu.VMEM),
    "s": pl.BlockSpec(memory_space=pltpu.SMEM),
    "h": pl.BlockSpec(memory_space=pltpu.HBM),
}


def call(body, name, ins, outs, scratch=(), flops=0, moved=2 * MIB, vmem=24, copies=32):
    arrays = [pltpu.with_memory_space_constraint(a, pltpu.HBM) if kind == "h" else a for kind, a in ins]
    shapes = [pltpu.HBM(like.shape, like.dtype) if kind == "h" else like for kind, like in outs]
    return pl.pallas_call(
        body,
        name=name,
        out_shape=shapes,
        in_specs=[SPECS[kind] for kind, _ in ins],
        out_specs=[SPECS[kind] for kind, _ in outs],
        scratch_shapes=[pltpu.VMEM(like.shape, like.dtype) for like in scratch]
        + [pltpu.SemaphoreType.DMA((copies,))],
        compiler_params=pltpu.CompilerParams(vmem_limit_bytes=vmem * MIB),
        cost_estimate=pl.CostEstimate(flops=flops, bytes_accessed=moved, transcendentals=0),
    )(*arrays)


def shape(dims, dtype=F32):
    return jax.ShapeDtypeStruct(dims, dtype)


def begin(source, target, sem):
    copy = pltpu.make_async_copy(source, target, sem)
    copy.start()
    return copy


def finish_all(copies):
    for copy in copies:
        copy.wait()


def rows_of(index):
    return pl.ds(pl.multiple_of(index * BW, BW), BW)


def piece(ref, k):
    return ref.at[k // 2, (k % 2) * BW : (k % 2 + 1) * BW, :]


def split2(value):
    high = value.astype(BF16)
    return high, (value - high.astype(F32)).astype(BF16)


def split3(value):
    high = value.astype(BF16)
    rest = value - high.astype(F32)
    middle = rest.astype(BF16)
    low = (rest - middle.astype(F32)).astype(BF16)
    return high, middle, low


def tile_of(values, dtype):
    height = tile_height(dtype)
    if dtype != F32:
        values = [part.astype(F32) for value in values for part in split3(value)]
    row = lax.broadcasted_iota(I32, (height, LANES), 0)
    tile = jnp.zeros((height, LANES), F32)
    for i, value in enumerate(values):
        tile = jnp.where(row == i, value, tile)
    return tile.astype(dtype)


def tile_height(dtype):
    return 8 if dtype == F32 else 16


def sum_tiles(ref):
    total = jnp.sum(ref[:, 2 * BW :, :].astype(F32), axis=0)
    if ref.dtype == F32:
        return total
    row = lax.broadcasted_iota(I32, (8, LANES), 0)
    value = total[0:1] + total[1:2] + total[2:3]
    return jnp.where(row == 0, value, 0.0)


def fill_and_send(fill, held, out, sems, first=0):
    copies = []
    step = out.shape[0] // 4
    for part in range(4):
        for d in range(part * step, (part + 1) * step):
            fill(d)
        chosen = pl.ds(part * step, step)
        copies.append(begin(held.at[chosen], out.at[chosen], sems.at[first + part]))
    return copies


def send_quarters(held, out, sems, first=0):
    return fill_and_send(lambda d: None, held, out, sems, first)


def fill_tiles(held, tile):
    for d in range(held.shape[0]):
        held[d, 2 * BW :, :] = tile


def place_blocks(slot, rows, value, held):
    for i in range(CHUNK // BW):
        k = slot[rows.start // BW + i]
        start = pl.multiple_of(lax.rem(k, 2) * BW, BW)
        held[lax.div(k, 2), pl.ds(start, BW), :] = value[i * BW : (i + 1) * BW].astype(held.dtype)


def pack_load_body(owner, owned_in, out, owned, held, sems):
    begin(owned_in, owned, sems.at[0]).wait()

    def fill(d):
        for k in (2 * d, 2 * d + 1):
            piece(held, k)[...] = owned[owner[k]]

    finish_all(fill_and_send(fill, held, out, sems, 1))


def coarse_contribution(basis_t, scaled):
    return jnp.dot(basis_t, scaled, precision=HIGHEST, preferred_element_type=F32)


def unpack_first_body(order, received, basis_t, basis_rows, index_tile, local_out, out, local, held, sems):
    for j in range(order.shape[0]):
        local[rows_of(order[j]), :] = piece(received, j)[...]
    copies = [begin(local, local_out, sems.at[0])]
    part = coarse_contribution(basis_t[...], 0.5 * local[...])
    tile = index_tile[...]

    def fill(d):
        held[d, 0:32, :] = part
        held[d, 32:40, :] = basis_rows[order[2 * d]]
        held[d, 40:48, :] = basis_rows[order[2 * d + 1]]
        held[d, 48:56, :] = tile

    finish_all(copies + fill_and_send(fill, held, out, sems, 1))


def unpack_second_body(
    slot, received, first_in, image_in, scalars_in, basis_t, local_out, out, first, image, local, held, scalars, sems
):
    load = begin(scalars_in, scalars, sems.at[0])
    parts = chunks(local)
    firsts = [begin(first_in.at[rows, :], first.at[rows, :], sems.at[1 + i]) for i, rows in enumerate(parts)]
    images = [begin(image_in.at[rows, :], image.at[rows, :], sems.at[9 + i]) for i, rows in enumerate(parts)]
    load.wait()
    alpha = scalars[0:1, :]
    copies = []
    for i, rows in enumerate(parts):
        firsts[i].wait()
        images[i].wait()
        for b in range(rows.start // BW, (rows.start + CHUNK) // BW):
            k = slot[b]
            start = pl.multiple_of(lax.rem(k, 2) * BW, BW)
            arrived = received[lax.div(k, 2), pl.ds(start, BW), :].astype(F32)
            block = pl.ds(b * BW, BW)
            local[block, :] = first[block, :] - alpha * (image[block, :] + arrived)
        copies.append(begin(local.at[rows, :], local_out.at[rows, :], sems.at[17 + i]))
    part = coarse_contribution(basis_t[...], 0.5 * local[...])

    def fill(d):
        held[d] = part

    finish_all(copies + fill_and_send(fill, held, out, sems, 25))


def stream(matrix, held, sems, first, ahead=5):
    count = held.shape[0] // CHUNK
    copies = []
    for i in range(count):
        rows = pl.ds(i * CHUNK, CHUNK)
        copies.append(pltpu.make_async_copy(matrix.at[0, rows, :], held.at[rows, :], sems.at[first + i]))
    for copy in copies[:ahead]:
        copy.start()

    def ready(i):
        copies[i].wait()
        if i + ahead < count:
            copies[i + ahead].start()

    return ready


def chunks(ref):
    return [pl.ds(i * CHUNK, CHUNK) for i in range(ref.shape[0] // CHUNK)]


def product_rows(held, rows, operand):
    return jnp.dot(held[rows, :], operand[...], preferred_element_type=F32)


def neumann_body(slot, local_in, matrix, out, sums_out, held, local, operand, work, staged, sums, sems):
    load = begin(local_in, local, sems.at[16])
    ready = stream(matrix, held, sems, 0)
    load.wait()
    operand[...] = (0.5 * local[...]).astype(BF16)
    for i, rows in enumerate(chunks(held)):
        ready(i)
        scaled = 0.5 * local[rows, :]
        work[rows, :] = scaled + scaled - RELAX * product_rows(held, rows, operand)
    operand[...] = work[...].astype(BF16)
    rz = jnp.zeros((1, LANES), F32)
    for rows in chunks(held):
        value = 0.5 * (0.5 * local[rows, :] + work[rows, :] - RELAX * product_rows(held, rows, operand))
        place_blocks(slot, rows, value, staged)
        rz = rz + jnp.sum(local[rows, :] * value, axis=0, keepdims=True)
    copies = send_quarters(staged, out, sems, 18)
    sums[...] = tile_of([rz], F32)
    finish_all([begin(sums, sums_out, sems.at[17])] + copies)


def first_sweep_body(local_in, matrix, base, swept, held, sums, local, operand, sems):
    load = begin(local_in, local, sems.at[16])
    ready = stream(matrix, held, sems, 0)
    load.wait()
    operand[...] = (0.5 * local[...]).astype(BF16)
    rz = jnp.zeros((1, LANES), F32)
    for i, rows in enumerate(chunks(held)):
        ready(i)
        product = product_rows(held, rows, operand)
        scaled = 0.5 * local[rows, :]
        value = scaled + scaled - RELAX * product
        rounded = value.astype(BF16)
        swept[rows, :] = rounded
        both = scaled + value
        base[rows, :] = both
        rz = rz + jnp.sum(scaled * both - RELAX * product * rounded.astype(F32), axis=0, keepdims=True)
    sums[...] = tile_of([rz], F32)


def second_sweep_body(slot, base, swept, held, out, sems):
    for rows in chunks(held):
        value = 0.5 * (base[rows, :] - RELAX * product_rows(held, rows, swept))
        place_blocks(slot, rows, value, out)


def pack_second_body(packed, sums0, sums1, sums2, sums3, out, token, staged, sems):
    total = sums0[...] + sums1[...] + sums2[...] + sums3[...]
    token[...] = total
    tile = tile_of([total[0:1]], out.dtype)

    def fill(d):
        staged[d, 0 : 2 * BW, :] = packed[d]
        staged[d, 2 * BW :, :] = tile

    finish_all(fill_and_send(fill, staged, out, sems))


def apply_first_body(
    order, slot, received, matrix, earlier_in, kept, out, image_out, kept_out, held, operand, image, staged, earlier, sems
):
    load = begin(earlier_in, earlier, sems.at[16])
    copies = [begin(kept, kept_out, sems.at[22])]
    dot = apply_matrix(order, slot, received, matrix, held, operand, image, staged, sems)
    copies.append(begin(image, image_out, sems.at[17]))
    load.wait()
    fill_tiles(staged, tile_of([dot, earlier[0:1, :]], out.dtype))
    finish_all(copies + send_quarters(staged, out, sems, 18))


def apply_second_body(order, slot, received, matrix, packed, sums, held, operand, sems):
    sums[...] = tile_of([apply_matrix(order, slot, received, matrix, held, operand, None, packed, sems)], F32)


def apply_matrix(order, slot, received, matrix, held, operand, image, staged, sems):
    ready = stream(matrix, held, sems, 0)
    for j in range(order.shape[0]):
        operand[rows_of(order[j]), :] = piece(received, j)[...]
    dot = jnp.zeros((1, LANES), F32)
    for i, rows in enumerate(chunks(held)):
        ready(i)
        product = product_rows(held, rows, operand)
        if image is not None:
            image[rows, :] = product
        place_blocks(slot, rows, product, staged)
        dot = dot + jnp.sum(product * operand[rows, :].astype(F32), axis=0, keepdims=True)
    return dot


def dot_split(high, low, value):
    parts = split2(value)
    wide = jnp.dot(high[...], jnp.concatenate(parts, axis=1), preferred_element_type=F32)
    return wide[:, 0:LANES] + wide[:, LANES:] + jnp.dot(low[...], parts[0], preferred_element_type=F32)


def coarse_sum_body(place, index_row, received, token, out0, out1, out2, out3, sems):
    parts = received[:, 0:32, :].astype(F32).reshape(-1, LANES)
    split = jnp.concatenate(split3(parts), axis=1)
    group = place[0]
    for t, out in enumerate((out0, out1, out2, out3)):
        base = lax.rem(group + t, 4) * out.shape[0]
        row = lax.broadcasted_iota(I32, (out.shape[0], parts.shape[0]), 0) + base
        table = jnp.where(row == index_row[...], 1.0, 0.0).astype(BF16)
        sums = jnp.dot(table, split, preferred_element_type=F32)
        out[...] = sums[:, 0:LANES] + sums[:, LANES : 2 * LANES] + sums[:, 2 * LANES :]


def assemble_body(
    owner, index_rows, received, inverse_in, token, inverse_high, inverse_low, high, low, table, wide, inverse, sems
):
    load = begin(inverse_in, inverse, sems.at[0])
    wide[...] = jnp.zeros(wide.shape, F32)
    group = lax.broadcasted_iota(I32, (8, LANES), 1) // 32
    for k in range(owner.shape[0]):
        s, m = k // 2, k % 2
        packed = 0.5 * received[s, 32 + 8 * m : 40 + 8 * m, :]
        lanes = slice(s // 4 * LANES, (s // 4 + 1) * LANES)
        start = owner[k] * BW
        for i in range(4):
            turn = (32 * (s % 4 - i)) % LANES
            moved = pltpu.roll(packed, turn, 1) if turn else packed
            rows = pl.ds(pl.multiple_of(start + 8 * i, 8), 8)
            wide[rows, lanes] += jnp.where(group == s % 4, moved, 0.0)
    for rows in chunks(wide):
        high[rows, :], low[rows, :] = split2(wide[rows, :])
    count = index_rows.shape[0]
    turned = jnp.transpose(
        jnp.concatenate([index_rows[...], jnp.zeros((LANES - count, LANES), F32)], axis=0)
    )
    column = lax.broadcasted_iota(I32, (LANES, table.shape[1]), 1).astype(F32)
    for q in range(count):
        hit = column == turned[:, q : q + 1]
        table[q * LANES : (q + 1) * LANES, :] = jnp.where(hit, 1.0, 0.0).astype(BF16)
    load.wait()
    for rows in chunks(inverse):
        inverse_high[rows, :], inverse_low[rows, :] = split2(inverse[rows, :])


def gather_quarters(place, parts, held):
    quarter = parts[0].shape[0]
    for t, part in enumerate(parts):
        base = pl.multiple_of(lax.rem(place[0] + 4 - t, 4) * quarter, quarter)
        held[pl.ds(base, quarter), :] = part[...]


def solve_body(
    place,
    part0,
    part1,
    part2,
    part3,
    inverse_high,
    inverse_low,
    high,
    low,
    table,
    out,
    rz_out,
    held,
    term,
    rz_tile,
    sems,
):
    gather_quarters(place, (part0, part1, part2, part3), held)
    solved = dot_split(inverse_high, inverse_low, held[...])
    rz = jnp.sum(held[...] * solved, axis=0, keepdims=True)
    rz_tile[...] = jnp.broadcast_to(rz, (8, LANES))
    copies = [begin(rz_tile, rz_out, sems.at[0])]
    sums = jnp.dot(table[...], jnp.concatenate(split2(solved), axis=1), preferred_element_type=F32)
    picked = sums[:, 0:LANES] + sums[:, LANES:]
    term[...] = dot_split(high, low, picked).reshape(term.shape)
    finish_all(copies + [begin(term, out, sems.at[1])])


def add_blocks(owner, received, total):
    total[...] = jnp.zeros(total.shape, F32)
    for k in range(owner.shape[0]):
        total[owner[k]] += piece(received, k)[...].astype(F32)


def direction_body(owner, term_in, received, direction, out, term, sems):
    load = begin(term_in, term, sems.at[0])
    add_blocks(owner, received, direction)
    load.wait()
    direction[...] += term[...]
    for k in range(owner.shape[0]):
        piece(out, k)[...] = direction[owner[k]].astype(out.dtype)


def image_body(owner, partner, received, image_out, sums, out, image, staged, sems):
    sums[...] = sum_tiles(received)

    def fill(d):
        for k in (2 * d, 2 * d + 1):
            source = partner[k]
            start = pl.multiple_of(lax.rem(source, 2) * BW, BW)
            piece(staged, k)[...] = received[lax.div(source, 2), pl.ds(start, BW), :].astype(out.dtype)

    copies = fill_and_send(fill, staged, out, sems)
    add_blocks(owner, received, image)
    finish_all(copies + [begin(image, image_out, sems.at[4])])


def next_direction_body(
    owner,
    term_in,
    received,
    before_in,
    rz_in,
    scalars_in,
    direction,
    out,
    later,
    term,
    before,
    rz_tile,
    scalars,
    sems,
):
    loads = [
        begin(source, target, sems.at[i])
        for i, (source, target) in enumerate(
            ((rz_in, rz_tile), (scalars_in, scalars), (term_in, term), (before_in, before))
        )
    ]
    total = sum_tiles(received)[0:1]
    add_blocks(owner, received, direction)
    finish_all(loads)
    rz = total + rz_tile[0:1, :]
    ratio = rz / scalars[1:2, :]
    later[...] = jnp.broadcast_to(rz, (8, LANES))
    direction[...] = direction[...] + term[...] + ratio[None] * before[...]
    for k in range(owner.shape[0]):
        piece(out, k)[...] = direction[owner[k]].astype(out.dtype)


def first_update_body(sums0, sums1, sums2, sums3, *rest):
    sources, outs, targets, scalars, sems = rest[0:4], rest[4:7], rest[7:11], rest[11], rest[12]
    loads = [begin(source, target, sems.at[i]) for i, (source, target) in enumerate(zip(sources, targets))]
    rz_tile, load, image, first = targets
    total = sums0[...] + sums1[...] + sums2[...] + sums3[...]
    finish_all(loads[0:1])
    rz = total[1:2] + rz_tile[0:1, :]
    alpha = rz / total[0:1]
    row = lax.broadcasted_iota(I32, (8, LANES), 0)
    scalars[...] = jnp.where(row == 0, alpha, jnp.where(row == 1, rz, 0.0))
    copies = [begin(scalars, outs[0], sems.at[4])]
    finish_all(loads[1:])
    load[...] = load[...] - alpha[None] * image[...]
    first[...] = alpha[None] * first[...]
    finish_all(copies + [begin(load, outs[1], sems.at[5]), begin(first, outs[2], sems.at[6])])


def finish_body(
    owner, received, base_in, part_in, second, later, solution_out, residual_out, base, part, image, sems
):
    loads = [begin(part_in, part, sems.at[0]), begin(base_in, base, sems.at[1])]
    alpha = (later[0:1, :] / sum_tiles(received)[0:1])[None]
    loads[0].wait()
    part[...] += alpha * second[...]
    copies = [begin(part, solution_out, sems.at[2])]
    add_blocks(owner, received, image)
    loads[1].wait()
    base[...] -= alpha * image[...]
    finish_all(copies + [begin(base, residual_out, sems.at[3])])


def shards(n_sub, n_grp, load, schur, coarse_basis, coarse_index, coarse_inverse, send_order, recv_owner):
    owned = shape(load.shape)
    blocks = send_order.shape[0]
    dofs = schur.shape[1]
    coarse = coarse_inverse.shape[0]
    quarter = coarse // n_grp
    local = shape((dofs, LANES))
    tile = shape((8, LANES))
    operand = shape((dofs, LANES), BF16)
    held = shape((dofs, dofs), BF16)
    square = shape((coarse, coarse), BF16)
    place = lax.axis_index("grp").astype(I32).reshape(1)
    product_flops = 2 * dofs * dofs * LANES

    def hop(payload):
        return lax.all_to_all(payload, "sub", split_axis=0, concat_axis=0, tiled=True)

    def shifted(value, step):
        return lax.ppermute(value, "grp", [(i, (i + step) % n_grp) for i in range(n_grp)])

    def over_groups(value):
        return [value] + [shifted(value, step) for step in range(1, n_grp)]

    def payload(height, dtype=F32):
        return shape((n_sub, height, LANES), dtype)

    def coarse_parts(received, token):
        return call(
            coarse_sum_body,
            "coarse_sum",
            [("s", place), ("v", index_row), ("v", received), ("v", token)],
            [("v", shape((quarter, LANES)))] * 4,
            flops=2 * coarse * coarse * LANES * 3,
        )

    def coarse_term(parts, early):
        mine = parts[0]
        for step in range(1, n_grp):
            mine = mine + shifted(parts[step], step)
        factors = call(
            assemble_body,
            "assemble",
            [("s", recv_owner), ("v", index_rows), ("v", shared0), ("h", coarse_inverse), ("v", parts[0] if early else mine)],
            [("v", square)] * 5,
            [shape((owned.shape[0] * BW, coarse)), shape((coarse, coarse))],
            moved=10 * MIB,
        )
        if early:
            mine, factors = lax.optimization_barrier((mine, factors))
        gathered = over_groups(mine)
        return call(
            solve_body,
            "coarse_solve",
            [("s", place)] + [("v", part) for part in gathered] + [("v", factor) for factor in factors],
            [("h", owned), ("h", tile)],
            [shape((coarse, LANES)), owned, tile],
            flops=2 * coarse * coarse * LANES * 8,
            moved=8 * MIB,
        )

    basis_t = jnp.swapaxes(coarse_basis[0], 0, 1)
    basis_rows = (
        coarse_basis[0].reshape(blocks, 4, 8, 32).transpose(0, 2, 1, 3).reshape(blocks, 8, LANES)
    )
    lane = lax.broadcasted_iota(I32, (8, LANES), 1)
    index_tile = jnp.where(
        lane // 32 == lax.rem(lax.axis_index("sub"), 4), jnp.tile(coarse_index.astype(F32), (8, 4)), 0.0
    )
    position = jnp.arange(blocks, dtype=I32)
    slot = jnp.sum(
        jnp.where(send_order[:, None] == position[None, :], position[:, None], 0), axis=0
    ).astype(I32)
    partner = jnp.sum(
        jnp.where(
            (recv_owner[:, None] == recv_owner[None, :]) & (position[:, None] != position[None, :]),
            position[None, :],
            0,
        ),
        axis=1,
    ).astype(I32)

    [sent] = call(
        pack_load_body,
        "pack_load",
        [("s", recv_owner), ("h", load)],
        [("h", payload(2 * BW))],
        [owned, payload(2 * BW)],
    )
    local0, parts0 = call(
        unpack_first_body,
        "unpack_first",
        [("s", send_order), ("v", hop(sent)), ("v", basis_t), ("v", basis_rows), ("v", index_tile)],
        [("h", local), ("h", payload(56))],
        [local, payload(56)],
    )
    shared0 = hop(parts0)
    sent, rz_part = call(
        neumann_body,
        "neumann",
        [("s", slot), ("h", local0), ("h", schur)],
        [("h", payload(2 * BW)), ("h", tile)],
        [held, local, operand, local, payload(2 * BW), tile],
        flops=2 * product_flops,
        moved=12 * MIB,
    )
    index_rows = shared0[:, 48, :].reshape(n_sub // 4, 4, LANES).sum(1)
    index_row = index_rows.reshape(1, -1).astype(I32)
    parts = coarse_parts(shared0, index_row)
    parts, sent = lax.optimization_barrier((parts, sent))
    gathered = hop(sent)
    term0, coarse_rz0 = coarse_term(parts, True)
    direction0, sent = call(
        direction_body,
        "direction",
        [("s", recv_owner), ("h", term0), ("v", gathered)],
        [("v", owned), ("v", payload(2 * BW, BF16))],
        [owned],
    )

    like = payload(2 * BW + tile_height(F32))
    sent, image_local, direction0 = call(
        apply_first_body,
        "apply_first",
        [
            ("s", send_order),
            ("s", slot),
            ("v", hop(sent)),
            ("h", schur),
            ("h", rz_part),
            ("v", direction0),
        ],
        [("h", like), ("h", local), ("h", owned)],
        [held, operand, local, like, tile],
        flops=product_flops,
        moved=12 * MIB,
    )
    image0, sums, sent = call(
        image_body,
        "image",
        [("s", recv_owner), ("s", partner), ("v", hop(sent))],
        [("h", owned), ("v", tile), ("h", payload(2 * BW, SPREAD_DTYPE))],
        [owned, payload(2 * BW, SPREAD_DTYPE)],
    )
    gathered = hop(sent)
    scalars, base0, part0 = call(
        first_update_body,
        "first_update",
        [("v", part) for part in over_groups(sums)]
        + [("h", a) for a in (coarse_rz0, load, image0, direction0)],
        [("h", tile), ("h", owned), ("h", owned)],
        [tile, owned, owned, owned, tile],
    )
    local1, parts1 = call(
        unpack_second_body,
        "unpack_second",
        [("s", slot), ("v", gathered), ("h", local0), ("h", image_local), ("h", scalars), ("v", basis_t)],
        [("h", local), ("h", payload(32))],
        [local, local, local, payload(32), tile],
    )

    shared1 = hop(parts1)
    base, swept, matrix, sums = call(
        first_sweep_body,
        "first_sweep",
        [("h", local1), ("h", schur)],
        [("v", local), ("v", operand), ("v", held), ("v", tile)],
        [local, operand],
        flops=product_flops,
        moved=12 * MIB,
    )
    [packed] = call(
        second_sweep_body,
        "second_sweep",
        [("s", slot), ("v", base), ("v", swept), ("v", matrix)],
        [("v", payload(2 * BW, COLLECT_DTYPE))],
        flops=product_flops,
        moved=4 * MIB,
    )
    like = payload(2 * BW + tile_height(COLLECT_DTYPE), COLLECT_DTYPE)
    sent, token = call(
        pack_second_body,
        "pack_second",
        [("v", packed)] + [("v", part) for part in over_groups(sums)],
        [("h", like), ("v", tile)],
        [like],
    )
    gathered = hop(sent)
    term1, coarse_rz1 = coarse_term(coarse_parts(shared1, token), False)
    direction1, sent, later = call(
        next_direction_body,
        "next_direction",
        [
            ("s", recv_owner),
            ("h", term1),
            ("v", gathered),
            ("h", direction0),
            ("h", coarse_rz1),
            ("h", scalars),
        ],
        [("v", owned), ("v", payload(2 * BW, BF16)), ("v", tile)],
        [owned, owned, tile, tile],
    )

    packed, sums = call(
        apply_second_body,
        "apply_second",
        [("s", send_order), ("s", slot), ("v", hop(sent)), ("h", schur)],
        [("v", payload(2 * BW, COLLECT_DTYPE)), ("v", tile)],
        [held, operand],
        flops=product_flops,
        moved=12 * MIB,
    )
    sent, _ = call(
        pack_second_body,
        "pack_third",
        [("v", packed)] + [("v", part) for part in over_groups(sums)],
        [("h", like), ("v", tile)],
        [like],
    )
    return tuple(
        call(
            finish_body,
            "finish",
            [("s", recv_owner), ("v", hop(sent)), ("h", base0), ("h", part0), ("v", direction1), ("v", later)],
            [("h", owned), ("h", owned)],
            [owned, owned, owned],
        )
    )


def solution(mesh):
    both = ("sub", "grp")
    in_specs = (
        P(both, None, None),
        P(both, None, None),
        P(both, None, None),
        P(both, None),
        P(),
        P(both),
        P(both),
    )
    out_specs = (P(both, None, None), P(both, None, None))
    body = functools.partial(shards, mesh.shape["sub"], mesh.shape["grp"])
    return jax.shard_map(body, mesh=mesh, in_specs=in_specs, out_specs=out_specs, check_vma=False)
```

```python
import functools

import jax
import jax.numpy as jnp
from jax import lax
from jax.experimental import pallas as pl
from jax.experimental.pallas import tpu as pltpu
from jax.sharding import PartitionSpec as P

F32, BF16, I32 = jnp.float32, jnp.bfloat16, jnp.int32
HIGHEST = lax.Precision.HIGHEST
RELAX = 0.2
BW = 32
LANES = 128
CHUNK = 256
MIB = 1 << 20

SPREAD_DTYPE = BF16
COLLECT_DTYPE = BF16

SPECS = {
    "v": pl.BlockSpec(memory_space=pltpu.VMEM),
    "s": pl.BlockSpec(memory_space=pltpu.SMEM),
    "h": pl.BlockSpec(memory_space=pltpu.HBM),
}


def call(body, name, ins, outs, scratch=(), flops=0, moved=2 * MIB, vmem=24, copies=40):
    arrays = [pltpu.with_memory_space_constraint(a, pltpu.HBM) if kind == "h" else a for kind, a in ins]
    shapes = [pltpu.HBM(like.shape, like.dtype) if kind == "h" else like for kind, like in outs]
    return pl.pallas_call(
        body,
        name=name,
        out_shape=shapes,
        in_specs=[SPECS[kind] for kind, _ in ins],
        out_specs=[SPECS[kind] for kind, _ in outs],
        scratch_shapes=[pltpu.VMEM(like.shape, like.dtype) for like in scratch]
        + [pltpu.SemaphoreType.DMA((copies,))],
        compiler_params=pltpu.CompilerParams(vmem_limit_bytes=vmem * MIB),
        cost_estimate=pl.CostEstimate(flops=flops, bytes_accessed=moved, transcendentals=0),
    )(*arrays)


def shape(dims, dtype=F32):
    return jax.ShapeDtypeStruct(dims, dtype)


def begin(source, target, sem):
    copy = pltpu.make_async_copy(source, target, sem)
    copy.start()
    return copy


def finish_all(copies):
    for copy in copies:
        copy.wait()


def rows_of(index):
    return pl.ds(pl.multiple_of(index * BW, BW), BW)


def piece(ref, k):
    return ref.at[k // 2, (k % 2) * BW : (k % 2 + 1) * BW, :]


def split2(value):
    high = value.astype(BF16)
    return high, (value - high.astype(F32)).astype(BF16)


def split3(value):
    high = value.astype(BF16)
    rest = value - high.astype(F32)
    middle = rest.astype(BF16)
    low = (rest - middle.astype(F32)).astype(BF16)
    return high, middle, low


def tile_of(values, dtype):
    height = tile_height(dtype)
    if dtype != F32:
        values = [part.astype(F32) for value in values for part in split3(value)]
    row = lax.broadcasted_iota(I32, (height, LANES), 0)
    tile = jnp.zeros((height, LANES), F32)
    for i, value in enumerate(values):
        tile = jnp.where(row == i, value, tile)
    return tile.astype(dtype)


def tile_height(dtype):
    return 8 if dtype == F32 else 16


def sum_tiles(ref):
    total = jnp.sum(ref[:, 2 * BW :, :].astype(F32), axis=0)
    if ref.dtype == F32:
        return total
    row = lax.broadcasted_iota(I32, (8, LANES), 0)
    value = total[0:1] + total[1:2] + total[2:3]
    return jnp.where(row == 0, value, 0.0)


def fill_and_send(fill, held, out, sems, first=0):
    copies = []
    step = out.shape[0] // 4
    for part in range(4):
        for d in range(part * step, (part + 1) * step):
            fill(d)
        chosen = pl.ds(part * step, step)
        copies.append(begin(held.at[chosen], out.at[chosen], sems.at[first + part]))
    return copies


def send_quarters(held, out, sems, first=0):
    return fill_and_send(lambda d: None, held, out, sems, first)


def fill_tiles(held, tile):
    for d in range(held.shape[0]):
        held[d, 2 * BW :, :] = tile


def place_blocks(slot, rows, value, held):
    for i in range(CHUNK // BW):
        k = slot[rows.start // BW + i]
        start = pl.multiple_of(lax.rem(k, 2) * BW, BW)
        held[lax.div(k, 2), pl.ds(start, BW), :] = value[i * BW : (i + 1) * BW].astype(held.dtype)


def pack_load_body(owner, owned_in, out, owned, held, sems):
    begin(owned_in, owned, sems.at[0]).wait()

    def fill(d):
        for k in (2 * d, 2 * d + 1):
            piece(held, k)[...] = owned[owner[k]]

    finish_all(fill_and_send(fill, held, out, sems, 1))


def coarse_contribution(basis_t, scaled):
    return jnp.dot(basis_t, scaled, precision=HIGHEST, preferred_element_type=F32)


def unpack_first_body(order, received, basis_t, basis_rows, index_tile, local_out, out, local, held, sems):
    for j in range(order.shape[0]):
        local[rows_of(order[j]), :] = piece(received, j)[...]
    copies = [begin(local, local_out, sems.at[0])]
    part = coarse_contribution(basis_t[...], 0.5 * local[...])
    tile = index_tile[...]

    def fill(d):
        held[d, 0:32, :] = part
        held[d, 32:40, :] = basis_rows[order[2 * d]]
        held[d, 40:48, :] = basis_rows[order[2 * d + 1]]
        held[d, 48:56, :] = tile

    finish_all(copies + fill_and_send(fill, held, out, sems, 1))


def stream(matrix, held, sems, first, ahead=5):
    count = held.shape[0] // CHUNK
    copies = []
    for i in range(count):
        rows = pl.ds(i * CHUNK, CHUNK)
        copies.append(pltpu.make_async_copy(matrix.at[0, rows, :], held.at[rows, :], sems.at[first + i]))
    for copy in copies[:ahead]:
        copy.start()

    def ready(i):
        copies[i].wait()
        if i + ahead < count:
            copies[i + ahead].start()

    return ready


def chunks(ref):
    return [pl.ds(i * CHUNK, CHUNK) for i in range(ref.shape[0] // CHUNK)]


def product_rows(held, rows, operand):
    return jnp.dot(held[rows, :], operand[...], preferred_element_type=F32)


def neumann_body(slot, local_in, matrix, out, sums_out, held, local, operand, work, staged, sums, sems):
    load = begin(local_in, local, sems.at[16])
    ready = stream(matrix, held, sems, 0)
    load.wait()
    operand[...] = (0.5 * local[...]).astype(BF16)
    for i, rows in enumerate(chunks(held)):
        ready(i)
        scaled = 0.5 * local[rows, :]
        work[rows, :] = scaled + scaled - RELAX * product_rows(held, rows, operand)
    operand[...] = work[...].astype(BF16)
    rz = jnp.zeros((1, LANES), F32)
    for rows in chunks(held):
        value = 0.5 * (0.5 * local[rows, :] + work[rows, :] - RELAX * product_rows(held, rows, operand))
        place_blocks(slot, rows, value, staged)
        rz = rz + jnp.sum(local[rows, :] * value, axis=0, keepdims=True)
    copies = send_quarters(staged, out, sems, 18)
    sums[...] = tile_of([rz], F32)
    finish_all([begin(sums, sums_out, sems.at[17])] + copies)


def unpack_sweep_body(
    slot,
    received,
    first_in,
    image_in,
    sums0,
    sums1,
    sums2,
    sums3,
    rz_in,
    basis_t,
    matrix,
    out,
    scalars_out,
    base_out,
    swept_out,
    first,
    image,
    local,
    held,
    operand,
    base,
    swept,
    staged,
    rz_tile,
    scalars,
    sems,
):
    load = begin(rz_in, rz_tile, sems.at[0])
    parts = chunks(local)
    firsts = [begin(first_in.at[rows, :], first.at[rows, :], sems.at[1 + i]) for i, rows in enumerate(parts)]
    images = [begin(image_in.at[rows, :], image.at[rows, :], sems.at[9 + i]) for i, rows in enumerate(parts)]
    ready = stream(matrix, held, sems, 17)
    load.wait()
    total = sums0[...] + sums1[...] + sums2[...] + sums3[...]
    rz = total[1:2] + rz_tile[0:1, :]
    alpha = rz / total[0:1]
    row = lax.broadcasted_iota(I32, (8, LANES), 0)
    scalars[...] = jnp.where(row == 0, alpha, jnp.where(row == 1, rz, 0.0))
    copies = [begin(scalars, scalars_out, sems.at[25])]
    for i, rows in enumerate(parts):
        firsts[i].wait()
        images[i].wait()
        for b in range(rows.start // BW, (rows.start + CHUNK) // BW):
            k = slot[b]
            start = pl.multiple_of(lax.rem(k, 2) * BW, BW)
            arrived = received[lax.div(k, 2), pl.ds(start, BW), :].astype(F32)
            block = pl.ds(b * BW, BW)
            value = first[block, :] - alpha * (image[block, :] + arrived)
            local[block, :] = 0.5 * value
        operand[rows, :] = local[rows, :].astype(BF16)
    part = coarse_contribution(basis_t[...], local[...])
    rz = jnp.zeros((1, LANES), F32)
    for i, rows in enumerate(parts):
        ready(i)
        product = product_rows(held, rows, operand)
        scaled = local[rows, :]
        value = scaled + scaled - RELAX * product
        rounded = value.astype(BF16)
        swept[rows, :] = rounded
        both = scaled + value
        base[rows, :] = both
        rz = rz + jnp.sum(scaled * both - RELAX * product * rounded.astype(F32), axis=0, keepdims=True)
    tile = tile_of([rz], F32)

    def fill(d):
        staged[d, 0:32, :] = part
        staged[d, 32:40, :] = tile

    copies += fill_and_send(fill, staged, out, sems, 26)
    copies += [begin(base, base_out, sems.at[30]), begin(swept, swept_out, sems.at[31])]
    finish_all(copies)


def second_sweep_body(slot, base_in, swept_in, matrix, out, token, held, base, swept, staged, sems):
    loads = [begin(swept_in, swept, sems.at[8]), begin(base_in, base, sems.at[9])]
    ready = stream(matrix, held, sems, 0)
    finish_all(loads)
    for i, rows in enumerate(chunks(held)):
        ready(i)
        value = 0.5 * (base[rows, :] - RELAX * product_rows(held, rows, swept))
        place_blocks(slot, rows, value, staged)
    copies = send_quarters(staged, out, sems, 10)
    token[...] = base[0:8, :]
    finish_all(copies)


def apply_first_body(
    order, slot, received, matrix, earlier_in, kept, out, image_out, kept_out, held, operand, image, staged, earlier, sems
):
    load = begin(earlier_in, earlier, sems.at[16])
    copies = [begin(kept, kept_out, sems.at[22])]
    dot = apply_matrix(order, slot, received, matrix, held, operand, image, staged, sems)
    copies.append(begin(image, image_out, sems.at[17]))
    load.wait()
    fill_tiles(staged, tile_of([dot, earlier[0:1, :]], out.dtype))
    finish_all(copies + send_quarters(staged, out, sems, 18))


def apply_second_body(order, slot, received, matrix, out, held, operand, staged, sems):
    dot = apply_matrix(order, slot, received, matrix, held, operand, None, staged, sems)
    fill_tiles(staged, tile_of([dot], out.dtype))
    finish_all(send_quarters(staged, out, sems, 18))


def apply_matrix(order, slot, received, matrix, held, operand, image, staged, sems):
    ready = stream(matrix, held, sems, 0)
    for j in range(order.shape[0]):
        operand[rows_of(order[j]), :] = piece(received, j)[...]
    dot = jnp.zeros((1, LANES), F32)
    for i, rows in enumerate(chunks(held)):
        ready(i)
        product = product_rows(held, rows, operand)
        if image is not None:
            image[rows, :] = product
        place_blocks(slot, rows, product, staged)
        dot = dot + jnp.sum(product * operand[rows, :].astype(F32), axis=0, keepdims=True)
    return dot


def dot_split(high, low, value):
    parts = split2(value)
    wide = jnp.dot(high[...], jnp.concatenate(parts, axis=1), preferred_element_type=F32)
    return wide[:, 0:LANES] + wide[:, LANES:] + jnp.dot(low[...], parts[0], preferred_element_type=F32)


def coarse_sum_body(place, index_row, received, token, out0, out1, out2, out3, sems):
    parts = received[:, 0:32, :].astype(F32).reshape(-1, LANES)
    split = jnp.concatenate(split3(parts), axis=1)
    group = place[0]
    quarter = parts.shape[0] // 4
    for t, out in enumerate((out0, out1, out2, out3)):
        base = lax.rem(group + t, 4) * quarter
        row = lax.broadcasted_iota(I32, (quarter, parts.shape[0]), 0) + base
        table = jnp.where(row == index_row[...], 1.0, 0.0).astype(BF16)
        sums = jnp.dot(table, split, preferred_element_type=F32)
        out[0:quarter, :] = sums[:, 0:LANES] + sums[:, LANES : 2 * LANES] + sums[:, 2 * LANES :]
        if out.shape[0] > quarter:
            out[quarter:, :] = jnp.sum(received[:, 32:40, :], axis=0)


def assemble_body(
    owner, index_rows, received, inverse_in, token, inverse_high, inverse_low, high, low, table, wide, inverse, sems
):
    load = begin(inverse_in, inverse, sems.at[0])
    wide[...] = jnp.zeros(wide.shape, F32)
    group = lax.broadcasted_iota(I32, (8, LANES), 1) // 32
    for k in range(owner.shape[0]):
        s, m = k // 2, k % 2
        packed = 0.5 * received[s, 32 + 8 * m : 40 + 8 * m, :]
        lanes = slice(s // 4 * LANES, (s // 4 + 1) * LANES)
        start = owner[k] * BW
        for i in range(4):
            turn = (32 * (s % 4 - i)) % LANES
            moved = pltpu.roll(packed, turn, 1) if turn else packed
            rows = pl.ds(pl.multiple_of(start + 8 * i, 8), 8)
            wide[rows, lanes] += jnp.where(group == s % 4, moved, 0.0)
    for rows in chunks(wide):
        high[rows, :], low[rows, :] = split2(wide[rows, :])
    count = index_rows.shape[0]
    turned = jnp.transpose(
        jnp.concatenate([index_rows[...], jnp.zeros((LANES - count, LANES), F32)], axis=0)
    )
    column = lax.broadcasted_iota(I32, (LANES, table.shape[1]), 1).astype(F32)
    for q in range(count):
        hit = column == turned[:, q : q + 1]
        table[q * LANES : (q + 1) * LANES, :] = jnp.where(hit, 1.0, 0.0).astype(BF16)
    load.wait()
    for rows in chunks(inverse):
        inverse_high[rows, :], inverse_low[rows, :] = split2(inverse[rows, :])


def gather_quarters(place, parts, held):
    quarter = held.shape[0] // 4
    for t, part in enumerate(parts):
        base = pl.multiple_of(lax.rem(place[0] + 4 - t, 4) * quarter, quarter)
        held[pl.ds(base, quarter), :] = part[0:quarter, :]


def solve_body(
    place,
    part0,
    part1,
    part2,
    part3,
    inverse_high,
    inverse_low,
    high,
    low,
    table,
    out,
    rz_out,
    held,
    term,
    rz_tile,
    sems,
):
    gather_quarters(place, (part0, part1, part2, part3), held)
    solved = dot_split(inverse_high, inverse_low, held[...])
    rz = jnp.sum(held[...] * solved, axis=0, keepdims=True)
    if part0.shape[0] > held.shape[0] // 4:
        rz = rz + part0[held.shape[0] // 4 : held.shape[0] // 4 + 1, :]
    rz_tile[...] = jnp.broadcast_to(rz, (8, LANES))
    copies = [begin(rz_tile, rz_out, sems.at[0])]
    sums = jnp.dot(table[...], jnp.concatenate(split2(solved), axis=1), preferred_element_type=F32)
    picked = sums[:, 0:LANES] + sums[:, LANES:]
    term[...] = dot_split(high, low, picked).reshape(term.shape)
    finish_all(copies + [begin(term, out, sems.at[1])])


def add_blocks(owner, received, total):
    total[...] = jnp.zeros(total.shape, F32)
    for k in range(owner.shape[0]):
        total[owner[k]] += piece(received, k)[...].astype(F32)


def direction_body(owner, term_in, received, direction, out, term, sems):
    load = begin(term_in, term, sems.at[0])
    add_blocks(owner, received, direction)
    load.wait()
    direction[...] += term[...]
    for k in range(owner.shape[0]):
        piece(out, k)[...] = direction[owner[k]].astype(out.dtype)


def image_body(owner, partner, received, image_out, sums, out, image, staged, sems):
    sums[...] = sum_tiles(received)

    def fill(d):
        for k in (2 * d, 2 * d + 1):
            source = partner[k]
            start = pl.multiple_of(lax.rem(source, 2) * BW, BW)
            piece(staged, k)[...] = received[lax.div(source, 2), pl.ds(start, BW), :].astype(out.dtype)

    copies = fill_and_send(fill, staged, out, sems)
    add_blocks(owner, received, image)
    finish_all(copies + [begin(image, image_out, sems.at[4])])


def next_direction_body(
    owner,
    term_in,
    received,
    before_in,
    rz_in,
    scalars_in,
    direction,
    out,
    later,
    term,
    before,
    rz_tile,
    scalars,
    sems,
):
    loads = [
        begin(source, target, sems.at[i])
        for i, (source, target) in enumerate(
            ((rz_in, rz_tile), (scalars_in, scalars), (term_in, term), (before_in, before))
        )
    ]
    add_blocks(owner, received, direction)
    finish_all(loads)
    rz = rz_tile[0:1, :]
    ratio = rz / scalars[1:2, :]
    later[...] = jnp.broadcast_to(rz, (8, LANES))
    direction[...] = direction[...] + term[...] + ratio[None] * before[...]
    for k in range(owner.shape[0]):
        piece(out, k)[...] = direction[owner[k]].astype(out.dtype)


def before_last_body(owner, received, *rest):
    sources, (image1, part, base), targets, sems = rest[0:4], rest[4:7], rest[7:11], rest[11]
    loads = [begin(source, target, sems.at[i]) for i, (source, target) in enumerate(zip(sources, targets))]
    scalars, load, image, first = targets
    add_blocks(owner, received, image1)
    finish_all(loads)
    alpha = scalars[0:1, :][None]
    base[...] = load[...] - alpha * image[...]
    part[...] = alpha * first[...]


def finish_body(image1, part, base, second, later, sums0, sums1, sums2, sums3, *rest):
    solution_out, residual_out, solution, residual, sems = rest
    total = sums0[...] + sums1[...] + sums2[...] + sums3[...]
    alpha = (later[0:1, :] / total[0:1])[None]
    residual[...] = base[...] - alpha * image1[...]
    copies = [begin(residual, residual_out, sems.at[0])]
    solution[...] = part[...] + alpha * second[...]
    finish_all(copies + [begin(solution, solution_out, sems.at[1])])


def final_sums_body(received, sums, sems):
    sums[...] = sum_tiles(received)


def shards(n_sub, n_grp, load, schur, coarse_basis, coarse_index, coarse_inverse, send_order, recv_owner):
    owned = shape(load.shape)
    blocks = send_order.shape[0]
    dofs = schur.shape[1]
    coarse = coarse_inverse.shape[0]
    quarter = coarse // n_grp
    local = shape((dofs, LANES))
    tile = shape((8, LANES))
    operand = shape((dofs, LANES), BF16)
    held = shape((dofs, dofs), BF16)
    square = shape((coarse, coarse), BF16)
    place = lax.axis_index("grp").astype(I32).reshape(1)
    product_flops = 2 * dofs * dofs * LANES

    def hop(payload):
        return lax.all_to_all(payload, "sub", split_axis=0, concat_axis=0, tiled=True)

    def shifted(value, step):
        return lax.ppermute(value, "grp", [(i, (i + step) % n_grp) for i in range(n_grp)])

    def over_groups(value):
        return [value] + [shifted(value, step) for step in range(1, n_grp)]

    def payload(height, dtype=F32):
        return shape((n_sub, height, LANES), dtype)

    def coarse_parts(received, height, token):
        return call(
            coarse_sum_body,
            "coarse_sum",
            [("s", place), ("v", index_row), ("v", received), ("v", token)],
            [("v", shape((height, LANES)))] * 4,
            flops=2 * coarse * coarse * LANES * 3,
        )

    def coarse_term(parts, early):
        mine = parts[0]
        for step in range(1, n_grp):
            mine = mine + shifted(parts[step], step)
        factors = call(
            assemble_body,
            "assemble",
            [("s", recv_owner), ("v", index_rows), ("v", shared0), ("h", coarse_inverse), ("v", parts[0] if early else mine)],
            [("v", square)] * 5,
            [shape((owned.shape[0] * BW, coarse)), shape((coarse, coarse))],
            moved=10 * MIB,
        )
        if early:
            mine, factors = lax.optimization_barrier((mine, factors))
        gathered = over_groups(mine)
        return call(
            solve_body,
            "coarse_solve",
            [("s", place)] + [("v", part) for part in gathered] + [("v", factor) for factor in factors],
            [("h", owned), ("h", tile)],
            [shape((coarse, LANES)), owned, tile],
            flops=2 * coarse * coarse * LANES * 8,
            moved=8 * MIB,
        )

    basis_t = jnp.swapaxes(coarse_basis[0], 0, 1)
    basis_rows = (
        coarse_basis[0].reshape(blocks, 4, 8, 32).transpose(0, 2, 1, 3).reshape(blocks, 8, LANES)
    )
    lane = lax.broadcasted_iota(I32, (8, LANES), 1)
    index_tile = jnp.where(
        lane // 32 == lax.rem(lax.axis_index("sub"), 4), jnp.tile(coarse_index.astype(F32), (8, 4)), 0.0
    )
    position = jnp.arange(blocks, dtype=I32)
    slot = jnp.sum(
        jnp.where(send_order[:, None] == position[None, :], position[:, None], 0), axis=0
    ).astype(I32)
    partner = jnp.sum(
        jnp.where(
            (recv_owner[:, None] == recv_owner[None, :]) & (position[:, None] != position[None, :]),
            position[None, :],
            0,
        ),
        axis=1,
    ).astype(I32)

    [sent] = call(
        pack_load_body,
        "pack_load",
        [("s", recv_owner), ("h", load)],
        [("h", payload(2 * BW))],
        [owned, payload(2 * BW)],
    )
    local0, parts0 = call(
        unpack_first_body,
        "unpack_first",
        [("s", send_order), ("v", hop(sent)), ("v", basis_t), ("v", basis_rows), ("v", index_tile)],
        [("h", local), ("h", payload(56))],
        [local, payload(56)],
    )
    shared0 = hop(parts0)
    sent, rz_part = call(
        neumann_body,
        "neumann",
        [("s", slot), ("h", local0), ("h", schur)],
        [("h", payload(2 * BW)), ("h", tile)],
        [held, local, operand, local, payload(2 * BW), tile],
        flops=2 * product_flops,
        moved=12 * MIB,
    )
    index_rows = shared0[:, 48, :].reshape(n_sub // 4, 4, LANES).sum(1)
    index_row = index_rows.reshape(1, -1).astype(I32)
    parts = coarse_parts(shared0, quarter, index_row)
    parts, sent = lax.optimization_barrier((parts, sent))
    gathered = hop(sent)
    term0, coarse_rz0 = coarse_term(parts, True)
    direction0, sent = call(
        direction_body,
        "direction",
        [("s", recv_owner), ("h", term0), ("v", gathered)],
        [("v", owned), ("v", payload(2 * BW, BF16))],
        [owned],
    )

    like = payload(2 * BW + tile_height(F32))
    sent, image_local, direction0 = call(
        apply_first_body,
        "apply_first",
        [
            ("s", send_order),
            ("s", slot),
            ("v", hop(sent)),
            ("h", schur),
            ("h", rz_part),
            ("v", direction0),
        ],
        [("h", like), ("h", local), ("h", owned)],
        [held, operand, local, like, tile],
        flops=product_flops,
        moved=12 * MIB,
    )
    image0, sums, sent = call(
        image_body,
        "image",
        [("s", recv_owner), ("s", partner), ("v", hop(sent))],
        [("h", owned), ("v", tile), ("h", payload(2 * BW, SPREAD_DTYPE))],
        [owned, payload(2 * BW, SPREAD_DTYPE)],
    )
    parts1, scalars, base, swept = call(
        unpack_sweep_body,
        "unpack_sweep",
        [("s", slot), ("v", hop(sent)), ("h", local0), ("h", image_local)]
        + [("v", part) for part in over_groups(sums)]
        + [("h", coarse_rz0), ("v", basis_t), ("h", schur)],
        [("h", payload(40)), ("h", tile), ("h", local), ("h", operand)],
        [local, local, local, held, operand, local, operand, payload(40), tile, tile],
        flops=product_flops,
        moved=14 * MIB,
    )

    shared1 = hop(parts1)
    like = payload(2 * BW, COLLECT_DTYPE)
    sent, token = call(
        second_sweep_body,
        "second_sweep",
        [("s", slot), ("h", base), ("h", swept), ("h", schur)],
        [("h", like), ("v", tile)],
        [held, local, operand, like],
        flops=product_flops,
        moved=12 * MIB,
    )
    gathered = hop(sent)
    term1, coarse_rz1 = coarse_term(coarse_parts(shared1, quarter + 8, token), False)
    direction1, sent, later = call(
        next_direction_body,
        "next_direction",
        [
            ("s", recv_owner),
            ("h", term1),
            ("v", gathered),
            ("h", direction0),
            ("h", coarse_rz1),
            ("h", scalars),
        ],
        [("v", owned), ("v", payload(2 * BW, BF16)), ("v", tile)],
        [owned, owned, tile, tile],
    )

    like = payload(2 * BW + tile_height(COLLECT_DTYPE), COLLECT_DTYPE)
    [sent] = call(
        apply_second_body,
        "apply_second",
        [("s", send_order), ("s", slot), ("v", hop(sent)), ("h", schur)],
        [("h", like)],
        [held, operand, like],
        flops=product_flops,
        moved=12 * MIB,
    )
    gathered = hop(sent)
    [sums] = call(final_sums_body, "final_sums", [("v", gathered)], [("v", tile)])
    image1, part, base = call(
        before_last_body,
        "before_last",
        [("s", recv_owner), ("v", gathered)] + [("h", a) for a in (scalars, load, image0, direction0)],
        [("v", owned)] * 3,
        [tile, owned, owned, owned],
    )
    return tuple(
        call(
            finish_body,
            "finish",
            [("v", a) for a in (image1, part, base, direction1, later, *over_groups(sums))],
            [("h", owned), ("h", owned)],
            [owned, owned],
        )
    )


def solution(mesh):
    both = ("sub", "grp")
    in_specs = (
        P(both, None, None),
        P(both, None, None),
        P(both, None, None),
        P(both, None),
        P(),
        P(both),
        P(both),
    )
    out_specs = (P(both, None, None), P(both, None, None))
    body = functools.partial(shards, mesh.shape["sub"], mesh.shape["grp"])
    return jax.shard_map(body, mesh=mesh, in_specs=in_specs, out_specs=out_specs, check_vma=False)
```

```python
import functools

import jax
import jax.numpy as jnp
from jax import lax
from jax.experimental import pallas as pl
from jax.experimental.pallas import tpu as pltpu
from jax.sharding import PartitionSpec as P

F32, BF16, I32 = jnp.float32, jnp.bfloat16, jnp.int32
HIGHEST = lax.Precision.HIGHEST
RELAX = 0.2
BW = 32
LANES = 128
CHUNK = 256
MIB = 1 << 20

SPREAD_DTYPE = BF16
COLLECT_DTYPE = BF16

SPECS = {
    "v": pl.BlockSpec(memory_space=pltpu.VMEM),
    "s": pl.BlockSpec(memory_space=pltpu.SMEM),
    "h": pl.BlockSpec(memory_space=pltpu.HBM),
}


def call(body, name, ins, outs, scratch=(), flops=0, moved=2 * MIB, vmem=24, copies=40):
    arrays = [pltpu.with_memory_space_constraint(a, pltpu.HBM) if kind == "h" else a for kind, a in ins]
    shapes = [pltpu.HBM(like.shape, like.dtype) if kind == "h" else like for kind, like in outs]
    return pl.pallas_call(
        body,
        name=name,
        out_shape=shapes,
        in_specs=[SPECS[kind] for kind, _ in ins],
        out_specs=[SPECS[kind] for kind, _ in outs],
        scratch_shapes=[pltpu.VMEM(like.shape, like.dtype) for like in scratch]
        + [pltpu.SemaphoreType.DMA((copies,))],
        compiler_params=pltpu.CompilerParams(vmem_limit_bytes=vmem * MIB),
        cost_estimate=pl.CostEstimate(flops=flops, bytes_accessed=moved, transcendentals=0),
    )(*arrays)


def shape(dims, dtype=F32):
    return jax.ShapeDtypeStruct(dims, dtype)


def begin(source, target, sem):
    copy = pltpu.make_async_copy(source, target, sem)
    copy.start()
    return copy


def finish_all(copies):
    for copy in copies:
        copy.wait()


def rows_of(index):
    return pl.ds(pl.multiple_of(index * BW, BW), BW)


def piece(ref, k):
    return ref.at[k // 2, (k % 2) * BW : (k % 2 + 1) * BW, :]


def split2(value):
    high = value.astype(BF16)
    return high, (value - high.astype(F32)).astype(BF16)


def split3(value):
    high = value.astype(BF16)
    rest = value - high.astype(F32)
    middle = rest.astype(BF16)
    low = (rest - middle.astype(F32)).astype(BF16)
    return high, middle, low


def tile_of(values, dtype):
    height = tile_height(dtype)
    if dtype != F32:
        values = [part.astype(F32) for value in values for part in split3(value)]
    row = lax.broadcasted_iota(I32, (height, LANES), 0)
    tile = jnp.zeros((height, LANES), F32)
    for i, value in enumerate(values):
        tile = jnp.where(row == i, value, tile)
    return tile.astype(dtype)


def tile_height(dtype):
    return 8 if dtype == F32 else 16


def sum_tiles(ref):
    total = jnp.sum(ref[:, 2 * BW :, :].astype(F32), axis=0)
    if ref.dtype == F32:
        return total
    row = lax.broadcasted_iota(I32, (8, LANES), 0)
    value = total[0:1] + total[1:2] + total[2:3]
    return jnp.where(row == 0, value, 0.0)


def fill_and_send(fill, held, out, sems, first=0):
    copies = []
    step = out.shape[0] // 4
    for part in range(4):
        for d in range(part * step, (part + 1) * step):
            fill(d)
        chosen = pl.ds(part * step, step)
        copies.append(begin(held.at[chosen], out.at[chosen], sems.at[first + part]))
    return copies


def send_quarters(held, out, sems, first=0):
    return fill_and_send(lambda d: None, held, out, sems, first)


def fill_tiles(held, tile):
    for d in range(held.shape[0]):
        held[d, 2 * BW :, :] = tile


def place_blocks(slot, rows, value, held):
    for i in range(CHUNK // BW):
        k = slot[rows.start // BW + i]
        start = pl.multiple_of(lax.rem(k, 2) * BW, BW)
        held[lax.div(k, 2), pl.ds(start, BW), :] = value[i * BW : (i + 1) * BW].astype(held.dtype)


def pack_load_body(owner, owned_in, out, owned, held, sems):
    begin(owned_in, owned, sems.at[0]).wait()

    def fill(d):
        for k in (2 * d, 2 * d + 1):
            piece(held, k)[...] = owned[owner[k]]

    finish_all(fill_and_send(fill, held, out, sems, 1))


def coarse_contribution(basis_t, scaled):
    return jnp.dot(basis_t, scaled, precision=HIGHEST, preferred_element_type=F32)


def unpack_first_body(order, received, basis_t, basis_rows, index_tile, local_out, out, local, held, sems):
    for j in range(order.shape[0]):
        local[rows_of(order[j]), :] = piece(received, j)[...]
    copies = [begin(local, local_out, sems.at[0])]
    part = coarse_contribution(basis_t[...], 0.5 * local[...])
    tile = index_tile[...]

    def fill(d):
        held[d, 0:32, :] = part
        held[d, 32:40, :] = basis_rows[order[2 * d]]
        held[d, 40:48, :] = basis_rows[order[2 * d + 1]]
        held[d, 48:56, :] = tile

    finish_all(copies + fill_and_send(fill, held, out, sems, 1))


def stream(matrix, held, sems, first, ahead=5):
    count = held.shape[0] // CHUNK
    copies = []
    for i in range(count):
        rows = pl.ds(i * CHUNK, CHUNK)
        copies.append(pltpu.make_async_copy(matrix.at[0, rows, :], held.at[rows, :], sems.at[first + i]))
    for copy in copies[:ahead]:
        copy.start()

    def ready(i):
        copies[i].wait()
        if i + ahead < count:
            copies[i + ahead].start()

    return ready


def chunks(ref):
    return [pl.ds(i * CHUNK, CHUNK) for i in range(ref.shape[0] // CHUNK)]


def product_rows(held, rows, operand):
    return jnp.dot(held[rows, :], operand[...], preferred_element_type=F32)


def neumann_body(slot, local_in, matrix, out, sums_out, held, local, operand, work, staged, sums, sems):
    load = begin(local_in, local, sems.at[16])
    ready = stream(matrix, held, sems, 0)
    load.wait()
    operand[...] = (0.5 * local[...]).astype(BF16)
    for i, rows in enumerate(chunks(held)):
        ready(i)
        scaled = 0.5 * local[rows, :]
        work[rows, :] = scaled + scaled - RELAX * product_rows(held, rows, operand)
    operand[...] = work[...].astype(BF16)
    rz = jnp.zeros((1, LANES), F32)
    for rows in chunks(held):
        value = 0.5 * (0.5 * local[rows, :] + work[rows, :] - RELAX * product_rows(held, rows, operand))
        place_blocks(slot, rows, value, staged)
        rz = rz + jnp.sum(local[rows, :] * value, axis=0, keepdims=True)
    copies = send_quarters(staged, out, sems, 18)
    sums[...] = tile_of([rz], F32)
    finish_all([begin(sums, sums_out, sems.at[17])] + copies)


def unpack_sweep_body(
    slot,
    received,
    first_in,
    image_in,
    rz_in,
    basis_t,
    matrix,
    out,
    scalars_out,
    base_out,
    swept_out,
    first,
    image,
    local,
    held,
    operand,
    base,
    swept,
    staged,
    rz_tile,
    scalars,
    sems,
):
    load = begin(rz_in, rz_tile, sems.at[0])
    parts = chunks(local)
    firsts = [begin(first_in.at[rows, :], first.at[rows, :], sems.at[1 + i]) for i, rows in enumerate(parts)]
    images = [begin(image_in.at[rows, :], image.at[rows, :], sems.at[9 + i]) for i, rows in enumerate(parts)]
    ready = stream(matrix, held, sems, 17)
    load.wait()
    total = jnp.sum(received[:, 2 * BW :, :].astype(F32), axis=0)
    rz = total[3:4] + total[4:5] + total[5:6] + rz_tile[0:1, :]
    alpha = rz / (total[0:1] + total[1:2] + total[2:3])
    row = lax.broadcasted_iota(I32, (8, LANES), 0)
    scalars[...] = jnp.where(row == 0, alpha, jnp.where(row == 1, rz, 0.0))
    copies = [begin(scalars, scalars_out, sems.at[25])]
    for i, rows in enumerate(parts):
        firsts[i].wait()
        images[i].wait()
        for b in range(rows.start // BW, (rows.start + CHUNK) // BW):
            k = slot[b]
            start = pl.multiple_of(lax.rem(k, 2) * BW, BW)
            arrived = received[lax.div(k, 2), pl.ds(start, BW), :].astype(F32)
            block = pl.ds(b * BW, BW)
            value = first[block, :] - alpha * (image[block, :] + arrived)
            local[block, :] = 0.5 * value
        operand[rows, :] = local[rows, :].astype(BF16)
    part = coarse_contribution(basis_t[...], local[...])
    rz = jnp.zeros((1, LANES), F32)
    for i, rows in enumerate(parts):
        ready(i)
        product = product_rows(held, rows, operand)
        scaled = local[rows, :]
        value = scaled + scaled - RELAX * product
        rounded = value.astype(BF16)
        swept[rows, :] = rounded
        both = scaled + value
        base[rows, :] = both
        rz = rz + jnp.sum(scaled * both - RELAX * product * rounded.astype(F32), axis=0, keepdims=True)
    tile = tile_of([rz], F32)

    def fill(d):
        staged[d, 0:32, :] = part
        staged[d, 32:40, :] = tile

    copies += fill_and_send(fill, staged, out, sems, 26)
    copies += [begin(base, base_out, sems.at[30]), begin(swept, swept_out, sems.at[31])]
    finish_all(copies)


def second_sweep_body(slot, base_in, swept_in, matrix, out, token, held, base, swept, staged, sems):
    loads = [begin(swept_in, swept, sems.at[8]), begin(base_in, base, sems.at[9])]
    ready = stream(matrix, held, sems, 0)
    finish_all(loads)
    for i, rows in enumerate(chunks(held)):
        ready(i)
        value = 0.5 * (base[rows, :] - RELAX * product_rows(held, rows, swept))
        place_blocks(slot, rows, value, staged)
    copies = send_quarters(staged, out, sems, 10)
    token[...] = base[0:8, :]
    finish_all(copies)


def apply_first_body(
    order, slot, received, matrix, earlier_in, kept, out, image_out, kept_out, sums, held, operand, image, staged, earlier, sems
):
    load = begin(earlier_in, earlier, sems.at[16])
    copies = [begin(kept, kept_out, sems.at[22])]

    def save(i, rows):
        copies.append(begin(image.at[rows, :], image_out.at[rows, :], sems.at[23 + i]))

    dot = apply_matrix(order, slot, received, matrix, held, operand, (image, save), staged, sems)
    copies += send_quarters(staged, out, sems, 18)
    load.wait()
    sums[...] = tile_of([dot, earlier[0:1, :]], F32)
    finish_all(copies)


def apply_second_body(order, slot, received, matrix, out, held, operand, staged, sems):
    dot = apply_matrix(order, slot, received, matrix, held, operand, None, staged, sems)
    fill_tiles(staged, tile_of([dot], out.dtype))
    finish_all(send_quarters(staged, out, sems, 18))


def apply_matrix(order, slot, received, matrix, held, operand, image, staged, sems):
    ready = stream(matrix, held, sems, 0)
    for j in range(order.shape[0]):
        operand[rows_of(order[j]), :] = piece(received, j)[...]
    dot = jnp.zeros((1, LANES), F32)
    for i, rows in enumerate(chunks(held)):
        ready(i)
        product = product_rows(held, rows, operand)
        if image is not None:
            image[0][rows, :] = product
            image[1](i, rows)
        place_blocks(slot, rows, product, staged)
        dot = dot + jnp.sum(product * operand[rows, :].astype(F32), axis=0, keepdims=True)
    return dot


def dot_split(high, low, value):
    parts = split2(value)
    wide = jnp.dot(high[...], jnp.concatenate(parts, axis=1), preferred_element_type=F32)
    return wide[:, 0:LANES] + wide[:, LANES:] + jnp.dot(low[...], parts[0], preferred_element_type=F32)


def coarse_sum_body(place, index_row, received, token, out0, out1, out2, out3, sems):
    parts = received[:, 0:32, :].astype(F32).reshape(-1, LANES)
    split = jnp.concatenate(split3(parts), axis=1)
    group = place[0]
    quarter = parts.shape[0] // 4
    for t, out in enumerate((out0, out1, out2, out3)):
        base = lax.rem(group + t, 4) * quarter
        row = lax.broadcasted_iota(I32, (quarter, parts.shape[0]), 0) + base
        table = jnp.where(row == index_row[...], 1.0, 0.0).astype(BF16)
        sums = jnp.dot(table, split, preferred_element_type=F32)
        out[0:quarter, :] = sums[:, 0:LANES] + sums[:, LANES : 2 * LANES] + sums[:, 2 * LANES :]
        if out.shape[0] > quarter:
            out[quarter:, :] = jnp.sum(received[:, 32:40, :], axis=0)


def assemble_body(
    owner, index_rows, received, inverse_in, token, inverse_high, inverse_low, high, low, table, wide, inverse, sems
):
    load = begin(inverse_in, inverse, sems.at[0])
    wide[...] = jnp.zeros(wide.shape, F32)
    group = lax.broadcasted_iota(I32, (8, LANES), 1) // 32
    for k in range(owner.shape[0]):
        s, m = k // 2, k % 2
        packed = 0.5 * received[s, 32 + 8 * m : 40 + 8 * m, :]
        lanes = slice(s // 4 * LANES, (s // 4 + 1) * LANES)
        start = owner[k] * BW
        for i in range(4):
            turn = (32 * (s % 4 - i)) % LANES
            moved = pltpu.roll(packed, turn, 1) if turn else packed
            rows = pl.ds(pl.multiple_of(start + 8 * i, 8), 8)
            wide[rows, lanes] += jnp.where(group == s % 4, moved, 0.0)
    for rows in chunks(wide):
        high[rows, :], low[rows, :] = split2(wide[rows, :])
    count = index_rows.shape[0]
    turned = jnp.transpose(
        jnp.concatenate([index_rows[...], jnp.zeros((LANES - count, LANES), F32)], axis=0)
    )
    column = lax.broadcasted_iota(I32, (LANES, table.shape[1]), 1).astype(F32)
    for q in range(count):
        hit = column == turned[:, q : q + 1]
        table[q * LANES : (q + 1) * LANES, :] = jnp.where(hit, 1.0, 0.0).astype(BF16)
    load.wait()
    for rows in chunks(inverse):
        inverse_high[rows, :], inverse_low[rows, :] = split2(inverse[rows, :])


def gather_quarters(place, parts, held):
    quarter = held.shape[0] // 4
    for t, part in enumerate(parts):
        base = pl.multiple_of(lax.rem(place[0] + 4 - t, 4) * quarter, quarter)
        held[pl.ds(base, quarter), :] = part[0:quarter, :]


def solve_body(
    place,
    part0,
    part1,
    part2,
    part3,
    inverse_high,
    inverse_low,
    high,
    low,
    table,
    out,
    rz_out,
    held,
    term,
    rz_tile,
    sems,
):
    gather_quarters(place, (part0, part1, part2, part3), held)
    solved = dot_split(inverse_high, inverse_low, held[...])
    rz = jnp.sum(held[...] * solved, axis=0, keepdims=True)
    if part0.shape[0] > held.shape[0] // 4:
        rz = rz + part0[held.shape[0] // 4 : held.shape[0] // 4 + 1, :]
    rz_tile[...] = jnp.broadcast_to(rz, (8, LANES))
    copies = [begin(rz_tile, rz_out, sems.at[0])]
    sums = jnp.dot(table[...], jnp.concatenate(split2(solved), axis=1), preferred_element_type=F32)
    picked = sums[:, 0:LANES] + sums[:, LANES:]
    term[...] = dot_split(high, low, picked).reshape(term.shape)
    finish_all(copies + [begin(term, out, sems.at[1])])


def add_blocks(owner, received, total):
    total[...] = jnp.zeros(total.shape, F32)
    for k in range(owner.shape[0]):
        total[owner[k]] += piece(received, k)[...].astype(F32)


def direction_body(owner, term_in, received, direction, out, term, sems):
    load = begin(term_in, term, sems.at[0])
    add_blocks(owner, received, direction)
    load.wait()
    direction[...] += term[...]
    for k in range(owner.shape[0]):
        piece(out, k)[...] = direction[owner[k]].astype(out.dtype)


def image_body(
    owner, partner, received, sums0, sums1, sums2, sums3, image_out, out, image, staged, sems
):
    total = sums0[...] + sums1[...] + sums2[...] + sums3[...]
    tile = tile_of([total[0:1], total[1:2]], out.dtype)

    def fill(d):
        for k in (2 * d, 2 * d + 1):
            source = partner[k]
            start = pl.multiple_of(lax.rem(source, 2) * BW, BW)
            piece(staged, k)[...] = received[lax.div(source, 2), pl.ds(start, BW), :].astype(out.dtype)
        staged[d, 2 * BW :, :] = tile

    copies = fill_and_send(fill, staged, out, sems)
    add_blocks(owner, received, image)
    finish_all(copies + [begin(image, image_out, sems.at[4])])


def next_direction_body(
    owner,
    term_in,
    received,
    before_in,
    rz_in,
    scalars_in,
    direction,
    out,
    later,
    term,
    before,
    rz_tile,
    scalars,
    sems,
):
    loads = [
        begin(source, target, sems.at[i])
        for i, (source, target) in enumerate(
            ((rz_in, rz_tile), (scalars_in, scalars), (term_in, term), (before_in, before))
        )
    ]
    add_blocks(owner, received, direction)
    finish_all(loads)
    rz = rz_tile[0:1, :]
    ratio = rz / scalars[1:2, :]
    later[...] = jnp.broadcast_to(rz, (8, LANES))
    direction[...] = direction[...] + term[...] + ratio[None] * before[...]
    for k in range(owner.shape[0]):
        piece(out, k)[...] = direction[owner[k]].astype(out.dtype)


def before_last_body(owner, received, *rest):
    sources, (image1, part, base), targets, sems = rest[0:4], rest[4:7], rest[7:11], rest[11]
    loads = [begin(source, target, sems.at[i]) for i, (source, target) in enumerate(zip(sources, targets))]
    scalars, load, image, first = targets
    add_blocks(owner, received, image1)
    finish_all(loads)
    alpha = scalars[0:1, :][None]
    base[...] = load[...] - alpha * image[...]
    part[...] = alpha * first[...]


def finish_body(image1, part, base, second, later, sums0, sums1, sums2, sums3, *rest):
    solution_out, residual_out, solution, residual, sems = rest
    total = sums0[...] + sums1[...] + sums2[...] + sums3[...]
    alpha = (later[0:1, :] / total[0:1])[None]
    residual[...] = base[...] - alpha * image1[...]
    copies = [begin(residual, residual_out, sems.at[0])]
    solution[...] = part[...] + alpha * second[...]
    finish_all(copies + [begin(solution, solution_out, sems.at[1])])


def final_sums_body(received, sums, sems):
    sums[...] = sum_tiles(received)


def shards(n_sub, n_grp, load, schur, coarse_basis, coarse_index, coarse_inverse, send_order, recv_owner):
    owned = shape(load.shape)
    blocks = send_order.shape[0]
    dofs = schur.shape[1]
    coarse = coarse_inverse.shape[0]
    quarter = coarse // n_grp
    local = shape((dofs, LANES))
    tile = shape((8, LANES))
    operand = shape((dofs, LANES), BF16)
    held = shape((dofs, dofs), BF16)
    square = shape((coarse, coarse), BF16)
    place = lax.axis_index("grp").astype(I32).reshape(1)
    product_flops = 2 * dofs * dofs * LANES

    def hop(payload):
        return lax.all_to_all(payload, "sub", split_axis=0, concat_axis=0, tiled=True)

    def shifted(value, step):
        return lax.ppermute(value, "grp", [(i, (i + step) % n_grp) for i in range(n_grp)])

    def over_groups(value):
        return [value] + [shifted(value, step) for step in range(1, n_grp)]

    def payload(height, dtype=F32):
        return shape((n_sub, height, LANES), dtype)

    def coarse_parts(received, height, token):
        return call(
            coarse_sum_body,
            "coarse_sum",
            [("s", place), ("v", index_row), ("v", received), ("v", token)],
            [("v", shape((height, LANES)))] * 4,
            flops=2 * coarse * coarse * LANES * 3,
        )

    def coarse_term(parts, early):
        mine = parts[0]
        for step in range(1, n_grp):
            mine = mine + shifted(parts[step], step)
        factors = call(
            assemble_body,
            "assemble",
            [("s", recv_owner), ("v", index_rows), ("v", shared0), ("h", coarse_inverse), ("v", parts[0] if early else mine)],
            [("v", square)] * 5,
            [shape((owned.shape[0] * BW, coarse)), shape((coarse, coarse))],
            moved=10 * MIB,
        )
        if early:
            mine, factors = lax.optimization_barrier((mine, factors))
        gathered = over_groups(mine)
        return call(
            solve_body,
            "coarse_solve",
            [("s", place)] + [("v", part) for part in gathered] + [("v", factor) for factor in factors],
            [("h", owned), ("h", tile)],
            [shape((coarse, LANES)), owned, tile],
            flops=2 * coarse * coarse * LANES * 8,
            moved=8 * MIB,
        )

    basis_t = jnp.swapaxes(coarse_basis[0], 0, 1)
    basis_rows = (
        coarse_basis[0].reshape(blocks, 4, 8, 32).transpose(0, 2, 1, 3).reshape(blocks, 8, LANES)
    )
    lane = lax.broadcasted_iota(I32, (8, LANES), 1)
    index_tile = jnp.where(
        lane // 32 == lax.rem(lax.axis_index("sub"), 4), jnp.tile(coarse_index.astype(F32), (8, 4)), 0.0
    )
    position = jnp.arange(blocks, dtype=I32)
    slot = jnp.sum(
        jnp.where(send_order[:, None] == position[None, :], position[:, None], 0), axis=0
    ).astype(I32)
    partner = jnp.sum(
        jnp.where(
            (recv_owner[:, None] == recv_owner[None, :]) & (position[:, None] != position[None, :]),
            position[None, :],
            0,
        ),
        axis=1,
    ).astype(I32)

    [sent] = call(
        pack_load_body,
        "pack_load",
        [("s", recv_owner), ("h", load)],
        [("h", payload(2 * BW))],
        [owned, payload(2 * BW)],
    )
    local0, parts0 = call(
        unpack_first_body,
        "unpack_first",
        [("s", send_order), ("v", hop(sent)), ("v", basis_t), ("v", basis_rows), ("v", index_tile)],
        [("h", local), ("h", payload(56))],
        [local, payload(56)],
    )
    shared0 = hop(parts0)
    sent, rz_part = call(
        neumann_body,
        "neumann",
        [("s", slot), ("h", local0), ("h", schur)],
        [("h", payload(2 * BW)), ("h", tile)],
        [held, local, operand, local, payload(2 * BW), tile],
        flops=2 * product_flops,
        moved=12 * MIB,
    )
    index_rows = shared0[:, 48, :].reshape(n_sub // 4, 4, LANES).sum(1)
    index_row = index_rows.reshape(1, -1).astype(I32)
    parts = coarse_parts(shared0, quarter, index_row)
    parts, sent = lax.optimization_barrier((parts, sent))
    gathered = hop(sent)
    term0, coarse_rz0 = coarse_term(parts, True)
    direction0, sent = call(
        direction_body,
        "direction",
        [("s", recv_owner), ("h", term0), ("v", gathered)],
        [("v", owned), ("v", payload(2 * BW, BF16))],
        [owned],
    )

    like = payload(2 * BW)
    sent, image_local, direction0, sums = call(
        apply_first_body,
        "apply_first",
        [
            ("s", send_order),
            ("s", slot),
            ("v", hop(sent)),
            ("h", schur),
            ("h", rz_part),
            ("v", direction0),
        ],
        [("h", like), ("h", local), ("h", owned), ("v", tile)],
        [held, operand, local, like, tile],
        flops=product_flops,
        moved=12 * MIB,
    )
    like = payload(2 * BW + tile_height(SPREAD_DTYPE), SPREAD_DTYPE)
    image0, sent = call(
        image_body,
        "image",
        [("s", recv_owner), ("s", partner), ("v", hop(sent))] + [("v", part) for part in over_groups(sums)],
        [("h", owned), ("h", like)],
        [owned, like],
    )
    parts1, scalars, base, swept = call(
        unpack_sweep_body,
        "unpack_sweep",
        [("s", slot), ("v", hop(sent)), ("h", local0), ("h", image_local)]
        + [("h", coarse_rz0), ("v", basis_t), ("h", schur)],
        [("h", payload(40)), ("h", tile), ("h", local), ("h", operand)],
        [local, local, local, held, operand, local, operand, payload(40), tile, tile],
        flops=product_flops,
        moved=14 * MIB,
    )

    shared1 = hop(parts1)
    like = payload(2 * BW, COLLECT_DTYPE)
    sent, token = call(
        second_sweep_body,
        "second_sweep",
        [("s", slot), ("h", base), ("h", swept), ("h", schur)],
        [("h", like), ("v", tile)],
        [held, local, operand, like],
        flops=product_flops,
        moved=12 * MIB,
    )
    gathered = hop(sent)
    term1, coarse_rz1 = coarse_term(coarse_parts(shared1, quarter + 8, token), False)
    direction1, sent, later = call(
        next_direction_body,
        "next_direction",
        [
            ("s", recv_owner),
            ("h", term1),
            ("v", gathered),
            ("h", direction0),
            ("h", coarse_rz1),
            ("h", scalars),
        ],
        [("v", owned), ("v", payload(2 * BW, BF16)), ("v", tile)],
        [owned, owned, tile, tile],
    )

    like = payload(2 * BW + tile_height(COLLECT_DTYPE), COLLECT_DTYPE)
    [sent] = call(
        apply_second_body,
        "apply_second",
        [("s", send_order), ("s", slot), ("v", hop(sent)), ("h", schur)],
        [("h", like)],
        [held, operand, like],
        flops=product_flops,
        moved=12 * MIB,
    )
    gathered = hop(sent)
    [sums] = call(final_sums_body, "final_sums", [("v", gathered)], [("v", tile)])
    image1, part, base = call(
        before_last_body,
        "before_last",
        [("s", recv_owner), ("v", gathered)] + [("h", a) for a in (scalars, load, image0, direction0)],
        [("v", owned)] * 3,
        [tile, owned, owned, owned],
    )
    return tuple(
        call(
            finish_body,
            "finish",
            [("v", a) for a in (image1, part, base, direction1, later, *over_groups(sums))],
            [("h", owned), ("h", owned)],
            [owned, owned],
        )
    )


def solution(mesh):
    both = ("sub", "grp")
    in_specs = (
        P(both, None, None),
        P(both, None, None),
        P(both, None, None),
        P(both, None),
        P(),
        P(both),
        P(both),
    )
    out_specs = (P(both, None, None), P(both, None, None))
    body = functools.partial(shards, mesh.shape["sub"], mesh.shape["grp"])
    return jax.shard_map(body, mesh=mesh, in_specs=in_specs, out_specs=out_specs, check_vma=False)
```

```python
import functools

import jax
import jax.numpy as jnp
from jax import lax
from jax.experimental import pallas as pl
from jax.experimental.pallas import tpu as pltpu
from jax.sharding import PartitionSpec as P

F32, BF16, I32 = jnp.float32, jnp.bfloat16, jnp.int32
HIGHEST = lax.Precision.HIGHEST
RELAX = 0.2
BW = 32
LANES = 128
CHUNK = 256
MIB = 1 << 20

SPREAD_DTYPE = BF16
COLLECT_DTYPE = BF16

SPECS = {
    "v": pl.BlockSpec(memory_space=pltpu.VMEM),
    "s": pl.BlockSpec(memory_space=pltpu.SMEM),
    "h": pl.BlockSpec(memory_space=pltpu.HBM),
}


def call(body, name, ins, outs, scratch=(), flops=0, moved=2 * MIB, vmem=24, copies=48):
    arrays = [pltpu.with_memory_space_constraint(a, pltpu.HBM) if kind == "h" else a for kind, a in ins]
    shapes = [pltpu.HBM(like.shape, like.dtype) if kind == "h" else like for kind, like in outs]
    return pl.pallas_call(
        body,
        name=name,
        out_shape=shapes,
        in_specs=[SPECS[kind] for kind, _ in ins],
        out_specs=[SPECS[kind] for kind, _ in outs],
        scratch_shapes=[pltpu.VMEM(like.shape, like.dtype) for like in scratch]
        + [pltpu.SemaphoreType.DMA((copies,))],
        compiler_params=pltpu.CompilerParams(vmem_limit_bytes=vmem * MIB),
        cost_estimate=pl.CostEstimate(flops=flops, bytes_accessed=moved, transcendentals=0),
    )(*arrays)


def shape(dims, dtype=F32):
    return jax.ShapeDtypeStruct(dims, dtype)


def begin(source, target, sem):
    copy = pltpu.make_async_copy(source, target, sem)
    copy.start()
    return copy


def finish_all(copies):
    for copy in copies:
        copy.wait()


def rows_of(index):
    return pl.ds(pl.multiple_of(index * BW, BW), BW)


def piece(ref, k):
    return ref.at[k // 2, (k % 2) * BW : (k % 2 + 1) * BW, :]


def split2(value):
    high = value.astype(BF16)
    return high, (value - high.astype(F32)).astype(BF16)


def split3(value):
    high = value.astype(BF16)
    rest = value - high.astype(F32)
    middle = rest.astype(BF16)
    low = (rest - middle.astype(F32)).astype(BF16)
    return high, middle, low


def tile_of(values, dtype):
    height = tile_height(dtype)
    if dtype != F32:
        values = [part.astype(F32) for value in values for part in split3(value)]
    row = lax.broadcasted_iota(I32, (height, LANES), 0)
    tile = jnp.zeros((height, LANES), F32)
    for i, value in enumerate(values):
        tile = jnp.where(row == i, value, tile)
    return tile.astype(dtype)


def tile_height(dtype):
    return 8 if dtype == F32 else 16


def sum_tiles(ref):
    total = jnp.sum(ref[:, 2 * BW :, :].astype(F32), axis=0)
    if ref.dtype == F32:
        return total
    row = lax.broadcasted_iota(I32, (8, LANES), 0)
    value = total[0:1] + total[1:2] + total[2:3]
    return jnp.where(row == 0, value, 0.0)


def fill_and_send(fill, held, out, sems, first=0):
    copies = []
    step = out.shape[0] // 4
    for part in range(4):
        for d in range(part * step, (part + 1) * step):
            fill(d)
        chosen = pl.ds(part * step, step)
        copies.append(begin(held.at[chosen], out.at[chosen], sems.at[first + part]))
    return copies


def send_quarters(held, out, sems, first=0):
    return fill_and_send(lambda d: None, held, out, sems, first)


def fill_tiles(held, tile):
    for d in range(held.shape[0]):
        held[d, 2 * BW :, :] = tile


def place_blocks(slot, rows, value, held):
    for i in range(CHUNK // BW):
        k = slot[rows.start // BW + i]
        start = pl.multiple_of(lax.rem(k, 2) * BW, BW)
        held[lax.div(k, 2), pl.ds(start, BW), :] = value[i * BW : (i + 1) * BW].astype(held.dtype)


def pack_load_body(owner, owned_in, out, owned, held, sems):
    begin(owned_in, owned, sems.at[0]).wait()

    def fill(d):
        for k in (2 * d, 2 * d + 1):
            piece(held, k)[...] = owned[owner[k]]

    finish_all(fill_and_send(fill, held, out, sems, 1))


def coarse_contribution(basis_t, scaled):
    return jnp.dot(basis_t, scaled, precision=HIGHEST, preferred_element_type=F32)


def unpack_first_body(order, received, basis_t, basis_rows, index_tile, local_out, out, local, held, sems):
    for j in range(order.shape[0]):
        local[rows_of(order[j]), :] = piece(received, j)[...]
    copies = [begin(local, local_out, sems.at[0])]
    part = coarse_contribution(basis_t[...], 0.5 * local[...])
    tile = index_tile[...]

    def fill(d):
        held[d, 0:32, :] = part
        held[d, 32:40, :] = basis_rows[order[2 * d]]
        held[d, 40:48, :] = basis_rows[order[2 * d + 1]]
        held[d, 48:56, :] = tile

    finish_all(copies + fill_and_send(fill, held, out, sems, 1))


def stream(matrix, held, sems, first, ahead=5):
    count = held.shape[0] // CHUNK
    copies = []
    for i in range(count):
        rows = pl.ds(i * CHUNK, CHUNK)
        copies.append(pltpu.make_async_copy(matrix.at[0, rows, :], held.at[rows, :], sems.at[first + i]))
    for copy in copies[:ahead]:
        copy.start()

    def ready(i):
        copies[i].wait()
        if i + ahead < count:
            copies[i + ahead].start()

    return ready


def chunks(ref):
    return [pl.ds(i * CHUNK, CHUNK) for i in range(ref.shape[0] // CHUNK)]


def product_rows(held, rows, operand):
    return jnp.dot(held[rows, :], operand[...], preferred_element_type=F32)


def neumann_body(slot, local_in, matrix, out, sums_out, held, local, operand, work, staged, sums, sems):
    load = begin(local_in, local, sems.at[16])
    ready = stream(matrix, held, sems, 0)
    load.wait()
    operand[...] = (0.5 * local[...]).astype(BF16)
    for i, rows in enumerate(chunks(held)):
        ready(i)
        scaled = 0.5 * local[rows, :]
        work[rows, :] = scaled + scaled - RELAX * product_rows(held, rows, operand)
    operand[...] = work[...].astype(BF16)
    rz = jnp.zeros((1, LANES), F32)
    for rows in chunks(held):
        value = 0.5 * (0.5 * local[rows, :] + work[rows, :] - RELAX * product_rows(held, rows, operand))
        place_blocks(slot, rows, value, staged)
        rz = rz + jnp.sum(local[rows, :] * value, axis=0, keepdims=True)
    copies = send_quarters(staged, out, sems, 18)
    sums[...] = tile_of([rz], F32)
    finish_all([begin(sums, sums_out, sems.at[17])] + copies)


def unpack_sweep_body(
    slot,
    received,
    first_in,
    image_in,
    rz_in,
    basis_t,
    matrix,
    out,
    scalars_out,
    base_out,
    swept_out,
    first,
    image,
    local,
    held,
    operand,
    base,
    swept,
    staged,
    rz_tile,
    scalars,
    sems,
):
    load = begin(rz_in, rz_tile, sems.at[0])
    parts = chunks(local)
    firsts = [begin(first_in.at[rows, :], first.at[rows, :], sems.at[1 + i]) for i, rows in enumerate(parts)]
    images = [begin(image_in.at[rows, :], image.at[rows, :], sems.at[9 + i]) for i, rows in enumerate(parts)]
    ready = stream(matrix, held, sems, 17)
    load.wait()
    total = jnp.sum(received[:, 2 * BW :, :].astype(F32), axis=0)
    rz = total[3:4] + total[4:5] + total[5:6] + rz_tile[0:1, :]
    alpha = rz / (total[0:1] + total[1:2] + total[2:3])
    row = lax.broadcasted_iota(I32, (8, LANES), 0)
    scalars[...] = jnp.where(row == 0, alpha, jnp.where(row == 1, rz, 0.0))
    copies = [begin(scalars, scalars_out, sems.at[25])]
    for i, rows in enumerate(parts):
        firsts[i].wait()
        images[i].wait()
        for b in range(rows.start // BW, (rows.start + CHUNK) // BW):
            k = slot[b]
            start = pl.multiple_of(lax.rem(k, 2) * BW, BW)
            arrived = received[lax.div(k, 2), pl.ds(start, BW), :].astype(F32)
            block = pl.ds(b * BW, BW)
            value = first[block, :] - alpha * (image[block, :] + arrived)
            local[block, :] = 0.5 * value
        operand[rows, :] = local[rows, :].astype(BF16)
    part = coarse_contribution(basis_t[...], local[...])
    rz = jnp.zeros((1, LANES), F32)
    for i, rows in enumerate(parts):
        ready(i)
        product = product_rows(held, rows, operand)
        scaled = local[rows, :]
        value = scaled + scaled - RELAX * product
        rounded = value.astype(BF16)
        swept[rows, :] = rounded
        both = scaled + value
        base[rows, :] = both
        copies.append(begin(base.at[rows, :], base_out.at[rows, :], sems.at[30 + i]))
        copies.append(begin(swept.at[rows, :], swept_out.at[rows, :], sems.at[38 + i]))
        rz = rz + jnp.sum(scaled * both - RELAX * product * rounded.astype(F32), axis=0, keepdims=True)
    tile = tile_of([rz], F32)

    def fill(d):
        staged[d, 0:32, :] = part
        staged[d, 32:40, :] = tile

    copies += fill_and_send(fill, staged, out, sems, 26)
    finish_all(copies)


def second_sweep_body(slot, base_in, swept_in, matrix, out, token, held, base, swept, staged, sems):
    loads = [begin(swept_in, swept, sems.at[8]), begin(base_in, base, sems.at[9])]
    ready = stream(matrix, held, sems, 0)
    finish_all(loads)
    for i, rows in enumerate(chunks(held)):
        ready(i)
        value = 0.5 * (base[rows, :] - RELAX * product_rows(held, rows, swept))
        place_blocks(slot, rows, value, staged)
    copies = send_quarters(staged, out, sems, 10)
    token[...] = base[0:8, :]
    finish_all(copies)


def apply_first_body(
    order, slot, received, matrix, earlier_in, kept, out, image_out, kept_out, sums, held, operand, image, staged, earlier, sems
):
    load = begin(earlier_in, earlier, sems.at[16])
    copies = [begin(kept, kept_out, sems.at[22])]

    def save(i, rows):
        copies.append(begin(image.at[rows, :], image_out.at[rows, :], sems.at[23 + i]))

    dot = apply_matrix(order, slot, received, matrix, held, operand, (image, save), staged, sems)
    copies += send_quarters(staged, out, sems, 18)
    load.wait()
    sums[...] = tile_of([dot, earlier[0:1, :]], F32)
    finish_all(copies)


def apply_second_body(order, slot, received, matrix, out, held, operand, staged, sems):
    dot = apply_matrix(order, slot, received, matrix, held, operand, None, staged, sems)
    fill_tiles(staged, tile_of([dot], out.dtype))
    finish_all(send_quarters(staged, out, sems, 18))


def apply_matrix(order, slot, received, matrix, held, operand, image, staged, sems):
    ready = stream(matrix, held, sems, 0)
    for j in range(order.shape[0]):
        operand[rows_of(order[j]), :] = piece(received, j)[...]
    dot = jnp.zeros((1, LANES), F32)
    for i, rows in enumerate(chunks(held)):
        ready(i)
        product = product_rows(held, rows, operand)
        if image is not None:
            image[0][rows, :] = product
            image[1](i, rows)
        place_blocks(slot, rows, product, staged)
        dot = dot + jnp.sum(product * operand[rows, :].astype(F32), axis=0, keepdims=True)
    return dot


def dot_split(high, low, value):
    parts = split2(value)
    wide = jnp.dot(high[...], jnp.concatenate(parts, axis=1), preferred_element_type=F32)
    return wide[:, 0:LANES] + wide[:, LANES:] + jnp.dot(low[...], parts[0], preferred_element_type=F32)


def coarse_sum_body(place, index_row, received, token, out0, out1, out2, out3, sems):
    parts = received[:, 0:32, :].astype(F32).reshape(-1, LANES)
    split = jnp.concatenate(split3(parts), axis=1)
    group = place[0]
    quarter = parts.shape[0] // 4
    for t, out in enumerate((out0, out1, out2, out3)):
        base = lax.rem(group + t, 4) * quarter
        row = lax.broadcasted_iota(I32, (quarter, parts.shape[0]), 0) + base
        table = jnp.where(row == index_row[...], 1.0, 0.0).astype(BF16)
        sums = jnp.dot(table, split, preferred_element_type=F32)
        out[0:quarter, :] = sums[:, 0:LANES] + sums[:, LANES : 2 * LANES] + sums[:, 2 * LANES :]
        if out.shape[0] > quarter:
            out[quarter:, :] = jnp.sum(received[:, 32:40, :], axis=0)


def assemble_body(
    owner, index_rows, received, inverse_in, token, inverse_high, inverse_low, high, low, table, wide, inverse, sems
):
    load = begin(inverse_in, inverse, sems.at[0])
    wide[...] = jnp.zeros(wide.shape, F32)
    group = lax.broadcasted_iota(I32, (8, LANES), 1) // 32
    for k in range(owner.shape[0]):
        s, m = k // 2, k % 2
        packed = 0.5 * received[s, 32 + 8 * m : 40 + 8 * m, :]
        lanes = slice(s // 4 * LANES, (s // 4 + 1) * LANES)
        start = owner[k] * BW
        for i in range(4):
            turn = (32 * (s % 4 - i)) % LANES
            moved = pltpu.roll(packed, turn, 1) if turn else packed
            rows = pl.ds(pl.multiple_of(start + 8 * i, 8), 8)
            wide[rows, lanes] += jnp.where(group == s % 4, moved, 0.0)
    for rows in chunks(wide):
        high[rows, :], low[rows, :] = split2(wide[rows, :])
    count = index_rows.shape[0]
    turned = jnp.transpose(
        jnp.concatenate([index_rows[...], jnp.zeros((LANES - count, LANES), F32)], axis=0)
    )
    column = lax.broadcasted_iota(I32, (LANES, table.shape[1]), 1).astype(F32)
    for q in range(count):
        hit = column == turned[:, q : q + 1]
        table[q * LANES : (q + 1) * LANES, :] = jnp.where(hit, 1.0, 0.0).astype(BF16)
    load.wait()
    for rows in chunks(inverse):
        inverse_high[rows, :], inverse_low[rows, :] = split2(inverse[rows, :])


def gather_quarters(place, parts, held):
    quarter = held.shape[0] // 4
    for t, part in enumerate(parts):
        base = pl.multiple_of(lax.rem(place[0] + 4 - t, 4) * quarter, quarter)
        held[pl.ds(base, quarter), :] = part[0:quarter, :]


def solve_body(
    place,
    part0,
    part1,
    part2,
    part3,
    inverse_high,
    inverse_low,
    high,
    low,
    table,
    out,
    rz_out,
    held,
    term,
    rz_tile,
    sems,
):
    gather_quarters(place, (part0, part1, part2, part3), held)
    solved = dot_split(inverse_high, inverse_low, held[...])
    rz = jnp.sum(held[...] * solved, axis=0, keepdims=True)
    if part0.shape[0] > held.shape[0] // 4:
        rz = rz + part0[held.shape[0] // 4 : held.shape[0] // 4 + 1, :]
    rz_tile[...] = jnp.broadcast_to(rz, (8, LANES))
    copies = [begin(rz_tile, rz_out, sems.at[0])]
    sums = jnp.dot(table[...], jnp.concatenate(split2(solved), axis=1), preferred_element_type=F32)
    picked = sums[:, 0:LANES] + sums[:, LANES:]
    blocks = term.shape[0] // 2
    for i in range(2):
        rows = pl.ds(i * blocks * BW, blocks * BW)
        chosen = pl.ds(i * blocks, blocks)
        value = dot_split(high.at[rows, :], low.at[rows, :], picked)
        term[chosen] = value.reshape(blocks, BW, LANES)
        copies.append(begin(term.at[chosen], out.at[chosen], sems.at[1 + i]))
    finish_all(copies)


def add_blocks(owner, received, total):
    total[...] = jnp.zeros(total.shape, F32)
    for k in range(owner.shape[0]):
        total[owner[k]] += piece(received, k)[...].astype(F32)


def direction_body(owner, term_in, received, direction, out, term, sems):
    load = begin(term_in, term, sems.at[0])
    add_blocks(owner, received, direction)
    load.wait()
    direction[...] += term[...]
    for k in range(owner.shape[0]):
        piece(out, k)[...] = direction[owner[k]].astype(out.dtype)


def image_body(
    owner, partner, received, sums0, sums1, sums2, sums3, image_out, out, image, staged, sems
):
    total = sums0[...] + sums1[...] + sums2[...] + sums3[...]
    tile = tile_of([total[0:1], total[1:2]], out.dtype)

    def fill(d):
        for k in (2 * d, 2 * d + 1):
            source = partner[k]
            start = pl.multiple_of(lax.rem(source, 2) * BW, BW)
            piece(staged, k)[...] = received[lax.div(source, 2), pl.ds(start, BW), :].astype(out.dtype)
        staged[d, 2 * BW :, :] = tile

    copies = fill_and_send(fill, staged, out, sems)
    add_blocks(owner, received, image)
    finish_all(copies + [begin(image, image_out, sems.at[4])])


def next_direction_body(
    owner,
    term_in,
    received,
    before_in,
    rz_in,
    scalars_in,
    direction,
    out,
    later,
    term,
    before,
    rz_tile,
    scalars,
    sems,
):
    loads = [
        begin(source, target, sems.at[i])
        for i, (source, target) in enumerate(
            ((rz_in, rz_tile), (scalars_in, scalars), (term_in, term), (before_in, before))
        )
    ]
    add_blocks(owner, received, direction)
    finish_all(loads)
    rz = rz_tile[0:1, :]
    ratio = rz / scalars[1:2, :]
    later[...] = jnp.broadcast_to(rz, (8, LANES))
    direction[...] = direction[...] + term[...] + ratio[None] * before[...]
    for k in range(owner.shape[0]):
        piece(out, k)[...] = direction[owner[k]].astype(out.dtype)


def before_last_body(owner, received, *rest):
    sources, (image1, part, base), targets, sems = rest[0:4], rest[4:7], rest[7:11], rest[11]
    loads = [begin(source, target, sems.at[i]) for i, (source, target) in enumerate(zip(sources, targets))]
    scalars, load, image, first = targets
    add_blocks(owner, received, image1)
    finish_all(loads)
    alpha = scalars[0:1, :][None]
    base[...] = load[...] - alpha * image[...]
    part[...] = alpha * first[...]


def finish_body(image1, part, base, second, later, sums0, sums1, sums2, sums3, *rest):
    solution_out, residual_out, solution, residual, sems = rest
    total = sums0[...] + sums1[...] + sums2[...] + sums3[...]
    alpha = (later[0:1, :] / total[0:1])[None]
    residual[...] = base[...] - alpha * image1[...]
    copies = [begin(residual, residual_out, sems.at[0])]
    solution[...] = part[...] + alpha * second[...]
    finish_all(copies + [begin(solution, solution_out, sems.at[1])])


def final_sums_body(received, sums, sems):
    sums[...] = sum_tiles(received)


def shards(n_sub, n_grp, load, schur, coarse_basis, coarse_index, coarse_inverse, send_order, recv_owner):
    owned = shape(load.shape)
    blocks = send_order.shape[0]
    dofs = schur.shape[1]
    coarse = coarse_inverse.shape[0]
    quarter = coarse // n_grp
    local = shape((dofs, LANES))
    tile = shape((8, LANES))
    operand = shape((dofs, LANES), BF16)
    held = shape((dofs, dofs), BF16)
    square = shape((coarse, coarse), BF16)
    place = lax.axis_index("grp").astype(I32).reshape(1)
    product_flops = 2 * dofs * dofs * LANES

    def hop(payload):
        return lax.all_to_all(payload, "sub", split_axis=0, concat_axis=0, tiled=True)

    def shifted(value, step):
        return lax.ppermute(value, "grp", [(i, (i + step) % n_grp) for i in range(n_grp)])

    def over_groups(value):
        return [value] + [shifted(value, step) for step in range(1, n_grp)]

    def payload(height, dtype=F32):
        return shape((n_sub, height, LANES), dtype)

    def coarse_parts(received, height, token):
        return call(
            coarse_sum_body,
            "coarse_sum",
            [("s", place), ("v", index_row), ("v", received), ("v", token)],
            [("v", shape((height, LANES)))] * 4,
            flops=2 * coarse * coarse * LANES * 3,
        )

    def coarse_term(parts, early):
        mine = parts[0]
        for step in range(1, n_grp):
            mine = mine + shifted(parts[step], step)
        factors = call(
            assemble_body,
            "assemble",
            [("s", recv_owner), ("v", index_rows), ("v", shared0), ("h", coarse_inverse), ("v", parts[0] if early else mine)],
            [("v", square)] * 5,
            [shape((owned.shape[0] * BW, coarse)), shape((coarse, coarse))],
            moved=10 * MIB,
        )
        if early:
            mine, factors = lax.optimization_barrier((mine, factors))
        gathered = over_groups(mine)
        return call(
            solve_body,
            "coarse_solve",
            [("s", place)] + [("v", part) for part in gathered] + [("v", factor) for factor in factors],
            [("h", owned), ("h", tile)],
            [shape((coarse, LANES)), owned, tile],
            flops=2 * coarse * coarse * LANES * 8,
            moved=8 * MIB,
        )

    basis_t = jnp.swapaxes(coarse_basis[0], 0, 1)
    basis_rows = (
        coarse_basis[0].reshape(blocks, 4, 8, 32).transpose(0, 2, 1, 3).reshape(blocks, 8, LANES)
    )
    lane = lax.broadcasted_iota(I32, (8, LANES), 1)
    index_tile = jnp.where(
        lane // 32 == lax.rem(lax.axis_index("sub"), 4), jnp.tile(coarse_index.astype(F32), (8, 4)), 0.0
    )
    position = jnp.arange(blocks, dtype=I32)
    slot = jnp.sum(
        jnp.where(send_order[:, None] == position[None, :], position[:, None], 0), axis=0
    ).astype(I32)
    partner = jnp.sum(
        jnp.where(
            (recv_owner[:, None] == recv_owner[None, :]) & (position[:, None] != position[None, :]),
            position[None, :],
            0,
        ),
        axis=1,
    ).astype(I32)

    [sent] = call(
        pack_load_body,
        "pack_load",
        [("s", recv_owner), ("h", load)],
        [("h", payload(2 * BW))],
        [owned, payload(2 * BW)],
    )
    local0, parts0 = call(
        unpack_first_body,
        "unpack_first",
        [("s", send_order), ("v", hop(sent)), ("v", basis_t), ("v", basis_rows), ("v", index_tile)],
        [("h", local), ("h", payload(56))],
        [local, payload(56)],
    )
    shared0 = hop(parts0)
    sent, rz_part = call(
        neumann_body,
        "neumann",
        [("s", slot), ("h", local0), ("h", schur)],
        [("h", payload(2 * BW)), ("h", tile)],
        [held, local, operand, local, payload(2 * BW), tile],
        flops=2 * product_flops,
        moved=12 * MIB,
    )
    index_rows = shared0[:, 48, :].reshape(n_sub // 4, 4, LANES).sum(1)
    index_row = index_rows.reshape(1, -1).astype(I32)
    parts = coarse_parts(shared0, quarter, index_row)
    parts, sent = lax.optimization_barrier((parts, sent))
    gathered = hop(sent)
    term0, coarse_rz0 = coarse_term(parts, True)
    direction0, sent = call(
        direction_body,
        "direction",
        [("s", recv_owner), ("h", term0), ("v", gathered)],
        [("v", owned), ("v", payload(2 * BW, BF16))],
        [owned],
    )

    like = payload(2 * BW)
    sent, image_local, direction0, sums = call(
        apply_first_body,
        "apply_first",
        [
            ("s", send_order),
            ("s", slot),
            ("v", hop(sent)),
            ("h", schur),
            ("h", rz_part),
            ("v", direction0),
        ],
        [("h", like), ("h", local), ("h", owned), ("v", tile)],
        [held, operand, local, like, tile],
        flops=product_flops,
        moved=12 * MIB,
    )
    like = payload(2 * BW + tile_height(SPREAD_DTYPE), SPREAD_DTYPE)
    image0, sent = call(
        image_body,
        "image",
        [("s", recv_owner), ("s", partner), ("v", hop(sent))] + [("v", part) for part in over_groups(sums)],
        [("h", owned), ("h", like)],
        [owned, like],
    )
    parts1, scalars, base, swept = call(
        unpack_sweep_body,
        "unpack_sweep",
        [("s", slot), ("v", hop(sent)), ("h", local0), ("h", image_local)]
        + [("h", coarse_rz0), ("v", basis_t), ("h", schur)],
        [("h", payload(40)), ("h", tile), ("h", local), ("h", operand)],
        [local, local, local, held, operand, local, operand, payload(40), tile, tile],
        flops=product_flops,
        moved=14 * MIB,
    )

    shared1 = hop(parts1)
    like = payload(2 * BW, COLLECT_DTYPE)
    sent, token = call(
        second_sweep_body,
        "second_sweep",
        [("s", slot), ("h", base), ("h", swept), ("h", schur)],
        [("h", like), ("v", tile)],
        [held, local, operand, like],
        flops=product_flops,
        moved=12 * MIB,
    )
    gathered = hop(sent)
    term1, coarse_rz1 = coarse_term(coarse_parts(shared1, quarter + 8, token), False)
    direction1, sent, later = call(
        next_direction_body,
        "next_direction",
        [
            ("s", recv_owner),
            ("h", term1),
            ("v", gathered),
            ("h", direction0),
            ("h", coarse_rz1),
            ("h", scalars),
        ],
        [("v", owned), ("v", payload(2 * BW, BF16)), ("v", tile)],
        [owned, owned, tile, tile],
    )

    like = payload(2 * BW + tile_height(COLLECT_DTYPE), COLLECT_DTYPE)
    [sent] = call(
        apply_second_body,
        "apply_second",
        [("s", send_order), ("s", slot), ("v", hop(sent)), ("h", schur)],
        [("h", like)],
        [held, operand, like],
        flops=product_flops,
        moved=12 * MIB,
    )
    gathered = hop(sent)
    [sums] = call(final_sums_body, "final_sums", [("v", gathered)], [("v", tile)])
    image1, part, base = call(
        before_last_body,
        "before_last",
        [("s", recv_owner), ("v", gathered)] + [("h", a) for a in (scalars, load, image0, direction0)],
        [("v", owned)] * 3,
        [tile, owned, owned, owned],
    )
    return tuple(
        call(
            finish_body,
            "finish",
            [("v", a) for a in (image1, part, base, direction1, later, *over_groups(sums))],
            [("h", owned), ("h", owned)],
            [owned, owned],
        )
    )


def solution(mesh):
    both = ("sub", "grp")
    in_specs = (
        P(both, None, None),
        P(both, None, None),
        P(both, None, None),
        P(both, None),
        P(),
        P(both),
        P(both),
    )
    out_specs = (P(both, None, None), P(both, None, None))
    body = functools.partial(shards, mesh.shape["sub"], mesh.shape["grp"])
    return jax.shard_map(body, mesh=mesh, in_specs=in_specs, out_specs=out_specs, check_vma=False)
```
